256 devices in a mesh: thick: 8 (over z), facade: 32 (over y, x, core).
Axes of the slice: x: 4, y: 4, z: 8, core: 2. Of those that a mesh axis runs over, the one named last changes fastest.
Arguments:
- solid_occupancy: float32 [64, 16, 16384], P('thick', None, 'facade'), may hold values from 0 to 1
- newer_occupancy_shift: float32 [64, 16, 16384], P('thick', None, 'facade'), may hold values from -0.1 to 0.1
- older_occupancy_shift: float32 [64, 16, 16384], P('thick', None, 'facade'), may hold values from -0.1 to 0.1
- below_limit_spacing: float32 [64, 16, 16384], P('thick', None, 'facade'), may hold values from 0.05 to 0.5
- above_limit_spacing: float32 [64, 16, 16384], P('thick', None, 'facade'), may hold values from 0.05 to 0.5
- thermal_state: float32 [64, 16, 16384], P('thick', None, 'facade'), may hold values from -6 to 6
- loss_state_derivative: float32 [64, 16, 16384], P('thick', None, 'facade'), may hold values from -6 to 6
- prior_dual_state: float32 [64, 16, 16384], P('thick', None, 'facade'), may hold values from -3 to 3
- cell_material: int32 [64, 16, 16384], P('thick', None, 'facade'), may hold values from 0 to 2
Outputs:
- density_new: float32 [64, 16, 16384], P('thick', None, 'facade')
- below_limit_line: float32 [64, 16, 16384], P('thick', None, 'facade')
- above_limit_line: float32 [64, 16, 16384], P('thick', None, 'facade')
- dual_state: float32 [64, 16, 16384], P('thick', None, 'facade')
The draws below stay inside these ranges and needn't reach their ends.
Inputs may be any that keep to these rules, and one draw needn't show every extreme that they name: `cell_material`: 0 marks glass, 1 frame (the design voxels), 2 steel anchors.
All inputs are finite; a program needn't handle non-finite values. Where the reference program divides by a largest or mean magnitude, that divisor is 1e-20 or more.
Results may differ from the reference program's by a relative error of at most 0.0003.
Values sent between devices are 32-bit elements; how exact they have to be, the bound alone decides.
No kernel may reach another device: no remote copies, remote signals or barrier semaphores. Data moves between devices by JAX's collectives and lax.ppermute only.
A program may use at most 64 MiB of HBM per device.

```python
import math
import jax
import jax.numpy as jnp
from jax import lax

VERTICAL_CELLS = 16
RADIUS = 4
SWEEPS = 3
NEWTON = 8
DEPTH_CELLS = 64
FRONT_CELLS = 16384


def with_ends(drawn, own_key, low, largest):
    longest = drawn.shape.index(max(drawn.shape))
    spots = []
    for shift in (0, 1):
        where = [jax.random.randint(jax.random.fold_in(own_key, axis), (), 0, length) for axis, length in enumerate(drawn.shape)]
        where[longest] = (where[longest] + shift) % drawn.shape[longest]
        spots.append(tuple(where))
    return drawn.at[spots[0]].set(low).at[spots[1]].set(largest)


def shard_levels(own_key, dims, split, least, high):
    factor_of = 1.0
    for dim, parts in split:
        heights = jax.random.uniform(jax.random.fold_in(jax.random.fold_in(own_key, 6), dim), (parts,), jnp.float32, least / len(split), high / len(split))
        factor_of = factor_of * jnp.repeat(jnp.exp(heights), dims[dim] // parts).reshape((-1,) + (1,) * (len(dims) - 1 - dim))
    return factor_of


def gaussian(rng, dims, width, limit, shards=(), kind=jnp.bfloat16):
    loudness = shard_levels(rng, dims, shards, -0.22, 0.18) if shards else 1.0
    array = jax.random.normal(rng, dims, jnp.float32) * width * loudness
    return jnp.minimum(jnp.maximum(array, -limit), limit).astype(kind)


def setup_inputs(seed: int = 0) -> dict:
    key_of = jax.random.split(jax.random.key(seed), 10)
    solid_occupancy = jnp.clip(1.0 * jax.random.uniform(key_of[0], (DEPTH_CELLS, VERTICAL_CELLS, FRONT_CELLS), jnp.float32) ** shard_levels(key_of[0], (DEPTH_CELLS, VERTICAL_CELLS, FRONT_CELLS), ((0, 8), (2, 32)), -0.2, 0.2), 0.0, 1.0)
    newer_occupancy_shift = jnp.clip(jax.random.uniform(key_of[1], (DEPTH_CELLS, VERTICAL_CELLS, FRONT_CELLS), jnp.float32, -0.1, 0.1) * shard_levels(key_of[1], (DEPTH_CELLS, VERTICAL_CELLS, FRONT_CELLS), ((0, 8), (2, 32)), -0.4, 0.0), -0.1, 0.1)
    older_occupancy_shift = jnp.clip(jax.random.uniform(key_of[2], (DEPTH_CELLS, VERTICAL_CELLS, FRONT_CELLS), jnp.float32, -0.1, 0.1) * shard_levels(key_of[2], (DEPTH_CELLS, VERTICAL_CELLS, FRONT_CELLS), ((0, 8), (2, 32)), -0.4, 0.0), -0.1, 0.1)
    below_limit_spacing = jnp.clip(jnp.exp(math.log(0.5) - 2.3025851 * jax.random.uniform(key_of[3], (DEPTH_CELLS, VERTICAL_CELLS, FRONT_CELLS), jnp.float32) ** shard_levels(key_of[3], (DEPTH_CELLS, VERTICAL_CELLS, FRONT_CELLS), ((0, 8), (2, 32)), -0.2, 0.2)), 0.05, 0.5)
    above_limit_spacing = jnp.clip(jnp.exp(math.log(0.5) - 2.3025851 * jax.random.uniform(key_of[4], (DEPTH_CELLS, VERTICAL_CELLS, FRONT_CELLS), jnp.float32) ** shard_levels(key_of[4], (DEPTH_CELLS, VERTICAL_CELLS, FRONT_CELLS), ((0, 8), (2, 32)), -0.2, 0.2)), 0.05, 0.5)
    thermal_state = gaussian(key_of[5], (DEPTH_CELLS, VERTICAL_CELLS, FRONT_CELLS), 1.0, 6.0, ((0, 8), (2, 32)), jnp.float32)
    loss_state_derivative = gaussian(key_of[6], (DEPTH_CELLS, VERTICAL_CELLS, FRONT_CELLS), 1.0, 6.0, ((0, 8), (2, 32)), jnp.float32)
    prior_dual_state = gaussian(key_of[7], (DEPTH_CELLS, VERTICAL_CELLS, FRONT_CELLS), 0.5, 3.0, ((0, 8), (2, 32)), jnp.float32)
    cell_material = with_ends(jax.random.randint(key_of[8], (DEPTH_CELLS, VERTICAL_CELLS, FRONT_CELLS), 0, 3), jax.random.fold_in(key_of[8], 1), 0, 2).astype(jnp.int32)
    return {"solid_occupancy": solid_occupancy, "newer_occupancy_shift": newer_occupancy_shift, "older_occupancy_shift": older_occupancy_shift, "below_limit_spacing": below_limit_spacing, "above_limit_spacing": above_limit_spacing, "thermal_state": thermal_state, "loss_state_derivative": loss_state_derivative, "prior_dual_state": prior_dual_state, "cell_material": cell_material}


k_void = 0.03
k_frame = 160.0
k_glass = 1.0
k_anchor = 50.0
loss_rate = 0.05
spectrum_low = 0.05
spectrum_high = 2.0
solid_allowance = 0.35
curve_floor = 0.05
move_limit = 0.2
gamma_slope = 200.0

def convolve_axis(values, axis, radius):
    count = values.shape[axis] - 2 * radius
    total = None
    for offset in range(-radius, radius + 1):
        weight = float(radius + 1 - abs(offset))
        piece = lax.slice_in_dim(values, radius + offset, radius + offset + count, axis=axis)
        total = weight * piece if total is None else total + weight * piece
    return total

def smooth(values, radius):
    out = convolve_axis(values, 0, radius)
    out = jnp.pad(out, ((0, 0), (radius, radius), (0, 0)))
    out = convolve_axis(out, 1, radius)
    return convolve_axis(out, 2, radius)

def axis_norm(start, count, total, radius):
    position = start + jnp.arange(count, dtype=jnp.int32)
    acc = jnp.zeros((count,), jnp.float32)
    for offset in range(-radius, radius + 1):
        weight = float(radius + 1 - abs(offset))
        inside = ((position + offset >= 0) & (position + offset < total)).astype(jnp.float32)
        acc = acc + weight * inside
    return acc

def neighbour_views(padded):
    center = padded[1:-1, 1:-1, 1:-1]
    views = [padded[2:, 1:-1, 1:-1], padded[:-2, 1:-1, 1:-1], padded[1:-1, 2:, 1:-1], padded[1:-1, :-2, 1:-1], padded[1:-1, 1:-1, 2:], padded[1:-1, 1:-1, :-2]]
    return (center, views)

def pad_middle(values):
    return jnp.pad(values, ((0, 0), (1, 1), (0, 0)))

def conductances(padded_conductance_rim):
    center, views = neighbour_views(pad_middle(padded_conductance_rim))
    return [2.0 * center * view / (center + view) for view in views]

def matrix_product(field_rim, heat_flux):
    center, views = neighbour_views(pad_middle(field_rim))
    total = loss_rate * center
    for face, view in zip(heat_flux, views):
        total = total + face * (center - view)
    return total

def fraction_derivative(padded_conductance_rim, adjoint_rim, temp_rim):
    k_center, k_views = neighbour_views(pad_middle(padded_conductance_rim))
    a_center, a_views = neighbour_views(pad_middle(adjoint_rim))
    t_center, t_views = neighbour_views(pad_middle(temp_rim))
    total = jnp.zeros_like(k_center)
    for k_view, a_view, t_view in zip(k_views, a_views, t_views):
        share = k_view / (k_center + k_view)
        total = total - 2.0 * share * share * (a_center - a_view) * (t_center - t_view)
    return total

def conductivity(rho, layout_candidate, glass):
    frame_value = k_void + (k_frame - k_void) * rho * rho * rho
    return jnp.where(layout_candidate, frame_value, jnp.where(glass, k_glass, k_anchor))

def ready_limit_lines(solid_occupancy, newer_occupancy_shift, older_occupancy_shift, below_limit_spacing, above_limit_spacing, normalised_element):
    spectral_weight = 0.95 + 0.25 * jnp.tanh(gamma_slope * newer_occupancy_shift * older_occupancy_shift)
    below_limit_line = solid_occupancy - spectral_weight * below_limit_spacing
    above_limit_line = solid_occupancy + spectral_weight * above_limit_spacing
    floor_limit = jnp.maximum(jnp.maximum(0.0, below_limit_line + 0.1 * (solid_occupancy - below_limit_line)), solid_occupancy - move_limit)
    ceiling_limit = jnp.minimum(jnp.minimum(1.0, above_limit_line - 0.1 * (above_limit_line - solid_occupancy)), solid_occupancy + move_limit)
    up_sq = (above_limit_line - solid_occupancy) ** 2
    low_sq = (solid_occupancy - below_limit_line) ** 2
    plus = jnp.maximum(normalised_element, 0.0)
    minus = jnp.maximum(-normalised_element, 0.0)
    above_dividend_offset = up_sq * (1.001 * plus + 0.001 * minus + 1e-05)
    below_dividend_offset = low_sq * (0.001 * plus + 1.001 * minus + 1e-05)
    above_dividend_scale = up_sq * (1.001 + 1e-05)
    below_dividend_scale = low_sq * (0.001 + 1e-05)
    shared_summands = solid_occupancy - solid_allowance - above_dividend_scale / (above_limit_line - solid_occupancy) - below_dividend_scale / (solid_occupancy - below_limit_line)
    return (below_limit_line, above_limit_line, floor_limit, ceiling_limit, above_dividend_offset, below_dividend_offset, above_dividend_scale, below_dividend_scale, shared_summands)

def dual_terms(multiplier, below_limit_line, above_limit_line, floor_limit, ceiling_limit, above_dividend_offset, below_dividend_offset, above_dividend_scale, below_dividend_scale):
    root_upper = jnp.sqrt(above_dividend_offset + multiplier * above_dividend_scale)
    root_lower = jnp.sqrt(below_dividend_offset + multiplier * below_dividend_scale)
    total = root_upper + root_lower
    trial = below_limit_line + (above_limit_line - below_limit_line) * root_lower / total
    chosen = jnp.clip(trial, floor_limit, ceiling_limit)
    free = (trial > floor_limit) & (trial < ceiling_limit)
    rate = (above_limit_line - below_limit_line) * (root_upper * below_dividend_scale / (2.0 * root_lower) - root_lower * above_dividend_scale / (2.0 * root_upper)) / (total * total)
    rate = jnp.where(free, rate, 0.0)
    slope = above_dividend_scale / (above_limit_line - chosen) ** 2 - below_dividend_scale / (chosen - below_limit_line) ** 2
    g_terms = above_dividend_scale / (above_limit_line - chosen) + below_dividend_scale / (chosen - below_limit_line)
    h_terms = curve_floor + jnp.abs(slope * rate)
    return (chosen, g_terms, h_terms)

def reference(solid_occupancy, newer_occupancy_shift, older_occupancy_shift, below_limit_spacing, above_limit_spacing, thermal_state, loss_state_derivative, prior_dual_state, cell_material):
    layout_candidate = cell_material == 1
    glass = cell_material == 0
    rows, height, cols = solid_occupancy.shape
    norm = axis_norm(0, rows, rows, RADIUS)[:, None, None] * axis_norm(0, height, height, RADIUS)[None, :, None] * axis_norm(0, cols, cols, RADIUS)[None, None, :]
    rim_deep = ((RADIUS, RADIUS), (0, 0), (RADIUS, RADIUS))
    unit_rim_width = ((1, 1), (0, 0), (1, 1))
    rho = smooth(jnp.pad(solid_occupancy, rim_deep), RADIUS) / norm
    material_coefficient = conductivity(rho, layout_candidate, glass)
    padded_conductance_rim = jnp.pad(material_coefficient, unit_rim_width)
    heat_flux = conductances(padded_conductance_rim)
    diagonal = loss_rate + heat_flux[0]
    for face in heat_flux[1:]:
        diagonal = diagonal + face
    centre_value = 0.5 * (spectrum_high + spectrum_low)
    half_width = 0.5 * (spectrum_high - spectrum_low)
    ratio_value = centre_value / half_width
    dual_state = prior_dual_state
    equation_mismatch = loss_state_derivative - matrix_product(jnp.pad(dual_state, unit_rim_width), heat_flux)
    direction = equation_mismatch / diagonal / centre_value
    factor = 1.0 / ratio_value
    for sweep in range(SWEEPS):
        dual_state = dual_state + direction
        if sweep < SWEEPS - 1:
            equation_mismatch = equation_mismatch - matrix_product(jnp.pad(direction, unit_rim_width), heat_flux)
            factor_next = 1.0 / (2.0 * ratio_value - factor)
            direction = factor_next * factor * direction + 2.0 * factor_next / half_width * (equation_mismatch / diagonal)
            factor = factor_next
    derivative_map = fraction_derivative(padded_conductance_rim, jnp.pad(dual_state, unit_rim_width), jnp.pad(thermal_state, unit_rim_width))
    weighted = jnp.where(layout_candidate, derivative_map * (3.0 * (k_frame - k_void)) * rho * rho, 0.0) / norm
    grad = smooth(jnp.pad(weighted, rim_deep), RADIUS)
    scale = jnp.max(jnp.where(layout_candidate, jnp.abs(grad), 0.0))
    normalised_element = grad / (scale + 1e-06)
    below_limit_line, above_limit_line, floor_limit, ceiling_limit, above_dividend_offset, below_dividend_offset, above_dividend_scale, below_dividend_scale, shared_summands = ready_limit_lines(solid_occupancy, newer_occupancy_shift, older_occupancy_shift, below_limit_spacing, above_limit_spacing, normalised_element)
    reference_point = jnp.sum(jnp.where(layout_candidate, shared_summands, 0.0))
    multiplier = jnp.float32(1.0)
    for step in range(NEWTON):
        chosen, g_terms, h_terms = dual_terms(multiplier, below_limit_line, above_limit_line, floor_limit, ceiling_limit, above_dividend_offset, below_dividend_offset, above_dividend_scale, below_dividend_scale)
        slope_sum = reference_point + jnp.sum(jnp.where(layout_candidate, g_terms, 0.0))
        curve = jnp.sum(jnp.where(layout_candidate, h_terms, 0.0))
        multiplier = jnp.maximum(jnp.float32(0.0), multiplier + slope_sum / curve)
    chosen, g_terms, h_terms = dual_terms(multiplier, below_limit_line, above_limit_line, floor_limit, ceiling_limit, above_dividend_offset, below_dividend_offset, above_dividend_scale, below_dividend_scale)
    density_new = jnp.where(layout_candidate, chosen, solid_occupancy)
    return (density_new, below_limit_line, above_limit_line, dual_state)
```

```python
import jax
import jax.numpy as jnp
from jax import lax
from jax.sharding import PartitionSpec as P

RADIUS = 4
SWEEPS = 3
NEWTON = 8


k_void = 0.03
k_frame = 160.0
k_glass = 1.0
k_anchor = 50.0
loss_rate = 0.05
spectrum_low = 0.05
spectrum_high = 2.0
solid_allowance = 0.35
curve_floor = 0.05
move_limit = 0.2
gamma_slope = 200.0


def with_halo(value, sides, width):
    for axis, dim in sides:
        size, length = (lax.axis_size(axis), value.shape[dim])
        up = [(i, (i + 1) % size) for i in range(size - 1)]
        down = [(j, i) for i, j in up]
        last = lax.slice_in_dim(value, length - width, length, axis=dim)
        first = lax.slice_in_dim(value, 0, width, axis=dim)
        before = lax.ppermute(last, axis, up)
        after = lax.ppermute(first, axis, down)
        value = jnp.concatenate([before, value, after], axis=dim)
    return value


def convolve_axis(values, axis, radius):
    count = values.shape[axis] - 2 * radius
    total = None
    for offset in range(-radius, radius + 1):
        weight = float(radius + 1 - abs(offset))
        piece = lax.slice_in_dim(values, radius + offset, radius + offset + count, axis=axis)
        total = weight * piece if total is None else total + weight * piece
    return total


def smooth(values, radius):
    out = convolve_axis(values, 0, radius)
    out = jnp.pad(out, ((0, 0), (radius, radius), (0, 0)))
    out = convolve_axis(out, 1, radius)
    return convolve_axis(out, 2, radius)


def axis_norm(start, count, total, radius):
    position = start + jnp.arange(count, dtype=jnp.int32)
    acc = jnp.zeros((count,), jnp.float32)
    for offset in range(-radius, radius + 1):
        weight = float(radius + 1 - abs(offset))
        inside = ((position + offset >= 0) & (position + offset < total)).astype(jnp.float32)
        acc = acc + weight * inside
    return acc


def neighbour_views(padded):
    center = padded[1:-1, 1:-1, 1:-1]
    views = [
        padded[2:, 1:-1, 1:-1],
        padded[:-2, 1:-1, 1:-1],
        padded[1:-1, 2:, 1:-1],
        padded[1:-1, :-2, 1:-1],
        padded[1:-1, 1:-1, 2:],
        padded[1:-1, 1:-1, :-2],
    ]
    return (center, views)


def pad_middle(values):
    return jnp.pad(values, ((0, 0), (1, 1), (0, 0)))


def conductances(padded_conductance_rim):
    center, views = neighbour_views(pad_middle(padded_conductance_rim))
    faces = []
    for view in views:
        summed = center + view
        positive = summed > 0.0
        safe_sum = jnp.where(positive, summed, 1.0)
        faces.append(jnp.where(positive, 2.0 * center * view / safe_sum, 0.0))
    return faces


def matrix_product(field_rim, heat_flux):
    center, views = neighbour_views(pad_middle(field_rim))
    total = loss_rate * center
    for face, view in zip(heat_flux, views):
        total = total + face * (center - view)
    return total


def fraction_derivative(padded_conductance_rim, adjoint_rim, temp_rim):
    k_center, k_views = neighbour_views(pad_middle(padded_conductance_rim))
    a_center, a_views = neighbour_views(pad_middle(adjoint_rim))
    t_center, t_views = neighbour_views(pad_middle(temp_rim))
    total = jnp.zeros_like(k_center)
    for k_view, a_view, t_view in zip(k_views, a_views, t_views):
        share = k_view / (k_center + k_view)
        total = total - 2.0 * share * share * (a_center - a_view) * (t_center - t_view)
    return total


def conductivity(rho, layout_candidate, glass):
    frame_value = k_void + (k_frame - k_void) * rho * rho * rho
    return jnp.where(layout_candidate, frame_value, jnp.where(glass, k_glass, k_anchor))


def diagonal_of(heat_flux):
    diagonal = loss_rate + heat_flux[0]
    for face in heat_flux[1:]:
        diagonal = diagonal + face
    return diagonal


def ready_limit_lines(
    solid_occupancy,
    newer_occupancy_shift,
    older_occupancy_shift,
    below_limit_spacing,
    above_limit_spacing,
    normalised_element,
):
    spectral_weight = 0.95 + 0.25 * jnp.tanh(
        gamma_slope * newer_occupancy_shift * older_occupancy_shift
    )
    below_limit_line = solid_occupancy - spectral_weight * below_limit_spacing
    above_limit_line = solid_occupancy + spectral_weight * above_limit_spacing
    floor_limit = jnp.maximum(
        jnp.maximum(0.0, below_limit_line + 0.1 * (solid_occupancy - below_limit_line)),
        solid_occupancy - move_limit,
    )
    ceiling_limit = jnp.minimum(
        jnp.minimum(1.0, above_limit_line - 0.1 * (above_limit_line - solid_occupancy)),
        solid_occupancy + move_limit,
    )
    up_sq = (above_limit_line - solid_occupancy) ** 2
    low_sq = (solid_occupancy - below_limit_line) ** 2
    plus = jnp.maximum(normalised_element, 0.0)
    minus = jnp.maximum(-normalised_element, 0.0)
    above_dividend_offset = up_sq * (1.001 * plus + 0.001 * minus + 1e-05)
    below_dividend_offset = low_sq * (0.001 * plus + 1.001 * minus + 1e-05)
    above_dividend_scale = up_sq * (1.001 + 1e-05)
    below_dividend_scale = low_sq * (0.001 + 1e-05)
    shared_summands = (
        solid_occupancy
        - solid_allowance
        - above_dividend_scale / (above_limit_line - solid_occupancy)
        - below_dividend_scale / (solid_occupancy - below_limit_line)
    )
    return (
        below_limit_line,
        above_limit_line,
        floor_limit,
        ceiling_limit,
        above_dividend_offset,
        below_dividend_offset,
        above_dividend_scale,
        below_dividend_scale,
        shared_summands,
    )


def dual_terms(
    multiplier,
    below_limit_line,
    above_limit_line,
    floor_limit,
    ceiling_limit,
    above_dividend_offset,
    below_dividend_offset,
    above_dividend_scale,
    below_dividend_scale,
):
    root_upper = jnp.sqrt(above_dividend_offset + multiplier * above_dividend_scale)
    root_lower = jnp.sqrt(below_dividend_offset + multiplier * below_dividend_scale)
    total = root_upper + root_lower
    trial = below_limit_line + (above_limit_line - below_limit_line) * root_lower / total
    chosen = jnp.clip(trial, floor_limit, ceiling_limit)
    free = (trial > floor_limit) & (trial < ceiling_limit)
    rate = (
        (above_limit_line - below_limit_line)
        * (
            root_upper * below_dividend_scale / (2.0 * root_lower)
            - root_lower * above_dividend_scale / (2.0 * root_upper)
        )
        / (total * total)
    )
    rate = jnp.where(free, rate, 0.0)
    slope = (
        above_dividend_scale / (above_limit_line - chosen) ** 2
        - below_dividend_scale / (chosen - below_limit_line) ** 2
    )
    g_terms = above_dividend_scale / (above_limit_line - chosen) + below_dividend_scale / (
        chosen - below_limit_line
    )
    h_terms = curve_floor + jnp.abs(slope * rate)
    return (chosen, g_terms, h_terms)


def iteration_margin(values):
    return with_halo(values, (("thick", 0), ("facade", 2)), 1)


def everyone(row):
    axes = ("thick", "facade")
    count = lax.axis_size("thick") * lax.axis_size("facade")
    copies = jnp.broadcast_to(row, (count, row.shape[-1]))
    return lax.all_to_all(copies, axes, 0, 0, tiled=True)


def dual_reduce(slope_part, curve_part):
    half = jnp.arange(128) < 64
    rows = everyone(jnp.where(half, slope_part, curve_part)[None, :])
    total = jnp.sum(rows, axis=0)
    return total[0], total[64]


def on_device(
    solid_occupancy,
    newer_occupancy_shift,
    older_occupancy_shift,
    below_limit_spacing,
    above_limit_spacing,
    thermal_state,
    loss_state_derivative,
    prior_dual_state,
    cell_material,
):
    rows_dev, height, cols_dev = solid_occupancy.shape
    rows_total = rows_dev * lax.axis_size("thick")
    cols_total = cols_dev * lax.axis_size("facade")
    row_start = lax.axis_index("thick") * rows_dev
    col_start = lax.axis_index("facade") * cols_dev
    layout_candidate = cell_material == 1
    glass = cell_material == 0
    first = axis_norm(row_start - 0, rows_dev + 2 * 0, rows_total, RADIUS)
    middle = axis_norm(0, height, height, RADIUS)
    last = axis_norm(col_start - 0, cols_dev + 2 * 0, cols_total, RADIUS)
    norm = first[:, None, None] * middle[None, :, None] * last[None, None, :]
    centre_value = 0.5 * (spectrum_high + spectrum_low)
    half_width = 0.5 * (spectrum_high - spectrum_low)
    ratio_value = centre_value / half_width
    density_ext = with_halo(solid_occupancy, (("thick", 0), ("facade", 2)), RADIUS)
    rho = smooth(density_ext, RADIUS) / norm
    material_coefficient = conductivity(rho, layout_candidate, glass)
    both_sides = with_halo(
        jnp.stack([material_coefficient, thermal_state]), (("thick", 1), ("facade", 3)), 1
    )
    padded_conductance_rim = both_sides[0]
    temp_rim = both_sides[1]
    heat_flux = conductances(padded_conductance_rim)
    diagonal = diagonal_of(heat_flux)
    dual_state = prior_dual_state
    equation_mismatch = loss_state_derivative - matrix_product(
        iteration_margin(dual_state), heat_flux
    )
    direction = equation_mismatch / diagonal / centre_value
    factor = 1.0 / ratio_value
    for sweep in range(SWEEPS):
        dual_state = dual_state + direction
        if sweep < SWEEPS - 1:
            equation_mismatch = equation_mismatch - matrix_product(
                iteration_margin(direction), heat_flux
            )
            factor_next = 1.0 / (2.0 * ratio_value - factor)
            direction = factor_next * factor * direction + 2.0 * factor_next / half_width * (
                equation_mismatch / diagonal
            )
            factor = factor_next
    derivative_map = fraction_derivative(
        padded_conductance_rim, iteration_margin(dual_state), temp_rim
    )
    weighted = (
        jnp.where(layout_candidate, derivative_map * (3.0 * (k_frame - k_void)) * rho * rho, 0.0)
        / norm
    )
    weighted_ext = with_halo(weighted, (("thick", 0), ("facade", 2)), RADIUS)
    grad = smooth(weighted_ext, RADIUS)
    scale_here = jnp.max(jnp.where(layout_candidate, jnp.abs(grad), 0.0))
    scale = jnp.max(everyone(jnp.full((1, 128), scale_here)))
    normalised_element = grad / (scale + 1e-06)
    (
        below_limit_line,
        above_limit_line,
        floor_limit,
        ceiling_limit,
        above_dividend_offset,
        below_dividend_offset,
        above_dividend_scale,
        below_dividend_scale,
        shared_summands,
    ) = ready_limit_lines(
        solid_occupancy,
        newer_occupancy_shift,
        older_occupancy_shift,
        below_limit_spacing,
        above_limit_spacing,
        normalised_element,
    )
    reference_point_here = jnp.sum(jnp.where(layout_candidate, shared_summands, 0.0))
    multiplier = jnp.float32(1.0)
    for step in range(NEWTON):
        chosen, g_terms, h_terms = dual_terms(
            multiplier,
            below_limit_line,
            above_limit_line,
            floor_limit,
            ceiling_limit,
            above_dividend_offset,
            below_dividend_offset,
            above_dividend_scale,
            below_dividend_scale,
        )
        slope_sum, curve = dual_reduce(
            reference_point_here + jnp.sum(jnp.where(layout_candidate, g_terms, 0.0)),
            jnp.sum(jnp.where(layout_candidate, h_terms, 0.0)),
        )
        multiplier = jnp.maximum(jnp.float32(0.0), multiplier + slope_sum / curve)
    chosen, g_terms, h_terms = dual_terms(
        multiplier,
        below_limit_line,
        above_limit_line,
        floor_limit,
        ceiling_limit,
        above_dividend_offset,
        below_dividend_offset,
        above_dividend_scale,
        below_dividend_scale,
    )
    density_new = jnp.where(layout_candidate, chosen, solid_occupancy)
    return (density_new, below_limit_line, above_limit_line, dual_state)


def solution(mesh):
    return jax.shard_map(
        on_device,
        mesh=mesh,
        in_specs=(
            P("thick", None, "facade"),
            P("thick", None, "facade"),
            P("thick", None, "facade"),
            P("thick", None, "facade"),
            P("thick", None, "facade"),
            P("thick", None, "facade"),
            P("thick", None, "facade"),
            P("thick", None, "facade"),
            P("thick", None, "facade"),
        ),
        out_specs=(
            P("thick", None, "facade"),
            P("thick", None, "facade"),
            P("thick", None, "facade"),
            P("thick", None, "facade"),
        ),
        check_vma=False,
    )
```

```python
import functools
import jax
import jax.numpy as jnp
from jax import lax
from jax.experimental import pallas as pl
from jax.experimental.pallas import tpu as pltpu
from jax.sharding import PartitionSpec as P

RADIUS = 4
SWEEPS = 3
NEWTON = 8

k_void = 0.03
k_frame = 160.0
k_glass = 1.0
k_anchor = 50.0
loss_rate = 0.05
spectrum_low = 0.05
spectrum_high = 2.0
solid_allowance = 0.35
curve_floor = 0.05
move_limit = 0.2
gamma_slope = 200.0

LANES = 128
STRIP = 16
above_weight = 1.001 + 1e-05
below_weight = 0.001 + 1e-05

f32 = jnp.float32
AXES = ("thick", "facade")
BOTH_SIDES = 16


def call(kernel, outs, args, scratch=()):
    vmem = pl.BlockSpec(memory_space=pltpu.VMEM)
    return pl.pallas_call(
        kernel,
        out_shape=[jax.ShapeDtypeStruct(shape, f32) for shape in outs],
        in_specs=[vmem] * len(args),
        out_specs=[vmem] * len(outs),
        scratch_shapes=[pltpu.VMEM(shape, f32) for shape in scratch],
        compiler_params=pltpu.CompilerParams(vmem_limit_bytes=40 * 1024 * 1024),
    )(*args)


def lane_iota(shape):
    return lax.broadcasted_iota(jnp.int32, shape, len(shape) - 1)


def sub_iota(shape):
    return lax.broadcasted_iota(jnp.int32, shape, len(shape) - 2)


def ahead(value, step, axis):
    return pltpu.roll(value, (value.shape[axis] - step) % value.shape[axis], axis)


def behind(value, step, axis):
    return pltpu.roll(value, step, axis)


def pack_kernel(*refs):
    firsts, lasts, to_left, to_right = refs[0:5], refs[5:10], refs[10], refs[11]
    rows, height, _ = to_left.shape
    group = lane_iota((height, LANES)) // STRIP
    for row in range(rows):
        for source, target, place in ((firsts, to_left, 0), (lasts, to_right, LANES - STRIP)):
            packed = jnp.zeros((height, LANES), f32)
            for index, ref in enumerate(source):
                value = ref[row]
                if value.dtype != f32:
                    value = value.astype(f32) + 1.0
                shift = (STRIP * index - place) % LANES
                if shift:
                    value = pltpu.roll(value, shift, 1)
                packed = jnp.where(group == index, value, packed)
            target[row] = packed


def halo_lanes(left, right, index):
    lane = lane_iota(left.shape)
    shift = (LANES - STRIP * index) % LANES
    after = pltpu.roll(right, shift, 1) if shift else right
    shift = (LANES - STRIP - STRIP * index) % LANES
    before = pltpu.roll(left, shift, 1) if shift else left
    return jnp.where(lane < STRIP, after, jnp.where(lane >= LANES - STRIP, before, 0.0))


def axis_weight(position, total):
    acc = jnp.zeros(position.shape, f32)
    for offset in range(-RADIUS, RADIUS + 1):
        weight = float(RADIUS + 1 - abs(offset))
        inside = (position + offset >= 0) & (position + offset < total)
        acc = acc + jnp.where(inside, weight, 0.0)
    return jnp.maximum(acc, 1.0)


def inverse_plane(height, own, cols_total, col_start):
    width = own + LANES
    lane = lane_iota((1, width))
    place = jnp.where(lane < own + LANES // 2, lane, lane - width) + col_start
    middle = axis_weight(sub_iota((height, 1)), height)
    return 1.0 / (middle * axis_weight(place, cols_total))


def row_weight(row, rows_total, row_start):
    return 1.0 / axis_weight(jnp.full((1, 1), row + row_start, jnp.int32), rows_total)


def boxes(values):
    pairs = [a + b for a, b in zip(values[:-1], values[1:])]
    fours = [a + b for a, b in zip(pairs[:-2], pairs[2:])]
    return [a + b for a, b in zip(fours, values[4:])]


def filter_depth(get, put, count):
    singles = [get(r) for r in range(count)]
    return boxes(boxes(singles))


def filter_height(value):
    height = value.shape[0]
    level = sub_iota((height, 1))
    total = float(RADIUS + 1) * value
    for offset in range(1, RADIUS + 1):
        weight = float(RADIUS + 1 - offset)
        up = jnp.where(level < height - offset, weight, 0.0)
        down = jnp.where(level >= offset, weight, 0.0)
        total = total + up * ahead(value, offset, 0) + down * behind(value, offset, 0)
    return total


def filter_lanes(value):
    def box(v):
        pair = v + ahead(v, 1, 1)
        return pair + ahead(pair, 2, 1) + behind(v, 1, 1)

    def box_back(v):
        pair = v + behind(v, 1, 1)
        return pair + behind(pair, 2, 1) + ahead(v, 1, 1)

    return box_back(box(value))


def depth_filter(source, middle, target):
    count = source.shape[0]
    for r in range(count - 4):
        middle[r] = (source[r] + source[r + 1]) + (source[r + 2] + source[r + 3]) + source[r + 4]
    for r in range(count - 8):
        target[r] = (middle[r] + middle[r + 1]) + (middle[r + 2] + middle[r + 3]) + middle[r + 4]


def rho_kernel(
    rows_total, cols_total, place,
    density, material, from_above, from_below, left, right, corner_above, corner_below,
    rho_out, cond_first, cond_last,
    ext, middle, summed,
):
    rows, height, own = density.shape
    for r in range(4):
        ext[r, :, :own] = from_above[r]
        ext[r, :, own:] = halo_lanes(corner_above[r], corner_above[4 + r], 0)
        ext[rows + 4 + r, :, :own] = from_below[r]
        ext[rows + 4 + r, :, own:] = halo_lanes(corner_below[r], corner_below[4 + r], 0)
    for r in range(rows):
        ext[4 + r, :, :own] = density[r]
        ext[4 + r, :, own:] = halo_lanes(left[r], right[r], 0)
    depth_filter(ext, middle, summed)
    row_start = place[0]
    plane = inverse_plane(height, own, cols_total, place[1])
    for r in range(rows):
        rho = filter_lanes(filter_height(summed[r])) * (
            plane * row_weight(r, rows_total, row_start)
        )
        code = jnp.concatenate(
            [material[r].astype(f32) + 1.0, halo_lanes(left[r], right[r], 1)], axis=1
        )
        frame = k_void + (k_frame - k_void) * rho * rho * rho
        cond = jnp.where(code == 2.0, frame, jnp.where(code == 1.0, k_glass, k_anchor))
        cond = jnp.where(code == 0.0, 0.0, cond)
        rho_out[r] = rho
        if r < 4:
            cond_first[r] = cond
        else:
            cond_last[r - 4] = cond


def sweep_kernel(
    rows_total, cols_total, place,
    cond_above, cond_first, cond_last, cond_below, rho, material,
    prior, source, temp, rows_above, rows_below, left, right, corner_above, corner_below,
    dual_out, weighted_first, weighted_last,
    cond, field, load, heat, depth_face, height_face, lane_face, inverse, residual, next_field, dual,
):
    rows, height, own = prior.shape
    width = own + LANES
    last_level = sub_iota((height, 1)) == height - 1
    for r in range(4):
        cond[r] = cond_above[r]
        cond[4 + r] = cond_first[r]
        cond[8 + r] = cond_last[r]
        cond[12 + r] = cond_below[r]
    for r in range(4):
        field[r, :, :own] = rows_above[r]
        field[r, :, own:] = halo_lanes(corner_above[r], corner_above[4 + r], 3)
        field[12 + r, :, :own] = rows_below[r]
        field[12 + r, :, own:] = halo_lanes(corner_below[r], corner_below[4 + r], 3)
    for r in range(3):
        load[1 + r, :, :own] = rows_above[4 + r]
        load[1 + r, :, own:] = halo_lanes(corner_above[1 + r], corner_above[5 + r], 2)
        load[12 + r, :, :own] = rows_below[4 + r]
        load[12 + r, :, own:] = halo_lanes(corner_below[r], corner_below[4 + r], 2)
    heat[0, :, :own] = rows_above[7]
    heat[0, :, own:] = halo_lanes(corner_above[3], corner_above[7], 4)
    heat[9, :, :own] = rows_below[7]
    heat[9, :, own:] = halo_lanes(corner_below[0], corner_below[4], 4)
    for r in range(rows):
        field[4 + r, :, :own] = prior[r]
        field[4 + r, :, own:] = halo_lanes(left[r], right[r], 3)
        load[4 + r, :, :own] = source[r]
        load[4 + r, :, own:] = halo_lanes(left[r], right[r], 2)
        heat[1 + r, :, :own] = temp[r]
        heat[1 + r, :, own:] = halo_lanes(left[r], right[r], 4)

    def face(one, other):
        return 2.0 * one * other / jnp.maximum(one + other, 1e-3)

    depth_face[0] = face(cond[0], cond[1])

    def make_faces(r, carry):
        here = cond[r]
        deep = face(here, cond[r + 1])
        tall = jnp.where(last_level, 0.0, face(here, ahead(here, 1, 0)))
        wide = face(here, ahead(here, 1, 1))
        depth_face[r] = deep
        height_face[r] = tall
        lane_face[r] = wide
        diagonal = (
            loss_rate + (deep + depth_face[r - 1]) + (tall + behind(tall, 1, 0))
            + (wide + behind(wide, 1, 1))
        )
        inverse[r] = 1.0 / diagonal
        return carry

    lax.fori_loop(1, 15, make_faces, 0)

    def product(ref, r):
        here = ref[r]
        deep = depth_face[r] * (here - ref[r + 1]) + depth_face[r - 1] * (here - ref[r - 1])
        tall = height_face[r] * (here - ahead(here, 1, 0))
        wide = lane_face[r] * (here - ahead(here, 1, 1))
        return (
            loss_rate * here + deep + (tall - behind(tall, 1, 0)) + (wide - behind(wide, 1, 1))
        )

    centre = 0.5 * (spectrum_high + spectrum_low)
    half = 0.5 * (spectrum_high - spectrum_low)
    ratio = centre / half

    def begin(r, carry):
        left_over = load[r] - product(field, r)
        residual[r] = left_over
        direction = left_over * inverse[r] * (1.0 / centre)
        next_field[r] = direction
        dual[r] = field[r] + direction
        return carry

    lax.fori_loop(1, 15, begin, 0)
    factor = 1.0 / ratio
    now, then = next_field, field
    for sweep in range(SWEEPS - 1):
        factor_next = 1.0 / (2.0 * ratio - factor)
        keep, add = factor_next * factor, 2.0 * factor_next / half

        def step(r, carry, now=now, then=then, keep=keep, add=add):
            left_over = residual[r] - product(now, r)
            residual[r] = left_over
            direction = keep * now[r] + add * (left_over * inverse[r])
            then[r] = direction
            dual[r] = dual[r] + direction
            return carry

        lax.fori_loop(2 + sweep, 14 - sweep, step, 0)
        factor = factor_next
        now, then = then, now

    row_start = place[0]
    plane = inverse_plane(height, own, cols_total, place[1])
    for r in range(rows):
        dual_out[r] = dual[4 + r, :, :own]

    def sens(r, deep_before):
        c, a, t = cond[r], dual[r], heat[r - 3]

        def shared(c_q, a_q, t_q):
            inv = 1.0 / jnp.maximum(c + c_q, 1e-3)
            return (a - a_q) * (t - t_q) * (inv * inv)

        c_q = cond[r + 1]
        deep = shared(c_q, dual[r + 1], heat[r - 2])
        c_sq = c * c
        total = deep * (c_q * c_q)
        deep_next = deep * c_sq
        c_q = ahead(c, 1, 0)
        tall = jnp.where(last_level, 0.0, shared(c_q, ahead(a, 1, 0), ahead(t, 1, 0)))
        total = total + tall * (c_q * c_q) + behind(tall * c_sq, 1, 0)
        c_q = ahead(c, 1, 1)
        wide = shared(c_q, ahead(a, 1, 1), ahead(t, 1, 1))
        total = total + wide * (c_q * c_q) + behind(wide * c_sq, 1, 1)
        return -2.0 * (total + deep_before), deep_next

    c, c_q = cond[3], cond[4]
    inv = 1.0 / jnp.maximum(c + c_q, 1e-3)
    deep_before = (dual[3] - dual[4]) * (heat[0] - heat[1]) * (inv * inv) * (c * c)
    for r in range(rows):
        value, deep_before = sens(4 + r, deep_before)
        code = jnp.concatenate(
            [material[r].astype(f32) + 1.0, halo_lanes(left[r], right[r], 1)], axis=1
        )
        squared = rho[r] * rho[r]
        value = value * (3.0 * (k_frame - k_void)) * squared * (
            plane * row_weight(r, rows_total, row_start)
        )
        value = jnp.where(code == 2.0, value, 0.0)
        if r < 4:
            weighted_first[r] = value
        else:
            weighted_last[r - 4] = value


def grad_kernel(from_above, first, last, from_below, material, grad_out, message, ext, middle, summed):
    rows, height, own = grad_out.shape
    for r in range(4):
        ext[r] = from_above[r]
        ext[4 + r] = first[r]
        ext[8 + r] = last[r]
        ext[12 + r] = from_below[r]
    depth_filter(ext, middle, summed)
    largest = jnp.zeros((height, LANES), f32)
    for r in range(rows):
        grad = filter_lanes(filter_height(summed[r]))[:, :own]
        grad_out[r] = grad
        size = jnp.where(material[r] == 1, jnp.abs(grad), 0.0)
        for block in range(own // LANES):
            largest = jnp.maximum(largest, size[:, block * LANES:(block + 1) * LANES])
    message[...] = jnp.broadcast_to(jnp.max(largest, axis=0, keepdims=True), message.shape)


def lines_kernel(
    solid, newer, older, below_spacing, above_spacing, material,
    below_out, above_out, up_out, low_out, least_out, most_out, upper_out, lower_out, bend_out,
    tallies,
):
    rows, height, own = solid.shape
    base = jnp.zeros((height, LANES), f32)
    count = jnp.zeros((height, LANES), f32)
    for r in range(rows):
        x = solid[r]
        design = material[r] == 1
        gamma = 0.95 + 0.25 * jnp.tanh(gamma_slope * newer[r] * older[r])
        below = x - gamma * below_spacing[r]
        above = x + gamma * above_spacing[r]
        below_out[r] = below
        above_out[r] = above
        up = above - x
        low = x - below
        floor = jnp.maximum(jnp.maximum(0.0, below + 0.1 * low), x - move_limit)
        ceiling = jnp.minimum(jnp.minimum(1.0, above - 0.1 * up), x + move_limit)
        up_out[r] = up
        low_out[r] = low
        least_out[r] = floor - below
        most_out[r] = ceiling - below
        upper_out[r] = jnp.where(design, above_weight * up * up, 0.0)
        lower_out[r] = jnp.where(design, below_weight * low * low, 0.0)
        bend_out[r] = jnp.where(design, up * low / (2.0 * (up + low)), 0.0)
        term = jnp.where(
            design, x - solid_allowance - above_weight * up - below_weight * low, 0.0
        )
        one = jnp.where(design, curve_floor, 0.0)
        for block in range(own // LANES):
            base = base + term[:, block * LANES:(block + 1) * LANES]
            count = count + one[:, block * LANES:(block + 1) * LANES]
    tallies[0] = base
    tallies[1] = count


def reached(rate_above, rate_below, y, up, low, least, most):
    root_above = rate_above + y * above_weight
    root_below = rate_below + y * below_weight
    inv_above, inv_below = lax.rsqrt(root_above), lax.rsqrt(root_below)
    root_above, root_below = root_above * inv_above, root_below * inv_below
    width = up + low
    pull = low * root_below
    trial = width * pull / (up * root_above + pull)
    return trial, jnp.clip(trial, least, most), width, root_above, root_below, inv_above, inv_below


def sums_to_message(slope, curve, message):
    slope = jnp.sum(slope, axis=0, keepdims=True)
    curve = jnp.sum(curve, axis=0, keepdims=True)
    slope = slope + pltpu.roll(slope, LANES // 2, 1)
    curve = curve + pltpu.roll(curve, LANES // 2, 1)
    lane = lane_iota((1, LANES))
    message[...] = jnp.broadcast_to(jnp.where(lane < LANES // 2, slope, curve), message.shape)


def evaluate(y, rate_above, rate_below, up, low, least, most, upper, lower, bend, tallies, message):
    rows, height, own = up.shape
    slope_sum, curve_sum = tallies[0], tallies[1]
    for r in range(rows):
        trial, chosen, width, root_above, root_below, inv_above, inv_below = reached(
            rate_above(r), rate_below(r), y, up[r], low[r], least[r], most[r]
        )
        rest = width - chosen
        slope = (upper[r] * chosen + lower[r] * rest) / (rest * chosen)
        split = above_weight * (inv_above * inv_above) - below_weight * (inv_below * inv_below)
        curve = bend[r] * (root_above * root_below) * (split * split)
        free = (trial > least[r]) & (trial < most[r])
        curve = jnp.where(free, curve, 0.0)
        for block in range(own // LANES):
            slope_sum = slope_sum + slope[:, block * LANES:(block + 1) * LANES]
            curve_sum = curve_sum + curve[:, block * LANES:(block + 1) * LANES]
    sums_to_message(slope_sum, curve_sum, message)


def first_kernel(
    arrived, grad, up, low, least, most, upper, lower, bend, tallies,
    message, rate_above_out, rate_below_out,
):
    scale = jnp.max(jnp.max(arrived[...], axis=0, keepdims=True), axis=1, keepdims=True)
    inverse = 1.0 / (scale + 1e-06)

    def above(r):
        element = grad[r] * inverse
        value = jnp.maximum(1.001 * element, -0.001 * element) + 1e-05
        rate_above_out[r] = value
        return value

    def below(r):
        element = grad[r] * inverse
        value = jnp.maximum(0.001 * element, -1.001 * element) + 1e-05
        rate_below_out[r] = value
        return value

    evaluate(
        jnp.ones((1, 1), f32), above, below, up, low, least, most, upper, lower, bend, tallies, message
    )


def advance(arrived, y):
    total = jnp.sum(arrived[...], axis=0, keepdims=True)
    lane = lane_iota(total.shape)
    slope = jnp.sum(jnp.where(lane < LANES // 2, total, 0.0), axis=1, keepdims=True)
    curve = jnp.sum(jnp.where(lane < LANES // 2, 0.0, total), axis=1, keepdims=True)
    return jnp.maximum(0.0, y + slope / curve)


def step_kernel(
    arrived, y_ref, rate_above, rate_below, up, low, least, most, upper, lower, bend, tallies,
    message, y_out,
):
    y = advance(arrived, y_ref[0:1, 0:1])
    y_out[...] = jnp.broadcast_to(y, y_out.shape)
    evaluate(
        y, lambda r: rate_above[r], lambda r: rate_below[r],
        up, low, least, most, upper, lower, bend, tallies, message,
    )


def last_kernel(
    arrived, y_ref, rate_above, rate_below, up, low, least, most, below, solid, material, out
):
    y = advance(arrived, y_ref[0:1, 0:1])
    for r in range(out.shape[0]):
        chosen = reached(rate_above[r], rate_below[r], y, up[r], low[r], least[r], most[r])[1]
        out[r] = jnp.where(material[r] == 1, below[r] + chosen, solid[r])


def with_place(kernel, rows_total, cols_total):
    def body(place_ref, *refs):
        kernel(rows_total, cols_total, (place_ref[0], place_ref[1]), *refs)

    return body


def placed_call(kernel, place, outs, args, scratch, totals):
    vmem = pl.BlockSpec(memory_space=pltpu.VMEM)
    return pl.pallas_call(
        with_place(kernel, *totals),
        out_shape=[jax.ShapeDtypeStruct(shape, f32) for shape in outs],
        in_specs=[pl.BlockSpec(memory_space=pltpu.SMEM)] + [vmem] * len(args),
        out_specs=[vmem] * len(outs),
        scratch_shapes=[pltpu.VMEM(shape, f32) for shape in scratch],
        compiler_params=pltpu.CompilerParams(vmem_limit_bytes=40 * 1024 * 1024),
    )(place, *args)


def pack_strips(arrays):
    rows, height, own = arrays[0].shape
    end = own // LANES - 1
    block = (rows, height, LANES)
    first = pl.BlockSpec(block, lambda i: (0, 0, 0))
    last = pl.BlockSpec(block, lambda i: (0, 0, end))
    out = pl.BlockSpec(block, lambda i: (0, 0, 0))
    return pl.pallas_call(
        pack_kernel,
        grid=(1,),
        out_shape=[jax.ShapeDtypeStruct(block, f32)] * 2,
        in_specs=[first] * 5 + [last] * 5,
        out_specs=[out] * 2,
    )(*arrays, *arrays)


def on_device(
    solid_occupancy,
    newer_occupancy_shift,
    older_occupancy_shift,
    below_limit_spacing,
    above_limit_spacing,
    thermal_state,
    loss_state_derivative,
    prior_dual_state,
    cell_material,
):
    rows, height, own = solid_occupancy.shape
    deep, long = lax.axis_size("thick"), lax.axis_size("facade")
    totals = (rows * deep, own * long)
    place = jnp.stack(
        [lax.axis_index("thick") * rows, lax.axis_index("facade") * own]
    ).astype(jnp.int32)
    width = own + LANES
    whole = (rows, height, own)

    def shift(axis, size, step):
        pairs = [(i, i + step) for i in range(size) if 0 <= i + step < size]
        return lambda value: lax.ppermute(value, axis, pairs)

    to_right, to_left = shift("facade", long, 1), shift("facade", long, -1)
    to_deeper, to_nearer = shift("thick", deep, 1), shift("thick", deep, -1)

    first_strips, last_strips = pack_strips(
        (solid_occupancy, cell_material, loss_state_derivative, prior_dual_state, thermal_state)
    )
    right, left = to_left(first_strips), to_right(last_strips)
    density_above, density_below = (
        to_deeper(solid_occupancy[rows - 4:]),
        to_nearer(solid_occupancy[:4]),
    )
    rows_above = to_deeper(
        jnp.concatenate(
            [prior_dual_state[rows - 4:], loss_state_derivative[rows - 3:], thermal_state[rows - 1:]]
        )
    )
    rows_below = to_nearer(
        jnp.concatenate([prior_dual_state[:4], loss_state_derivative[:3], thermal_state[:1]])
    )
    corner_above = to_deeper(jnp.concatenate([left[rows - 4:], right[rows - 4:]]))
    corner_below = to_nearer(jnp.concatenate([left[:4], right[:4]]))

    (below, above, up, low, least, most, upper, lower, bend, tallies) = call(
        lines_kernel,
        [whole] * 9 + [(2, height, LANES)],
        (
            solid_occupancy, newer_occupancy_shift, older_occupancy_shift,
            below_limit_spacing, above_limit_spacing, cell_material,
        ),
    )

    four = (4, height, width)
    rho, cond_first, cond_last = placed_call(
        rho_kernel, place,
        [(rows, height, width), four, four],
        (
            solid_occupancy, cell_material, density_above, density_below, left, right,
            corner_above, corner_below,
        ),
        [(BOTH_SIDES, height, width), (BOTH_SIDES - 4, height, width), (rows, height, width)],
        totals,
    )
    cond_above, cond_below = to_deeper(cond_last), to_nearer(cond_first)
    tall = (BOTH_SIDES, height, width)
    dual_state, weighted_first, weighted_last = placed_call(
        sweep_kernel, place,
        [whole, four, four],
        (
            cond_above, cond_first, cond_last, cond_below, rho, cell_material,
            prior_dual_state, loss_state_derivative, thermal_state, rows_above, rows_below,
            left, right, corner_above, corner_below,
        ),
        [tall, tall, tall, (10, height, width)] + [tall] * 7,
        totals,
    )
    weighted_above, weighted_below = to_deeper(weighted_last), to_nearer(weighted_first)
    count = deep * long
    note = (count, LANES)
    grad, message = call(
        grad_kernel,
        [whole, note],
        (weighted_above, weighted_first, weighted_last, weighted_below, cell_material),
        [tall, (BOTH_SIDES - 4, height, width), (rows, height, width)],
    )

    def everyone(rows_out):
        return lax.all_to_all(rows_out, AXES, 0, 0, tiled=True)

    fixed = (up, low, least, most, upper, lower, bend, tallies)
    message, rate_above, rate_below = call(
        first_kernel, [note, whole, whole], (everyone(message), grad) + fixed
    )
    y = jnp.ones((8, LANES), f32)
    for _ in range(NEWTON - 1):
        message, y = call(
            step_kernel, [note, (8, LANES)],
            (everyone(message), y, rate_above, rate_below) + fixed,
        )
    (density_new,) = call(
        last_kernel, [whole],
        (
            everyone(message), y, rate_above, rate_below, up, low, least, most, below,
            solid_occupancy, cell_material,
        ),
    )
    return (density_new, below, above, dual_state)


def solution(mesh):
    spec = P("thick", None, "facade")
    return jax.shard_map(
        on_device,
        mesh=mesh,
        in_specs=(spec,) * 9,
        out_specs=(spec,) * 4,
        check_vma=False,
    )
```

```python
import functools
import jax
import jax.numpy as jnp
from jax import lax
from jax.experimental import pallas as pl
from jax.experimental.pallas import tpu as pltpu
from jax.sharding import PartitionSpec as P

RADIUS = 4
SWEEPS = 3
NEWTON = 8

k_void = 0.03
k_frame = 160.0
k_glass = 1.0
k_anchor = 50.0
loss_rate = 0.05
spectrum_low = 0.05
spectrum_high = 2.0
solid_allowance = 0.35
curve_floor = 0.05
move_limit = 0.2
gamma_slope = 200.0

LANES = 128
STRIP = 16
above_weight = 1.001 + 1e-05
below_weight = 0.001 + 1e-05

f32 = jnp.float32
AXES = ("thick", "facade")
BOTH_SIDES = 16


def call(kernel, outs, args, scratch=()):
    vmem = pl.BlockSpec(memory_space=pltpu.VMEM)
    return pl.pallas_call(
        kernel,
        out_shape=[jax.ShapeDtypeStruct(shape, f32) for shape in outs],
        in_specs=[vmem] * len(args),
        out_specs=[vmem] * len(outs),
        scratch_shapes=[pltpu.VMEM(shape, f32) for shape in scratch],
        compiler_params=pltpu.CompilerParams(vmem_limit_bytes=40 * 1024 * 1024),
    )(*args)


def lane_iota(shape):
    return lax.broadcasted_iota(jnp.int32, shape, len(shape) - 1)


def sub_iota(shape):
    return lax.broadcasted_iota(jnp.int32, shape, len(shape) - 2)


def ahead(value, step, axis):
    return pltpu.roll(value, (value.shape[axis] - step) % value.shape[axis], axis)


def behind(value, step, axis):
    return pltpu.roll(value, step, axis)


def pack_kernel(*refs):
    firsts, lasts, to_left, to_right = refs[0:5], refs[5:10], refs[10], refs[11]
    rows, height, _ = to_left.shape
    group = lane_iota((height, LANES)) // STRIP
    for row in range(rows):
        for source, target, place in ((firsts, to_left, 0), (lasts, to_right, LANES - STRIP)):
            packed = jnp.zeros((height, LANES), f32)
            for index, ref in enumerate(source):
                value = ref[row]
                if value.dtype != f32:
                    value = value.astype(f32) + 1.0
                shift = (STRIP * index - place) % LANES
                if shift:
                    value = pltpu.roll(value, shift, 1)
                packed = jnp.where(group == index, value, packed)
            target[row] = packed


def halo_lanes(left, right, index):
    lane = lane_iota(left.shape)
    shift = (LANES - STRIP * index) % LANES
    after = pltpu.roll(right, shift, 1) if shift else right
    shift = (LANES - STRIP - STRIP * index) % LANES
    before = pltpu.roll(left, shift, 1) if shift else left
    return jnp.where(lane < STRIP, after, jnp.where(lane >= LANES - STRIP, before, 0.0))


def axis_weight(position, total):
    acc = jnp.zeros(position.shape, f32)
    for offset in range(-RADIUS, RADIUS + 1):
        weight = float(RADIUS + 1 - abs(offset))
        inside = (position + offset >= 0) & (position + offset < total)
        acc = acc + jnp.where(inside, weight, 0.0)
    return jnp.maximum(acc, 1.0)


def inverse_plane(height, own, cols_total, col_start):
    width = own + LANES
    lane = lane_iota((1, width))
    place = jnp.where(lane < own + LANES // 2, lane, lane - width) + col_start
    middle = axis_weight(sub_iota((height, 1)), height)
    return 1.0 / (middle * axis_weight(place, cols_total))


def row_weight(row, rows_total, row_start):
    return 1.0 / axis_weight(jnp.full((1, 1), row + row_start, jnp.int32), rows_total)


def filter_height(value):
    height = value.shape[0]
    level = sub_iota((height, 1))
    total = float(RADIUS + 1) * value
    for offset in range(1, RADIUS + 1):
        weight = float(RADIUS + 1 - offset)
        up = jnp.where(level < height - offset, weight, 0.0)
        down = jnp.where(level >= offset, weight, 0.0)
        total = total + up * ahead(value, offset, 0) + down * behind(value, offset, 0)
    return total


def filter_lanes(value):
    def box(v):
        pair = v + ahead(v, 1, 1)
        return pair + ahead(pair, 2, 1) + behind(v, 1, 1)

    def box_back(v):
        pair = v + behind(v, 1, 1)
        return pair + behind(pair, 2, 1) + ahead(v, 1, 1)

    return box_back(box(value))


def depth_filter(source, middle, target):
    count = source.shape[0]
    for r in range(count - 4):
        middle[r] = (source[r] + source[r + 1]) + (source[r + 2] + source[r + 3]) + source[r + 4]
    for r in range(count - 8):
        target[r] = (middle[r] + middle[r + 1]) + (middle[r + 2] + middle[r + 3]) + middle[r + 4]


def present(place, rows, own, rows_total, cols_total):
    row_start, col_start = place

    def flag(condition):
        return jnp.where(condition, 1.0, 0.0).astype(f32)

    return (
        flag(row_start > 0), flag(row_start + rows < rows_total),
        flag(col_start > 0), flag(col_start + own < cols_total),
    )


def corner(message, row):
    lanes = slice(row * LANES, (row + 1) * LANES)
    return message[12, :, lanes], message[13, :, lanes]


def rho_kernel(
    rows_total, cols_total, place,
    density, material, from_above, from_below, left, right,
    rho_out, cond_first, cond_last,
    ext, middle, summed,
):
    rows, height, own = density.shape
    has_above, has_below, has_left, has_right = present(place, rows, own, rows_total, cols_total)

    def halo(strips, index):
        return halo_lanes(strips[0] * has_left, strips[1] * has_right, index)

    for r in range(4):
        ext[r, :, :own] = from_above[r] * has_above
        ext[r, :, own:] = halo(corner(from_above, r), 0) * has_above
        ext[rows + 4 + r, :, :own] = from_below[r] * has_below
        ext[rows + 4 + r, :, own:] = halo(corner(from_below, r), 0) * has_below
    for r in range(rows):
        ext[4 + r, :, :own] = density[r]
        ext[4 + r, :, own:] = halo((left[r], right[r]), 0)
    depth_filter(ext, middle, summed)
    plane = inverse_plane(height, own, cols_total, place[1])
    for r in range(rows):
        rho = filter_lanes(filter_height(summed[r])) * (
            plane * row_weight(r, rows_total, place[0])
        )
        code = jnp.concatenate(
            [material[r].astype(f32) + 1.0, halo((left[r], right[r]), 1)], axis=1
        )
        frame = k_void + (k_frame - k_void) * rho * rho * rho
        cond = jnp.where(code == 2.0, frame, jnp.where(code == 1.0, k_glass, k_anchor))
        cond = jnp.where(code == 0.0, 0.0, cond)
        rho_out[r] = rho
        if r < 4:
            cond_first[r] = cond
        else:
            cond_last[r - 4] = cond


def sweep_kernel(
    rows_total, cols_total, place,
    cond_above, cond_first, cond_last, cond_below, rho, material,
    prior, source, temp, from_above, from_below, left, right, tallies,
    dual_out, weighted_first, weighted_last,
    cond, field, load, heat, depth_face, height_face, lane_face, inverse, residual, next_field, dual,
    depth_here, depth_there, height_here, height_there, lane_here, lane_there,
):
    rows, height, own = prior.shape
    has_above, has_below, has_left, has_right = present(place, rows, own, rows_total, cols_total)
    last_level = sub_iota((height, 1)) == height - 1
    for r in range(4):
        cond[r] = cond_above[r] * has_above
        cond[4 + r] = cond_first[r]
        cond[8 + r] = cond_last[r]
        cond[12 + r] = cond_below[r] * has_below

    def place_row(target, row, main, strips, index):
        target[row, :, :own] = main
        target[row, :, own:] = halo_lanes(strips[0], strips[1], index)

    for r in range(4):
        place_row(field, r, from_above[4 + r], corner(from_above, r), 3)
        place_row(field, 12 + r, from_below[4 + r], corner(from_below, r), 3)
    for r in range(3):
        place_row(load, 1 + r, from_above[8 + r], corner(from_above, 1 + r), 2)
        place_row(load, 12 + r, from_below[8 + r], corner(from_below, r), 2)
    place_row(heat, 0, from_above[11], corner(from_above, 3), 4)
    place_row(heat, 9, from_below[11], corner(from_below, 0), 4)
    for r in range(rows):
        strips = (left[r], right[r])
        place_row(field, 4 + r, prior[r], strips, 3)
        place_row(load, 4 + r, source[r], strips, 2)
        place_row(heat, 1 + r, temp[r], strips, 4)

    centre = 0.5 * (spectrum_high + spectrum_low)
    half = 0.5 * (spectrum_high - spectrum_low)
    ratio = centre / half

    def face(one, other, keep, row, here, there):
        inv = 1.0 / jnp.maximum(one + other, 1e-3)
        part = one * inv
        if keep:
            rest = other * inv
            there[row] = part * part
            here[row] = rest * rest
        return 2.0 * part * other

    here = cond[0]
    following = cond[1]
    deep_before = face(here, following, False, 0, depth_here, depth_there)
    depth_face[0] = deep_before
    flux_before = deep_before * (field[0] - field[1])
    for r in range(1, 15):
        here, following = following, cond[r + 1]
        deep = face(here, following, 3 <= r < 12, r, depth_here, depth_there)
        tall = face(here, ahead(here, 1, 0), 4 <= r < 12, r, height_here, height_there)
        tall = jnp.where(last_level, 0.0, tall)
        wide = face(here, ahead(here, 1, 1), 4 <= r < 12, r, lane_here, lane_there)
        depth_face[r] = deep
        height_face[r] = tall
        lane_face[r] = wide
        inv_diagonal = 1.0 / (
            loss_rate + (deep + deep_before) + (tall + behind(tall, 1, 0))
            + (wide + behind(wide, 1, 1))
        )
        inverse[r] = inv_diagonal
        value = field[r]
        flux = deep * (value - field[r + 1])
        high = tall * (value - ahead(value, 1, 0))
        along = wide * (value - ahead(value, 1, 1))
        product = (
            loss_rate * value + (flux - flux_before) + (high - behind(high, 1, 0))
            + (along - behind(along, 1, 1))
        )
        left_over = load[r] - product
        residual[r] = left_over
        direction = left_over * inv_diagonal * (1.0 / centre)
        next_field[r] = direction
        if 3 <= r < 13:
            dual[r] = value + direction
        deep_before, flux_before = deep, flux

    factor = 1.0 / ratio
    now, then = next_field, field
    for sweep in range(SWEEPS - 1):
        factor_next = 1.0 / (2.0 * ratio - factor)
        keep, add = factor_next * factor, 2.0 * factor_next / half
        start, stop = 2 + sweep, 14 - sweep
        following = now[start]
        flux_before = depth_face[start - 1] * (now[start - 1] - following)
        for r in range(start, stop):
            value, following = following, now[r + 1]
            flux = depth_face[r] * (value - following)
            high = height_face[r] * (value - ahead(value, 1, 0))
            along = lane_face[r] * (value - ahead(value, 1, 1))
            product = (
                loss_rate * value + (flux - flux_before) + (high - behind(high, 1, 0))
                + (along - behind(along, 1, 1))
            )
            left_over = residual[r] - product
            if sweep < SWEEPS - 2:
                residual[r] = left_over
            direction = keep * value + add * (left_over * inverse[r])
            then[r] = direction
            if 3 <= r < 13:
                dual[r] = dual[r] + direction
            flux_before = flux
        factor = factor_next
        now, then = then, now

    plane = inverse_plane(height, own, cols_total, place[1])
    for r in range(rows):
        dual_out[r] = dual[4 + r, :, :own]
    a, t = dual[3], heat[0]
    a_next, t_next = dual[4], heat[1]
    deep_before = (a - a_next) * (t - t_next) * depth_there[3]
    for r in range(4, 4 + rows):
        a, t = a_next, t_next
        a_next, t_next = dual[r + 1], heat[r - 2]
        deep = (a - a_next) * (t - t_next)
        tall = (a - ahead(a, 1, 0)) * (t - ahead(t, 1, 0))
        tall = jnp.where(last_level, 0.0, tall)
        wide = (a - ahead(a, 1, 1)) * (t - ahead(t, 1, 1))
        total = (
            (deep * depth_here[r] + deep_before)
            + (tall * height_here[r] + behind(tall * height_there[r], 1, 0))
            + (wide * lane_here[r] + behind(wide * lane_there[r], 1, 1))
        )
        deep_before = deep * depth_there[r]
        row = r - 4
        strips = halo_lanes(left[row] * has_left, right[row] * has_right, 1)
        code = jnp.concatenate([material[row].astype(f32) + 1.0, strips], axis=1)
        thick_rho = rho[row]
        value = total * (thick_rho * thick_rho) * (
            plane * (row_weight(row, rows_total, place[0]) * (-6.0 * (k_frame - k_void)))
        )
        value = jnp.where(code == 2.0, value, 0.0)
        if row < 4:
            weighted_first[row] = value
        else:
            weighted_last[row - 4] = value


def grad_kernel(
    rows_total, cols_total, place,
    from_above, first, last, from_below, material, grad_out, message, ext, middle, summed,
):
    rows, height, own = grad_out.shape
    has_above, has_below, _, _ = present(place, rows, own, rows_total, cols_total)
    for r in range(4):
        ext[r] = from_above[r] * has_above
        ext[4 + r] = first[r]
        ext[8 + r] = last[r]
        ext[12 + r] = from_below[r] * has_below
    depth_filter(ext, middle, summed)
    largest = jnp.zeros((height, LANES), f32)
    for r in range(rows):
        grad = filter_lanes(filter_height(summed[r]))[:, :own]
        grad_out[r] = grad
        size = jnp.where(material[r] == 1, jnp.abs(grad), 0.0)
        for block in range(own // LANES):
            largest = jnp.maximum(largest, size[:, block * LANES:(block + 1) * LANES])
    message[...] = jnp.broadcast_to(jnp.max(largest, axis=0, keepdims=True), message.shape)


def lines_kernel(
    solid, newer, older, below_spacing, above_spacing, material,
    below_out, above_out, up_out, low_out, least_out, most_out, upper_out, lower_out, bend_out,
    tallies,
):
    rows, height, own = solid.shape
    base = jnp.zeros((height, LANES), f32)
    count = jnp.zeros((height, LANES), f32)
    for r in range(rows):
        x = solid[r]
        design = material[r] == 1
        gamma = 0.95 + 0.25 * jnp.tanh(gamma_slope * newer[r] * older[r])
        below = x - gamma * below_spacing[r]
        above = x + gamma * above_spacing[r]
        below_out[r] = below
        above_out[r] = above
        up = above - x
        low = x - below
        floor = jnp.maximum(jnp.maximum(0.0, below + 0.1 * low), x - move_limit)
        ceiling = jnp.minimum(jnp.minimum(1.0, above - 0.1 * up), x + move_limit)
        up_out[r] = up
        low_out[r] = low
        least_out[r] = floor - below
        most_out[r] = ceiling - below
        upper_out[r] = jnp.where(design, above_weight * up * up, 0.0)
        lower_out[r] = jnp.where(design, below_weight * low * low, 0.0)
        bend_out[r] = jnp.where(design, up * low / (2.0 * (up + low)), 0.0)
        term = jnp.where(
            design, x - solid_allowance - above_weight * up - below_weight * low, 0.0
        )
        one = jnp.where(design, curve_floor, 0.0)
        for block in range(own // LANES):
            base = base + term[:, block * LANES:(block + 1) * LANES]
            count = count + one[:, block * LANES:(block + 1) * LANES]
    tallies[0] = base
    tallies[1] = count


def reached(rate_above, rate_below, y, up, low, least, most):
    root_above = rate_above + y * above_weight
    root_below = rate_below + y * below_weight
    inv_above, inv_below = lax.rsqrt(root_above), lax.rsqrt(root_below)
    root_above, root_below = root_above * inv_above, root_below * inv_below
    width = up + low
    pull = low * root_below
    trial = width * pull / (up * root_above + pull)
    return trial, jnp.clip(trial, least, most), width, root_above, root_below, inv_above, inv_below


def sums_to_message(slope, curve, message):
    slope = jnp.sum(slope, axis=0, keepdims=True)
    curve = jnp.sum(curve, axis=0, keepdims=True)
    slope = slope + pltpu.roll(slope, LANES // 2, 1)
    curve = curve + pltpu.roll(curve, LANES // 2, 1)
    lane = lane_iota((1, LANES))
    message[...] = jnp.broadcast_to(jnp.where(lane < LANES // 2, slope, curve), message.shape)


def evaluate(y, rate_above, rate_below, up, low, least, most, upper, lower, bend, tallies, message):
    rows, height, own = up.shape
    slope_sum, curve_sum = tallies[0], tallies[1]
    for r in range(rows):
        trial, chosen, width, root_above, root_below, inv_above, inv_below = reached(
            rate_above(r), rate_below(r), y, up[r], low[r], least[r], most[r]
        )
        rest = width - chosen
        slope = (upper[r] * chosen + lower[r] * rest) / (rest * chosen)
        split = above_weight * (inv_above * inv_above) - below_weight * (inv_below * inv_below)
        curve = bend[r] * (root_above * root_below) * (split * split)
        free = (trial > least[r]) & (trial < most[r])
        curve = jnp.where(free, curve, 0.0)
        for block in range(own // LANES):
            slope_sum = slope_sum + slope[:, block * LANES:(block + 1) * LANES]
            curve_sum = curve_sum + curve[:, block * LANES:(block + 1) * LANES]
    sums_to_message(slope_sum, curve_sum, message)


def first_kernel(
    arrived, grad, up, low, least, most, upper, lower, bend, tallies,
    message, rate_above_out, rate_below_out,
):
    scale = jnp.max(jnp.max(arrived[...], axis=0, keepdims=True), axis=1, keepdims=True)
    inverse = 1.0 / (scale + 1e-06)

    def above(r):
        element = grad[r] * inverse
        value = jnp.maximum(1.001 * element, -0.001 * element) + 1e-05
        rate_above_out[r] = value
        return value

    def below(r):
        element = grad[r] * inverse
        value = jnp.maximum(0.001 * element, -1.001 * element) + 1e-05
        rate_below_out[r] = value
        return value

    evaluate(
        jnp.ones((1, 1), f32), above, below, up, low, least, most, upper, lower, bend, tallies, message
    )


def advance(arrived, y):
    total = jnp.sum(arrived[...], axis=0, keepdims=True)
    lane = lane_iota(total.shape)
    slope = jnp.sum(jnp.where(lane < LANES // 2, total, 0.0), axis=1, keepdims=True)
    curve = jnp.sum(jnp.where(lane < LANES // 2, 0.0, total), axis=1, keepdims=True)
    return jnp.maximum(0.0, y + slope / curve)


def step_kernel(
    arrived, y_ref, rate_above, rate_below, up, low, least, most, upper, lower, bend, tallies,
    message, y_out,
):
    y = advance(arrived, y_ref[0:1, 0:1])
    y_out[...] = jnp.broadcast_to(y, y_out.shape)
    evaluate(
        y, lambda r: rate_above[r], lambda r: rate_below[r],
        up, low, least, most, upper, lower, bend, tallies, message,
    )


def last_kernel(
    arrived, y_ref, rate_above, rate_below, up, low, least, most, below, solid, material, out
):
    y = advance(arrived, y_ref[0:1, 0:1])
    for r in range(out.shape[0]):
        chosen = reached(rate_above[r], rate_below[r], y, up[r], low[r], least[r], most[r])[1]
        out[r] = jnp.where(material[r] == 1, below[r] + chosen, solid[r])


def with_place(kernel, rows_total, cols_total):
    def body(place_ref, *refs):
        kernel(rows_total, cols_total, (place_ref[0], place_ref[1]), *refs)

    return body


def placed_call(kernel, place, outs, args, scratch, totals):
    vmem = pl.BlockSpec(memory_space=pltpu.VMEM)
    return pl.pallas_call(
        with_place(kernel, *totals),
        out_shape=[jax.ShapeDtypeStruct(shape, f32) for shape in outs],
        in_specs=[pl.BlockSpec(memory_space=pltpu.SMEM)] + [vmem] * len(args),
        out_specs=[vmem] * len(outs),
        scratch_shapes=[pltpu.VMEM(shape, f32) for shape in scratch],
        compiler_params=pltpu.CompilerParams(vmem_limit_bytes=40 * 1024 * 1024),
    )(place, *args)


def pack_strips(arrays):
    rows, height, own = arrays[0].shape
    end = own // LANES - 1
    block = (rows, height, LANES)
    first = pl.BlockSpec(block, lambda i: (0, 0, 0))
    last = pl.BlockSpec(block, lambda i: (0, 0, end))
    out = pl.BlockSpec(block, lambda i: (0, 0, 0))
    return pl.pallas_call(
        pack_kernel,
        grid=(1,),
        out_shape=[jax.ShapeDtypeStruct(block, f32)] * 2,
        in_specs=[first] * 5 + [last] * 5,
        out_specs=[out] * 2,
    )(*arrays, *arrays)


def on_device(
    solid_occupancy,
    newer_occupancy_shift,
    older_occupancy_shift,
    below_limit_spacing,
    above_limit_spacing,
    thermal_state,
    loss_state_derivative,
    prior_dual_state,
    cell_material,
):
    rows, height, own = solid_occupancy.shape
    deep, long = lax.axis_size("thick"), lax.axis_size("facade")
    totals = (rows * deep, own * long)
    place = jnp.stack(
        [lax.axis_index("thick") * rows, lax.axis_index("facade") * own]
    ).astype(jnp.int32)
    width = own + LANES
    whole = (rows, height, own)

    def turn(axis, size, step):
        pairs = [(i, (i + step) % size) for i in range(size)]
        return lambda value: lax.ppermute(value, axis, pairs)

    to_right, to_left = turn("facade", long, 1), turn("facade", long, -1)
    to_deeper, to_nearer = turn("thick", deep, 1), turn("thick", deep, -1)

    first_strips, last_strips = pack_strips(
        (solid_occupancy, cell_material, loss_state_derivative, prior_dual_state, thermal_state)
    )
    right, left = to_left(first_strips), to_right(last_strips)

    def side_by_side(strips, start):
        return jnp.concatenate([strips[start + r] for r in range(4)], axis=1)[None]

    def depth_message(last):
        def end(value, count):
            return value[rows - count:] if last else value[:count]

        start = rows - 4 if last else 0
        return jnp.concatenate(
            [
                end(solid_occupancy, 4), end(prior_dual_state, 4),
                end(loss_state_derivative, 3), end(thermal_state, 1),
                side_by_side(left, start), side_by_side(right, start),
            ]
        )

    from_above, from_below = to_deeper(depth_message(True)), to_nearer(depth_message(False))

    (below, above, up, low, least, most, upper, lower, bend, tallies) = call(
        lines_kernel,
        [whole] * 9 + [(2, height, LANES)],
        (
            solid_occupancy, newer_occupancy_shift, older_occupancy_shift,
            below_limit_spacing, above_limit_spacing, cell_material,
        ),
    )

    four = (4, height, width)
    rho, cond_first, cond_last = placed_call(
        rho_kernel, place,
        [(rows, height, width), four, four],
        (
            solid_occupancy, cell_material, from_above, from_below, left, right,
        ),
        [(BOTH_SIDES, height, width), (BOTH_SIDES - 4, height, width), (rows, height, width)],
        totals,
    )
    cond_above, cond_below = to_deeper(cond_last), to_nearer(cond_first)
    tall = (BOTH_SIDES, height, width)
    dual_state, weighted_first, weighted_last = placed_call(
        sweep_kernel, place,
        [whole, four, four],
        (
            cond_above, cond_first, cond_last, cond_below, rho, cell_material,
            prior_dual_state, loss_state_derivative, thermal_state, from_above, from_below,
            left, right, tallies,
        ),
        [tall, tall, tall, (10, height, width)] + [tall] * 13,
        totals,
    )
    weighted_above, weighted_below = to_deeper(weighted_last), to_nearer(weighted_first)
    count = deep * long
    note = (count, LANES)
    grad, message = placed_call(
        grad_kernel, place,
        [whole, note],
        (weighted_above, weighted_first, weighted_last, weighted_below, cell_material),
        [tall, (BOTH_SIDES - 4, height, width), (rows, height, width)],
        totals,
    )

    def everyone(rows_out):
        return lax.all_to_all(rows_out, AXES, 0, 0, tiled=True)

    fixed = (up, low, least, most, upper, lower, bend, tallies)
    message, rate_above, rate_below = call(
        first_kernel, [note, whole, whole], (everyone(message), grad) + fixed
    )
    y = jnp.ones((8, LANES), f32)
    for _ in range(NEWTON - 1):
        message, y = call(
            step_kernel, [note, (8, LANES)],
            (everyone(message), y, rate_above, rate_below) + fixed,
        )
    (density_new,) = call(
        last_kernel, [whole],
        (
            everyone(message), y, rate_above, rate_below, up, low, least, most, below,
            solid_occupancy, cell_material,
        ),
    )
    return (density_new, below, above, dual_state)


def solution(mesh):
    spec = P("thick", None, "facade")
    return jax.shard_map(
        on_device,
        mesh=mesh,
        in_specs=(spec,) * 9,
        out_specs=(spec,) * 4,
        check_vma=False,
    )
```

```python
import functools
import jax
import jax.numpy as jnp
from jax import lax
from jax.experimental import pallas as pl
from jax.experimental.pallas import tpu as pltpu
from jax.sharding import PartitionSpec as P

RADIUS = 4
SWEEPS = 3
NEWTON = 8

k_void = 0.03
k_frame = 160.0
k_glass = 1.0
k_anchor = 50.0
loss_rate = 0.05
spectrum_low = 0.05
spectrum_high = 2.0
solid_allowance = 0.35
curve_floor = 0.05
move_limit = 0.2
gamma_slope = 200.0

LANES = 128
STRIP = 16
above_weight = 1.001 + 1e-05
below_weight = 0.001 + 1e-05

f32 = jnp.float32
AXES = ("thick", "facade")
BOTH_SIDES = 16


def call(kernel, outs, args, scratch=()):
    vmem = pl.BlockSpec(memory_space=pltpu.VMEM)
    return pl.pallas_call(
        kernel,
        out_shape=[jax.ShapeDtypeStruct(shape, f32) for shape in outs],
        in_specs=[vmem] * len(args),
        out_specs=[vmem] * len(outs),
        scratch_shapes=[pltpu.VMEM(shape, f32) for shape in scratch],
        compiler_params=pltpu.CompilerParams(vmem_limit_bytes=40 * 1024 * 1024),
    )(*args)


def lane_iota(shape):
    return lax.broadcasted_iota(jnp.int32, shape, len(shape) - 1)


def sub_iota(shape):
    return lax.broadcasted_iota(jnp.int32, shape, len(shape) - 2)


def ahead(value, step, axis):
    return pltpu.roll(value, (value.shape[axis] - step) % value.shape[axis], axis)


def behind(value, step, axis):
    return pltpu.roll(value, step, axis)


def pack_kernel(*refs):
    firsts, lasts, to_left, to_right = refs[0:5], refs[5:10], refs[10], refs[11]
    rows, height, _ = to_left.shape
    group = lane_iota((height, LANES)) // STRIP
    for row in range(rows):
        for source, target, place in ((firsts, to_left, 0), (lasts, to_right, LANES - STRIP)):
            packed = jnp.zeros((height, LANES), f32)
            for index, ref in enumerate(source):
                value = ref[row]
                if value.dtype != f32:
                    value = value.astype(f32) + 1.0
                shift = (STRIP * index - place) % LANES
                if shift:
                    value = pltpu.roll(value, shift, 1)
                packed = jnp.where(group == index, value, packed)
            target[row] = packed


def halo_lanes(left, right, index):
    lane = lane_iota(left.shape)
    shift = (LANES - STRIP * index) % LANES
    after = pltpu.roll(right, shift, 1) if shift else right
    shift = (LANES - STRIP - STRIP * index) % LANES
    before = pltpu.roll(left, shift, 1) if shift else left
    return jnp.where(lane < STRIP, after, jnp.where(lane >= LANES - STRIP, before, 0.0))


def axis_weight(position, total):
    acc = jnp.zeros(position.shape, f32)
    for offset in range(-RADIUS, RADIUS + 1):
        weight = float(RADIUS + 1 - abs(offset))
        inside = (position + offset >= 0) & (position + offset < total)
        acc = acc + jnp.where(inside, weight, 0.0)
    return jnp.maximum(acc, 1.0)


def inverse_plane(height, own, cols_total, col_start):
    width = own + LANES
    lane = lane_iota((1, width))
    place = jnp.where(lane < own + LANES // 2, lane, lane - width) + col_start
    middle = axis_weight(sub_iota((height, 1)), height)
    return 1.0 / (middle * axis_weight(place, cols_total))


def row_weight(row, rows_total, row_start):
    return 1.0 / axis_weight(jnp.full((1, 1), row + row_start, jnp.int32), rows_total)


def filter_height(value):
    height = value.shape[0]
    level = sub_iota((height, 1))
    total = float(RADIUS + 1) * value
    for offset in range(1, RADIUS + 1):
        weight = float(RADIUS + 1 - offset)
        up = jnp.where(level < height - offset, weight, 0.0)
        down = jnp.where(level >= offset, weight, 0.0)
        total = total + up * ahead(value, offset, 0) + down * behind(value, offset, 0)
    return total


def filter_lanes(value):
    def box(v):
        pair = v + ahead(v, 1, 1)
        return pair + ahead(pair, 2, 1) + behind(v, 1, 1)

    def box_back(v):
        pair = v + behind(v, 1, 1)
        return pair + behind(pair, 2, 1) + ahead(v, 1, 1)

    return box_back(box(value))


def depth_filter(source, middle, target):
    count = source.shape[0]
    for r in range(count - 4):
        middle[r] = (source[r] + source[r + 1]) + (source[r + 2] + source[r + 3]) + source[r + 4]
    for r in range(count - 8):
        target[r] = (middle[r] + middle[r + 1]) + (middle[r + 2] + middle[r + 3]) + middle[r + 4]


def present(place, rows, own, rows_total, cols_total):
    row_start, col_start = place

    def flag(condition):
        return jnp.where(condition, 1.0, 0.0).astype(f32)

    return (
        flag(row_start > 0), flag(row_start + rows < rows_total),
        flag(col_start > 0), flag(col_start + own < cols_total),
    )


def corner(message, row):
    return message[row], message[4 + row]


def rho_kernel(
    rows_total, cols_total, place,
    density, material, from_above, from_below, corner_above, corner_below, left, right,
    rho_out, cond_first, cond_last,
    ext, middle, summed,
):
    rows, height, own = density.shape
    has_above, has_below, has_left, has_right = present(place, rows, own, rows_total, cols_total)

    def halo(strips, index):
        return halo_lanes(strips[0] * has_left, strips[1] * has_right, index)

    for r in range(4):
        ext[r, :, :own] = from_above[r] * has_above
        ext[r, :, own:] = halo(corner(corner_above, r), 0) * has_above
        ext[rows + 4 + r, :, :own] = from_below[r] * has_below
        ext[rows + 4 + r, :, own:] = halo(corner(corner_below, r), 0) * has_below
    for r in range(rows):
        ext[4 + r, :, :own] = density[r]
        ext[4 + r, :, own:] = halo((left[r], right[r]), 0)
    depth_filter(ext, middle, summed)
    plane = inverse_plane(height, own, cols_total, place[1])
    for r in range(rows):
        rho = filter_lanes(filter_height(summed[r])) * (
            plane * row_weight(r, rows_total, place[0])
        )
        code = jnp.concatenate(
            [material[r].astype(f32) + 1.0, halo((left[r], right[r]), 1)], axis=1
        )
        frame = k_void + (k_frame - k_void) * rho * rho * rho
        cond = jnp.where(code == 2.0, frame, jnp.where(code == 1.0, k_glass, k_anchor))
        cond = jnp.where(code == 0.0, 0.0, cond)
        rho_out[r] = rho
        if r < 4:
            cond_first[r] = cond
        else:
            cond_last[r - 4] = cond


centre_value = 0.5 * (spectrum_high + spectrum_low)
half_width = 0.5 * (spectrum_high - spectrum_low)
ratio_value = centre_value / half_width
INNER = range(5, 11)


class Rows:
    def __init__(self, ready, first, stop, rest):
        self.ready, self.first, self.stop, self.rest = ready, first, stop, rest

    def __getitem__(self, row):
        if self.first <= row < self.stop:
            return self.ready[row - self.first]
        return self.rest[row]


def face(one, other, store=None):
    inv = 1.0 / jnp.maximum(one + other, 1e-3)
    part = one * inv
    if store is not None:
        here, there, row = store
        rest = other * inv
        there[row] = part * part
        here[row] = rest * rest
    return 2.0 * part * other


def first_residual(value, before, after, load, deep_before, deep, tall, wide):
    inverse = 1.0 / (
        loss_rate + (deep + deep_before) + (tall + behind(tall, 1, 0)) + (wide + behind(wide, 1, 1))
    )
    left_over = load - operate(value, deep_before * (before - value), deep * (value - after), tall, wide)
    direction = left_over * inverse * (1.0 / centre_value)
    return inverse, left_over, direction


def operate(value, flux_before, flux, tall, wide):
    high = tall * (value - ahead(value, 1, 0))
    along = wide * (value - ahead(value, 1, 1))
    return (
        loss_rate * value + (flux - flux_before) + (high - behind(high, 1, 0))
        + (along - behind(along, 1, 1))
    )


def prepare_kernel(
    cond_first, cond_last, prior, source, temp,
    from_above, from_below, corner_above, corner_below, left, right,
    field, load, heat, depth_face, height_face, lane_face,
    depth_here, depth_there, height_here, height_there, lane_here, lane_there,
    inverse, residual, direction, dual,
):
    rows, height, own = prior.shape
    last_level = sub_iota((height, 1)) == height - 1

    def place_row(target, row, main, strips, index):
        target[row, :, :own] = main
        target[row, :, own:] = halo_lanes(strips[0], strips[1], index)

    for r in range(4):
        place_row(field, r, from_above[4 + r], corner(corner_above, r), 3)
        place_row(field, 12 + r, from_below[4 + r], corner(corner_below, r), 3)
    for r in range(3):
        place_row(load, 1 + r, from_above[8 + r], corner(corner_above, 1 + r), 2)
        place_row(load, 12 + r, from_below[8 + r], corner(corner_below, r), 2)
    load[0] = jnp.zeros(load.shape[1:], f32)
    load[15] = jnp.zeros(load.shape[1:], f32)
    place_row(heat, 0, from_above[11], corner(corner_above, 3), 4)
    place_row(heat, 9, from_below[11], corner(corner_below, 0), 4)
    for r in range(rows):
        strips = (left[r], right[r])
        place_row(field, 4 + r, prior[r], strips, 3)
        place_row(load, 4 + r, source[r], strips, 2)
        place_row(heat, 1 + r, temp[r], strips, 4)

    deep_before = None
    following = cond_first[0]
    for r in range(4, 12):
        i = r - 4
        here = following
        tall = jnp.where(
            last_level, 0.0, face(here, ahead(here, 1, 0), (height_here, height_there, i))
        )
        wide = face(here, ahead(here, 1, 1), (lane_here, lane_there, i))
        height_face[i] = tall
        lane_face[i] = wide
        if r < 11:
            following = cond_first[i + 1] if i < 3 else cond_last[i - 3]
            deep = face(here, following, (depth_here, depth_there, i))
            depth_face[i] = deep
        if r in INNER:
            value = field[r]
            one, two, three = first_residual(
                value, field[r - 1], field[r + 1], load[r], deep_before, deep, tall, wide
            )
            k = r - INNER.start
            inverse[k], residual[k], direction[k] = one, two, three
            dual[k] = value + three
        deep_before = deep


def sweep_kernel(
    rows_total, cols_total, place,
    cond_above, cond_first, cond_last, cond_below, rho, material,
    field, load, heat, own_depth_face, own_height_face, own_lane_face,
    own_depth_here, own_depth_there, height_here, height_there, lane_here, lane_there,
    own_inverse, own_residual, own_direction, own_dual, left, right, tallies,
    dual_out, weighted_first, weighted_last,
    depth_face, height_face, lane_face, inverse, residual, first_direction, next_direction, dual,
    edge_here, edge_there,
):
    rows, height, own = rho.shape[0], rho.shape[1], dual_out.shape[2]
    has_above, has_below, has_left, has_right = present(place, rows, own, rows_total, cols_total)
    last_level = sub_iota((height, 1)) == height - 1

    def cond(r):
        if r < 4:
            return cond_above[r] * has_above
        if r >= 12:
            return cond_below[r - 12] * has_below
        return cond_first[r - 4] if r < 8 else cond_last[r - 8]

    depth_faces = Rows(own_depth_face, 4, 11, depth_face)
    height_faces = Rows(own_height_face, 4, 12, height_face)
    lane_faces = Rows(own_lane_face, 4, 12, lane_face)
    inverses = Rows(own_inverse, INNER.start, INNER.stop, inverse)
    residuals = Rows(own_residual, INNER.start, INNER.stop, residual)
    directions = Rows(own_direction, INNER.start, INNER.stop, first_direction)
    duals = Rows(own_dual, INNER.start, INNER.stop, dual)

    following = cond(0)
    for r in range(15):
        if 4 <= r < 11:
            following = None
            continue
        here = cond(r) if following is None else following
        following = cond(r + 1)
        store = (edge_here, edge_there, 0 if r == 3 else 1) if r in (3, 11) else None
        depth_face[r] = face(here, following, store)
        if r in (1, 2, 3, 12, 13, 14):
            height_face[r] = jnp.where(last_level, 0.0, face(here, ahead(here, 1, 0)))
            lane_face[r] = face(here, ahead(here, 1, 1))
    for r in range(1, 15):
        if r in INNER:
            continue
        value = field[r]
        one, two, three = first_residual(
            value, field[r - 1], field[r + 1], load[r],
            depth_faces[r - 1], depth_faces[r], height_faces[r], lane_faces[r],
        )
        inverse[r], residual[r], first_direction[r] = one, two, three
        if 3 <= r < 13:
            dual[r] = value + three

    factor = 1.0 / ratio_value
    now = directions
    for sweep in range(SWEEPS - 1):
        factor_next = 1.0 / (2.0 * ratio_value - factor)
        keep, add = factor_next * factor, 2.0 * factor_next / half_width
        start, stop = 2 + sweep, 14 - sweep
        following = now[start]
        flux_before = depth_faces[start - 1] * (now[start - 1] - following)
        for r in range(start, stop):
            value, following = following, now[r + 1]
            flux = depth_faces[r] * (value - following)
            left_over = residuals[r] - operate(
                value, flux_before, flux, height_faces[r], lane_faces[r]
            )
            direction = keep * value + add * (left_over * inverses[r])
            if sweep < SWEEPS - 2:
                residual[r] = left_over
                next_direction[r] = direction
            if 3 <= r < 13:
                dual[r] = duals[r] + direction
            flux_before = flux
        factor = factor_next
        now, residuals, duals = next_direction, residual, dual

    depth_here = Rows(own_depth_here, 4, 11, {11: edge_here[1]})
    depth_there = Rows(own_depth_there, 4, 11, {3: edge_there[0], 11: edge_there[1]})
    plane = inverse_plane(height, own, cols_total, place[1])
    for r in range(rows):
        dual_out[r] = dual[4 + r, :, :own]
    a, t = dual[3], heat[0]
    a_next, t_next = dual[4], heat[1]
    deep_before = (a - a_next) * (t - t_next) * depth_there[3]
    for r in range(4, 4 + rows):
        row = r - 4
        a, t = a_next, t_next
        a_next, t_next = dual[r + 1], heat[r - 2]
        deep = (a - a_next) * (t - t_next)
        tall = (a - ahead(a, 1, 0)) * (t - ahead(t, 1, 0))
        tall = jnp.where(last_level, 0.0, tall)
        wide = (a - ahead(a, 1, 1)) * (t - ahead(t, 1, 1))
        total = (
            (deep * depth_here[r] + deep_before)
            + (tall * height_here[row] + behind(tall * height_there[row], 1, 0))
            + (wide * lane_here[row] + behind(wide * lane_there[row], 1, 1))
        )
        deep_before = deep * depth_there[r]
        strips = halo_lanes(left[row] * has_left, right[row] * has_right, 1)
        code = jnp.concatenate([material[row].astype(f32) + 1.0, strips], axis=1)
        thick_rho = rho[row]
        value = total * (thick_rho * thick_rho) * (
            plane * (row_weight(row, rows_total, place[0]) * (-6.0 * (k_frame - k_void)))
        )
        value = jnp.where(code == 2.0, value, 0.0)
        if row < 4:
            weighted_first[row] = value
        else:
            weighted_last[row - 4] = value


def grad_kernel(
    rows_total, cols_total, place,
    from_above, first, last, from_below, material, grad_out, message, ext, middle, summed,
):
    rows, height, own = grad_out.shape
    has_above, has_below, _, _ = present(place, rows, own, rows_total, cols_total)
    for r in range(4):
        ext[r] = from_above[r] * has_above
        ext[4 + r] = first[r]
        ext[8 + r] = last[r]
        ext[12 + r] = from_below[r] * has_below
    depth_filter(ext, middle, summed)
    largest = jnp.zeros((height, LANES), f32)
    for r in range(rows):
        grad = filter_lanes(filter_height(summed[r]))[:, :own]
        grad_out[r] = grad
        size = jnp.where(material[r] == 1, jnp.abs(grad), 0.0)
        for block in range(own // LANES):
            largest = jnp.maximum(largest, size[:, block * LANES:(block + 1) * LANES])
    message[...] = jnp.broadcast_to(jnp.max(largest, axis=0, keepdims=True), message.shape)


def lines_kernel(
    solid, newer, older, below_spacing, above_spacing, material,
    below_out, above_out, up_out, low_out, least_out, most_out, upper_out, lower_out, bend_out,
    tallies,
):
    rows, height, own = solid.shape
    base = jnp.zeros((height, LANES), f32)
    count = jnp.zeros((height, LANES), f32)
    for r in range(rows):
        x = solid[r]
        design = material[r] == 1
        gamma = 0.95 + 0.25 * jnp.tanh(gamma_slope * newer[r] * older[r])
        below = x - gamma * below_spacing[r]
        above = x + gamma * above_spacing[r]
        below_out[r] = below
        above_out[r] = above
        up = above - x
        low = x - below
        floor = jnp.maximum(jnp.maximum(0.0, below + 0.1 * low), x - move_limit)
        ceiling = jnp.minimum(jnp.minimum(1.0, above - 0.1 * up), x + move_limit)
        up_out[r] = up
        low_out[r] = low
        least_out[r] = floor - below
        most_out[r] = ceiling - below
        upper_out[r] = jnp.where(design, above_weight * up * up, 0.0)
        lower_out[r] = jnp.where(design, below_weight * low * low, 0.0)
        bend_out[r] = jnp.where(design, up * low / (2.0 * (up + low)), 0.0)
        term = jnp.where(
            design, x - solid_allowance - above_weight * up - below_weight * low, 0.0
        )
        one = jnp.where(design, curve_floor, 0.0)
        for block in range(own // LANES):
            base = base + term[:, block * LANES:(block + 1) * LANES]
            count = count + one[:, block * LANES:(block + 1) * LANES]
    tallies[0] = base
    tallies[1] = count


def reached(rate_above, rate_below, y, up, low, least, most):
    root_above = rate_above + y * above_weight
    root_below = rate_below + y * below_weight
    inv_above, inv_below = lax.rsqrt(root_above), lax.rsqrt(root_below)
    root_above, root_below = root_above * inv_above, root_below * inv_below
    width = up + low
    pull = low * root_below
    trial = width * pull / (up * root_above + pull)
    return trial, jnp.clip(trial, least, most), width, root_above, root_below, inv_above, inv_below


def sums_to_message(slope, curve, message):
    slope = jnp.sum(slope, axis=0, keepdims=True)
    curve = jnp.sum(curve, axis=0, keepdims=True)
    slope = slope + pltpu.roll(slope, LANES // 2, 1)
    curve = curve + pltpu.roll(curve, LANES // 2, 1)
    lane = lane_iota((1, LANES))
    message[...] = jnp.broadcast_to(jnp.where(lane < LANES // 2, slope, curve), message.shape)


def evaluate(y, rate_above, rate_below, up, low, least, most, upper, lower, bend, tallies, message):
    rows, height, own = up.shape
    slope_sum, curve_sum = tallies[0], tallies[1]
    for r in range(rows):
        trial, chosen, width, root_above, root_below, inv_above, inv_below = reached(
            rate_above(r), rate_below(r), y, up[r], low[r], least[r], most[r]
        )
        rest = width - chosen
        slope = (upper[r] * chosen + lower[r] * rest) / (rest * chosen)
        split = above_weight * (inv_above * inv_above) - below_weight * (inv_below * inv_below)
        curve = bend[r] * (root_above * root_below) * (split * split)
        free = (trial > least[r]) & (trial < most[r])
        curve = jnp.where(free, curve, 0.0)
        for block in range(own // LANES):
            slope_sum = slope_sum + slope[:, block * LANES:(block + 1) * LANES]
            curve_sum = curve_sum + curve[:, block * LANES:(block + 1) * LANES]
    sums_to_message(slope_sum, curve_sum, message)


def first_kernel(
    arrived, grad, up, low, least, most, upper, lower, bend, tallies,
    message, rate_above_out, rate_below_out,
):
    scale = jnp.max(jnp.max(arrived[...], axis=0, keepdims=True), axis=1, keepdims=True)
    inverse = 1.0 / (scale + 1e-06)

    def above(r):
        element = grad[r] * inverse
        value = jnp.maximum(1.001 * element, -0.001 * element) + 1e-05
        rate_above_out[r] = value
        return value

    def below(r):
        element = grad[r] * inverse
        value = jnp.maximum(0.001 * element, -1.001 * element) + 1e-05
        rate_below_out[r] = value
        return value

    evaluate(
        jnp.ones((1, 1), f32), above, below, up, low, least, most, upper, lower, bend, tallies, message
    )


def advance(arrived, y):
    total = jnp.sum(arrived[...], axis=0, keepdims=True)
    lane = lane_iota(total.shape)
    slope = jnp.sum(jnp.where(lane < LANES // 2, total, 0.0), axis=1, keepdims=True)
    curve = jnp.sum(jnp.where(lane < LANES // 2, 0.0, total), axis=1, keepdims=True)
    return jnp.maximum(0.0, y + slope / curve)


def step_kernel(
    arrived, y_ref, rate_above, rate_below, up, low, least, most, upper, lower, bend, tallies,
    message, y_out,
):
    y = advance(arrived, y_ref[0:1, 0:1])
    y_out[...] = jnp.broadcast_to(y, y_out.shape)
    evaluate(
        y, lambda r: rate_above[r], lambda r: rate_below[r],
        up, low, least, most, upper, lower, bend, tallies, message,
    )


def last_kernel(
    arrived, y_ref, rate_above, rate_below, up, low, least, most, below, solid, material, out
):
    y = advance(arrived, y_ref[0:1, 0:1])
    for r in range(out.shape[0]):
        chosen = reached(rate_above[r], rate_below[r], y, up[r], low[r], least[r], most[r])[1]
        out[r] = jnp.where(material[r] == 1, below[r] + chosen, solid[r])


def with_place(kernel, rows_total, cols_total):
    def body(place_ref, *refs):
        kernel(rows_total, cols_total, (place_ref[0], place_ref[1]), *refs)

    return body


def placed_call(kernel, place, outs, args, scratch, totals):
    vmem = pl.BlockSpec(memory_space=pltpu.VMEM)
    return pl.pallas_call(
        with_place(kernel, *totals),
        out_shape=[jax.ShapeDtypeStruct(shape, f32) for shape in outs],
        in_specs=[pl.BlockSpec(memory_space=pltpu.SMEM)] + [vmem] * len(args),
        out_specs=[vmem] * len(outs),
        scratch_shapes=[pltpu.VMEM(shape, f32) for shape in scratch],
        compiler_params=pltpu.CompilerParams(vmem_limit_bytes=40 * 1024 * 1024),
    )(place, *args)


def pack_strips(arrays):
    rows, height, own = arrays[0].shape
    end = own // LANES - 1
    block = (rows, height, LANES)
    first = pl.BlockSpec(block, lambda i: (0, 0, 0))
    last = pl.BlockSpec(block, lambda i: (0, 0, end))
    out = pl.BlockSpec(block, lambda i: (0, 0, 0))
    return pl.pallas_call(
        pack_kernel,
        grid=(1,),
        out_shape=[jax.ShapeDtypeStruct(block, f32)] * 2,
        in_specs=[first] * 5 + [last] * 5,
        out_specs=[out] * 2,
    )(*arrays, *arrays)


def on_device(
    solid_occupancy,
    newer_occupancy_shift,
    older_occupancy_shift,
    below_limit_spacing,
    above_limit_spacing,
    thermal_state,
    loss_state_derivative,
    prior_dual_state,
    cell_material,
):
    rows, height, own = solid_occupancy.shape
    deep, long = lax.axis_size("thick"), lax.axis_size("facade")
    totals = (rows * deep, own * long)
    place = jnp.stack(
        [lax.axis_index("thick") * rows, lax.axis_index("facade") * own]
    ).astype(jnp.int32)
    width = own + LANES
    whole = (rows, height, own)

    def turn(axis, size, step):
        pairs = [(i, (i + step) % size) for i in range(size)]
        return lambda value: lax.ppermute(value, axis, pairs)

    to_right, to_left = turn("facade", long, 1), turn("facade", long, -1)
    to_deeper, to_nearer = turn("thick", deep, 1), turn("thick", deep, -1)

    first_strips, last_strips = pack_strips(
        (solid_occupancy, cell_material, loss_state_derivative, prior_dual_state, thermal_state)
    )
    right, left = to_left(first_strips), to_right(last_strips)

    from_above = to_deeper(
        jnp.concatenate(
            [
                solid_occupancy[rows - 4:], prior_dual_state[rows - 4:],
                loss_state_derivative[rows - 3:], thermal_state[rows - 1:],
            ]
        )
    )
    from_below = to_nearer(
        jnp.concatenate(
            [
                solid_occupancy[:4], prior_dual_state[:4],
                loss_state_derivative[:3], thermal_state[:1],
            ]
        )
    )
    corner_above = to_deeper(jnp.concatenate([left[rows - 4:], right[rows - 4:]]))
    corner_below = to_nearer(jnp.concatenate([left[:4], right[:4]]))

    (below, above, up, low, least, most, upper, lower, bend, tallies) = call(
        lines_kernel,
        [whole] * 9 + [(2, height, LANES)],
        (
            solid_occupancy, newer_occupancy_shift, older_occupancy_shift,
            below_limit_spacing, above_limit_spacing, cell_material,
        ),
    )

    four = (4, height, width)
    rho, cond_first, cond_last = placed_call(
        rho_kernel, place,
        [(rows, height, width), four, four],
        (
            solid_occupancy, cell_material, from_above, from_below, corner_above, corner_below,
            left, right,
        ),
        [(BOTH_SIDES, height, width), (BOTH_SIDES - 4, height, width), (rows, height, width)],
        totals,
    )
    cond_above, cond_below = to_deeper(cond_last), to_nearer(cond_first)
    tall, own_wide, inner = (
        (BOTH_SIDES, height, width), (rows, height, width), (len(INNER), height, width),
    )
    prepared = call(
        prepare_kernel,
        [tall, tall, (rows + 2, height, width)] + [own_wide] * 9 + [inner] * 4,
        (
            cond_first, cond_last, prior_dual_state, loss_state_derivative, thermal_state,
            from_above, from_below, corner_above, corner_below, left, right,
        ),
    )
    dual_state, weighted_first, weighted_last = placed_call(
        sweep_kernel, place,
        [whole, four, four],
        (
            cond_above, cond_first, cond_last, cond_below, rho, cell_material, *prepared,
            left, right, tallies,
        ),
        [tall] * 8 + [(2, height, width)] * 2,
        totals,
    )
    weighted_above, weighted_below = to_deeper(weighted_last), to_nearer(weighted_first)
    count = deep * long
    note = (count, LANES)
    grad, message = placed_call(
        grad_kernel, place,
        [whole, note],
        (weighted_above, weighted_first, weighted_last, weighted_below, cell_material),
        [tall, (BOTH_SIDES - 4, height, width), (rows, height, width)],
        totals,
    )

    def everyone(rows_out):
        return lax.all_to_all(rows_out, AXES, 0, 0, tiled=True)

    fixed = (up, low, least, most, upper, lower, bend, tallies)
    message, rate_above, rate_below = call(
        first_kernel, [note, whole, whole], (everyone(message), grad) + fixed
    )
    y = jnp.ones((8, LANES), f32)
    for _ in range(NEWTON - 1):
        message, y = call(
            step_kernel, [note, (8, LANES)],
            (everyone(message), y, rate_above, rate_below) + fixed,
        )
    (density_new,) = call(
        last_kernel, [whole],
        (
            everyone(message), y, rate_above, rate_below, up, low, least, most, below,
            solid_occupancy, cell_material,
        ),
    )
    return (density_new, below, above, dual_state)


def solution(mesh):
    spec = P("thick", None, "facade")
    return jax.shard_map(
        on_device,
        mesh=mesh,
        in_specs=(spec,) * 9,
        out_specs=(spec,) * 4,
        check_vma=False,
    )
```

```python
import functools
import jax
import jax.numpy as jnp
from jax import lax
from jax.experimental import pallas as pl
from jax.experimental.pallas import tpu as pltpu
from jax.sharding import PartitionSpec as P

RADIUS = 4
SWEEPS = 3
NEWTON = 8

k_void = 0.03
k_frame = 160.0
k_glass = 1.0
k_anchor = 50.0
loss_rate = 0.05
spectrum_low = 0.05
spectrum_high = 2.0
solid_allowance = 0.35
curve_floor = 0.05
move_limit = 0.2
gamma_slope = 200.0

LANES = 128
STRIP = 16
above_weight = 1.001 + 1e-05
below_weight = 0.001 + 1e-05

f32 = jnp.float32
AXES = ("thick", "facade")
BOTH_SIDES = 16


def call(kernel, outs, args, scratch=()):
    vmem = pl.BlockSpec(memory_space=pltpu.VMEM)
    return pl.pallas_call(
        kernel,
        out_shape=[jax.ShapeDtypeStruct(shape, f32) for shape in outs],
        in_specs=[vmem] * len(args),
        out_specs=[vmem] * len(outs),
        scratch_shapes=[pltpu.VMEM(shape, f32) for shape in scratch],
        compiler_params=pltpu.CompilerParams(vmem_limit_bytes=40 * 1024 * 1024),
    )(*args)


def lane_iota(shape):
    return lax.broadcasted_iota(jnp.int32, shape, len(shape) - 1)


def sub_iota(shape):
    return lax.broadcasted_iota(jnp.int32, shape, len(shape) - 2)


def ahead(value, step, axis):
    return pltpu.roll(value, (value.shape[axis] - step) % value.shape[axis], axis)


def behind(value, step, axis):
    return pltpu.roll(value, step, axis)


def launch_kernel(*refs):
    firsts, lasts, nears, fars = refs[0:5], refs[5:10], refs[10:14], refs[14:18]
    to_left, to_right, rows_up, rows_down = refs[18:]
    rows, height, _ = to_left.shape
    group = lane_iota((height, LANES)) // STRIP
    for row in range(rows):
        for source, target, place in ((firsts, to_left, 0), (lasts, to_right, LANES - STRIP)):
            packed = jnp.zeros((height, LANES), f32)
            for index, ref in enumerate(source):
                value = ref[row]
                if value.dtype != f32:
                    value = value.astype(f32) + 1.0
                shift = (STRIP * index - place) % LANES
                if shift:
                    value = pltpu.roll(value, shift, 1)
                packed = jnp.where(group == index, value, packed)
            target[row] = packed
    start = 0
    for near, far, count in zip(nears, fars, (4, 4, 3, 1)):
        for r in range(count):
            rows_down[start + r] = near[r]
            rows_up[start + r] = far[far.shape[0] - count + r]
        start += count


def halo_lanes(left, right, index):
    lane = lane_iota(left.shape)
    shift = (LANES - STRIP * index) % LANES
    after = pltpu.roll(right, shift, 1) if shift else right
    shift = (LANES - STRIP - STRIP * index) % LANES
    before = pltpu.roll(left, shift, 1) if shift else left
    return jnp.where(lane < STRIP, after, jnp.where(lane >= LANES - STRIP, before, 0.0))


def axis_weight(position, total):
    acc = jnp.zeros(position.shape, f32)
    for offset in range(-RADIUS, RADIUS + 1):
        weight = float(RADIUS + 1 - abs(offset))
        inside = (position + offset >= 0) & (position + offset < total)
        acc = acc + jnp.where(inside, weight, 0.0)
    return jnp.maximum(acc, 1.0)


def inverse_plane(height, own, cols_total, col_start):
    width = own + LANES
    lane = lane_iota((1, width))
    place = jnp.where(lane < own + LANES // 2, lane, lane - width) + col_start
    middle = axis_weight(sub_iota((height, 1)), height)
    return 1.0 / (middle * axis_weight(place, cols_total))


def row_weight(row, rows_total, row_start):
    return 1.0 / axis_weight(jnp.full((1, 1), row + row_start, jnp.int32), rows_total)


def filter_height(value):
    height = value.shape[0]
    level = sub_iota((height, 1))
    total = float(RADIUS + 1) * value
    for offset in range(1, RADIUS + 1):
        weight = float(RADIUS + 1 - offset)
        up = jnp.where(level < height - offset, weight, 0.0)
        down = jnp.where(level >= offset, weight, 0.0)
        total = total + up * ahead(value, offset, 0) + down * behind(value, offset, 0)
    return total


def filter_lanes(value):
    def box(v):
        pair = v + ahead(v, 1, 1)
        return pair + ahead(pair, 2, 1) + behind(v, 1, 1)

    def box_back(v):
        pair = v + behind(v, 1, 1)
        return pair + behind(pair, 2, 1) + ahead(v, 1, 1)

    return box_back(box(value))


def depth_filter(source, middle, target):
    count = source.shape[0]
    for r in range(count - 4):
        middle[r] = (source[r] + source[r + 1]) + (source[r + 2] + source[r + 3]) + source[r + 4]
    for r in range(count - 8):
        target[r] = (middle[r] + middle[r + 1]) + (middle[r + 2] + middle[r + 3]) + middle[r + 4]


def present(place, rows, own, rows_total, cols_total):
    row_start, col_start = place

    def flag(condition):
        return jnp.where(condition, 1.0, 0.0).astype(f32)

    return (
        flag(row_start > 0), flag(row_start + rows < rows_total),
        flag(col_start > 0), flag(col_start + own < cols_total),
    )


def corner(message, row):
    return message[row], message[4 + row]


def rho_kernel(
    rows_total, cols_total, place,
    density, material, from_above, from_below, corner_above, corner_below, left, right,
    rho_out, cond_first, cond_last,
    ext, middle, summed,
):
    rows, height, own = density.shape
    has_above, has_below, has_left, has_right = present(place, rows, own, rows_total, cols_total)

    def halo(strips, index):
        return halo_lanes(strips[0] * has_left, strips[1] * has_right, index)

    for r in range(4):
        ext[r, :, :own] = from_above[r] * has_above
        ext[r, :, own:] = halo(corner(corner_above, r), 0) * has_above
        ext[rows + 4 + r, :, :own] = from_below[r] * has_below
        ext[rows + 4 + r, :, own:] = halo(corner(corner_below, r), 0) * has_below
    for r in range(rows):
        ext[4 + r, :, :own] = density[r]
        ext[4 + r, :, own:] = halo((left[r], right[r]), 0)
    depth_filter(ext, middle, summed)
    plane = inverse_plane(height, own, cols_total, place[1])
    for r in range(rows):
        rho = filter_lanes(filter_height(summed[r])) * (
            plane * row_weight(r, rows_total, place[0])
        )
        code = jnp.concatenate(
            [material[r].astype(f32) + 1.0, halo((left[r], right[r]), 1)], axis=1
        )
        frame = k_void + (k_frame - k_void) * rho * rho * rho
        cond = jnp.where(code == 2.0, frame, jnp.where(code == 1.0, k_glass, k_anchor))
        cond = jnp.where(code == 0.0, 0.0, cond)
        rho_out[r] = rho
        if r < 4:
            cond_first[r] = cond
        else:
            cond_last[r - 4] = cond


centre_value = 0.5 * (spectrum_high + spectrum_low)
half_width = 0.5 * (spectrum_high - spectrum_low)
ratio_value = centre_value / half_width
INNER = range(5, 11)


class Rows:
    def __init__(self, ready, first, stop, rest):
        self.ready, self.first, self.stop, self.rest = ready, first, stop, rest

    def __getitem__(self, row):
        if self.first <= row < self.stop:
            return self.ready[row - self.first]
        return self.rest[row]


def face(one, other, store=None):
    inv = 1.0 / jnp.maximum(one + other, 1e-3)
    part = one * inv
    if store is not None:
        here, there, row = store
        rest = other * inv
        there[row] = part * part
        here[row] = rest * rest
    return 2.0 * part * other


def first_residual(value, before, after, load, deep_before, deep, tall, wide):
    inverse = 1.0 / (
        loss_rate + (deep + deep_before) + (tall + behind(tall, 1, 0)) + (wide + behind(wide, 1, 1))
    )
    left_over = load - operate(value, deep_before * (before - value), deep * (value - after), tall, wide)
    direction = left_over * inverse * (1.0 / centre_value)
    return inverse, left_over, direction


def operate(value, flux_before, flux, tall, wide):
    high = tall * (value - ahead(value, 1, 0))
    along = wide * (value - ahead(value, 1, 1))
    return (
        loss_rate * value + (flux - flux_before) + (high - behind(high, 1, 0))
        + (along - behind(along, 1, 1))
    )


def prepare_kernel(
    cond_first, cond_last, prior, source, temp,
    from_above, from_below, corner_above, corner_below, left, right,
    field, load, heat, depth_face, height_face, lane_face,
    depth_here, depth_there, height_here, height_there, lane_here, lane_there,
    inverse, residual, direction, dual,
):
    rows, height, own = prior.shape
    last_level = sub_iota((height, 1)) == height - 1

    def place_row(target, row, main, strips, index):
        target[row, :, :own] = main
        target[row, :, own:] = halo_lanes(strips[0], strips[1], index)

    for r in range(4):
        place_row(field, r, from_above[4 + r], corner(corner_above, r), 3)
        place_row(field, 12 + r, from_below[4 + r], corner(corner_below, r), 3)
    for r in range(3):
        place_row(load, 1 + r, from_above[8 + r], corner(corner_above, 1 + r), 2)
        place_row(load, 12 + r, from_below[8 + r], corner(corner_below, r), 2)
    load[0] = jnp.zeros(load.shape[1:], f32)
    load[15] = jnp.zeros(load.shape[1:], f32)
    place_row(heat, 0, from_above[11], corner(corner_above, 3), 4)
    place_row(heat, 9, from_below[11], corner(corner_below, 0), 4)
    for r in range(rows):
        strips = (left[r], right[r])
        place_row(field, 4 + r, prior[r], strips, 3)
        place_row(load, 4 + r, source[r], strips, 2)
        place_row(heat, 1 + r, temp[r], strips, 4)

    deep_before = None
    following = cond_first[0]
    for r in range(4, 12):
        i = r - 4
        here = following
        tall = jnp.where(
            last_level, 0.0, face(here, ahead(here, 1, 0), (height_here, height_there, i))
        )
        wide = face(here, ahead(here, 1, 1), (lane_here, lane_there, i))
        height_face[i] = tall
        lane_face[i] = wide
        if r < 11:
            following = cond_first[i + 1] if i < 3 else cond_last[i - 3]
            deep = face(here, following, (depth_here, depth_there, i))
            depth_face[i] = deep
        if r in INNER:
            value = field[r]
            one, two, three = first_residual(
                value, field[r - 1], field[r + 1], load[r], deep_before, deep, tall, wide
            )
            k = r - INNER.start
            inverse[k], residual[k], direction[k] = one, two, three
            dual[k] = value + three
        deep_before = deep


def sweep_kernel(
    rows_total, cols_total, place,
    cond_above, cond_first, cond_last, cond_below, rho, material,
    field, load, heat, own_depth_face, own_height_face, own_lane_face,
    own_depth_here, own_depth_there, height_here, height_there, lane_here, lane_there,
    own_inverse, own_residual, own_direction, own_dual, left, right, tallies,
    dual_out, weighted_first, weighted_last,
    depth_face, height_face, lane_face, inverse, residual, first_direction, next_direction, dual,
    edge_here, edge_there,
):
    rows, height, own = rho.shape[0], rho.shape[1], dual_out.shape[2]
    has_above, has_below, has_left, has_right = present(place, rows, own, rows_total, cols_total)
    last_level = sub_iota((height, 1)) == height - 1

    def cond(r):
        if r < 4:
            return cond_above[r] * has_above
        if r >= 12:
            return cond_below[r - 12] * has_below
        return cond_first[r - 4] if r < 8 else cond_last[r - 8]

    depth_faces = Rows(own_depth_face, 4, 11, depth_face)
    height_faces = Rows(own_height_face, 4, 12, height_face)
    lane_faces = Rows(own_lane_face, 4, 12, lane_face)
    inverses = Rows(own_inverse, INNER.start, INNER.stop, inverse)
    residuals = Rows(own_residual, INNER.start, INNER.stop, residual)
    directions = Rows(own_direction, INNER.start, INNER.stop, first_direction)
    duals = Rows(own_dual, INNER.start, INNER.stop, dual)

    following = cond(0)
    for r in range(15):
        if 4 <= r < 11:
            following = None
            continue
        here = cond(r) if following is None else following
        following = cond(r + 1)
        store = (edge_here, edge_there, 0 if r == 3 else 1) if r in (3, 11) else None
        depth_face[r] = face(here, following, store)
        if r in (1, 2, 3, 12, 13, 14):
            height_face[r] = jnp.where(last_level, 0.0, face(here, ahead(here, 1, 0)))
            lane_face[r] = face(here, ahead(here, 1, 1))
    for r in range(1, 15):
        if r in INNER:
            continue
        value = field[r]
        one, two, three = first_residual(
            value, field[r - 1], field[r + 1], load[r],
            depth_faces[r - 1], depth_faces[r], height_faces[r], lane_faces[r],
        )
        inverse[r], residual[r], first_direction[r] = one, two, three
        if 3 <= r < 13:
            dual[r] = value + three

    factor = 1.0 / ratio_value
    now = directions
    for sweep in range(SWEEPS - 1):
        factor_next = 1.0 / (2.0 * ratio_value - factor)
        keep, add = factor_next * factor, 2.0 * factor_next / half_width
        start, stop = 2 + sweep, 14 - sweep
        following = now[start]
        flux_before = depth_faces[start - 1] * (now[start - 1] - following)
        for r in range(start, stop):
            value, following = following, now[r + 1]
            flux = depth_faces[r] * (value - following)
            left_over = residuals[r] - operate(
                value, flux_before, flux, height_faces[r], lane_faces[r]
            )
            direction = keep * value + add * (left_over * inverses[r])
            if sweep < SWEEPS - 2:
                residual[r] = left_over
                next_direction[r] = direction
            if 3 <= r < 13:
                dual[r] = duals[r] + direction
            flux_before = flux
        factor = factor_next
        now, residuals, duals = next_direction, residual, dual

    depth_here = Rows(own_depth_here, 4, 11, {11: edge_here[1]})
    depth_there = Rows(own_depth_there, 4, 11, {3: edge_there[0], 11: edge_there[1]})
    plane = inverse_plane(height, own, cols_total, place[1])
    for r in range(rows):
        dual_out[r] = dual[4 + r, :, :own]
    a, t = dual[3], heat[0]
    a_next, t_next = dual[4], heat[1]
    deep_before = (a - a_next) * (t - t_next) * depth_there[3]
    for r in range(4, 4 + rows):
        row = r - 4
        a, t = a_next, t_next
        a_next, t_next = dual[r + 1], heat[r - 2]
        deep = (a - a_next) * (t - t_next)
        tall = (a - ahead(a, 1, 0)) * (t - ahead(t, 1, 0))
        tall = jnp.where(last_level, 0.0, tall)
        wide = (a - ahead(a, 1, 1)) * (t - ahead(t, 1, 1))
        total = (
            (deep * depth_here[r] + deep_before)
            + (tall * height_here[row] + behind(tall * height_there[row], 1, 0))
            + (wide * lane_here[row] + behind(wide * lane_there[row], 1, 1))
        )
        deep_before = deep * depth_there[r]
        strips = halo_lanes(left[row] * has_left, right[row] * has_right, 1)
        code = jnp.concatenate([material[row].astype(f32) + 1.0, strips], axis=1)
        thick_rho = rho[row]
        value = total * (thick_rho * thick_rho) * (
            plane * (row_weight(row, rows_total, place[0]) * (-6.0 * (k_frame - k_void)))
        )
        value = jnp.where(code == 2.0, value, 0.0)
        if row < 4:
            weighted_first[row] = value
        else:
            weighted_last[row - 4] = value


def grad_kernel(
    rows_total, cols_total, place,
    from_above, first, last, from_below, material, grad_out, message, ext, middle, summed,
):
    rows, height, own = grad_out.shape
    has_above, has_below, _, _ = present(place, rows, own, rows_total, cols_total)
    for r in range(4):
        ext[r] = from_above[r] * has_above
        ext[4 + r] = first[r]
        ext[8 + r] = last[r]
        ext[12 + r] = from_below[r] * has_below
    depth_filter(ext, middle, summed)
    largest = jnp.zeros((height, LANES), f32)
    for r in range(rows):
        grad = filter_lanes(filter_height(summed[r]))[:, :own]
        grad_out[r] = grad
        size = jnp.where(material[r] == 1, jnp.abs(grad), 0.0)
        for block in range(own // LANES):
            largest = jnp.maximum(largest, size[:, block * LANES:(block + 1) * LANES])
    message[...] = jnp.broadcast_to(jnp.max(largest, axis=0, keepdims=True), message.shape)


def lines_kernel(
    solid, newer, older, below_spacing, above_spacing, material,
    below_out, above_out, up_out, low_out, least_out, most_out, upper_out, lower_out, bend_out,
    tallies,
):
    rows, height, own = solid.shape
    base = jnp.zeros((height, LANES), f32)
    count = jnp.zeros((height, LANES), f32)
    for r in range(rows):
        x = solid[r]
        design = material[r] == 1
        gamma = 0.95 + 0.25 * jnp.tanh(gamma_slope * newer[r] * older[r])
        below = x - gamma * below_spacing[r]
        above = x + gamma * above_spacing[r]
        below_out[r] = below
        above_out[r] = above
        up = above - x
        low = x - below
        floor = jnp.maximum(jnp.maximum(0.0, below + 0.1 * low), x - move_limit)
        ceiling = jnp.minimum(jnp.minimum(1.0, above - 0.1 * up), x + move_limit)
        up_out[r] = up
        low_out[r] = low
        least_out[r] = floor - below
        most_out[r] = ceiling - below
        upper_out[r] = jnp.where(design, above_weight * up * up, 0.0)
        lower_out[r] = jnp.where(design, below_weight * low * low, 0.0)
        bend_out[r] = jnp.where(design, up * low / (2.0 * (up + low)), 0.0)
        term = jnp.where(
            design, x - solid_allowance - above_weight * up - below_weight * low, 0.0
        )
        one = jnp.where(design, curve_floor, 0.0)
        for block in range(own // LANES):
            base = base + term[:, block * LANES:(block + 1) * LANES]
            count = count + one[:, block * LANES:(block + 1) * LANES]
    tallies[0] = base
    tallies[1] = count


def reached(rate_above, rate_below, y, up, low, least, most):
    root_above = rate_above + y * above_weight
    root_below = rate_below + y * below_weight
    inv_above, inv_below = lax.rsqrt(root_above), lax.rsqrt(root_below)
    root_above, root_below = root_above * inv_above, root_below * inv_below
    width = up + low
    pull = low * root_below
    trial = width * pull / (up * root_above + pull)
    return trial, jnp.clip(trial, least, most), width, root_above, root_below, inv_above, inv_below


def sums_to_message(slope, curve, message):
    slope = jnp.sum(slope, axis=0, keepdims=True)
    curve = jnp.sum(curve, axis=0, keepdims=True)
    slope = slope + pltpu.roll(slope, LANES // 2, 1)
    curve = curve + pltpu.roll(curve, LANES // 2, 1)
    lane = lane_iota((1, LANES))
    message[...] = jnp.broadcast_to(jnp.where(lane < LANES // 2, slope, curve), message.shape)


def evaluate(y, rate_above, rate_below, up, low, least, most, upper, lower, bend, tallies, message):
    rows, height, own = up.shape
    slope_sum, curve_sum = tallies[0], tallies[1]
    for r in range(rows):
        trial, chosen, width, root_above, root_below, inv_above, inv_below = reached(
            rate_above(r), rate_below(r), y, up[r], low[r], least[r], most[r]
        )
        rest = width - chosen
        slope = (upper[r] * chosen + lower[r] * rest) / (rest * chosen)
        split = above_weight * (inv_above * inv_above) - below_weight * (inv_below * inv_below)
        curve = bend[r] * (root_above * root_below) * (split * split)
        free = (trial > least[r]) & (trial < most[r])
        curve = jnp.where(free, curve, 0.0)
        for block in range(own // LANES):
            slope_sum = slope_sum + slope[:, block * LANES:(block + 1) * LANES]
            curve_sum = curve_sum + curve[:, block * LANES:(block + 1) * LANES]
    sums_to_message(slope_sum, curve_sum, message)


def first_kernel(
    arrived, grad, up, low, least, most, upper, lower, bend, tallies,
    message, rate_above_out, rate_below_out,
):
    scale = jnp.max(jnp.max(arrived[...], axis=0, keepdims=True), axis=1, keepdims=True)
    inverse = 1.0 / (scale + 1e-06)

    def above(r):
        element = grad[r] * inverse
        value = jnp.maximum(1.001 * element, -0.001 * element) + 1e-05
        rate_above_out[r] = value
        return value

    def below(r):
        element = grad[r] * inverse
        value = jnp.maximum(0.001 * element, -1.001 * element) + 1e-05
        rate_below_out[r] = value
        return value

    evaluate(
        jnp.ones((1, 1), f32), above, below, up, low, least, most, upper, lower, bend, tallies, message
    )


def advance(arrived, y):
    total = jnp.sum(arrived[...], axis=0, keepdims=True)
    lane = lane_iota(total.shape)
    slope = jnp.sum(jnp.where(lane < LANES // 2, total, 0.0), axis=1, keepdims=True)
    curve = jnp.sum(jnp.where(lane < LANES // 2, 0.0, total), axis=1, keepdims=True)
    return jnp.maximum(0.0, y + slope / curve)


def step_kernel(
    arrived, y_ref, rate_above, rate_below, up, low, least, most, upper, lower, bend, tallies,
    message, y_out,
):
    y = advance(arrived, y_ref[0:1, 0:1])
    y_out[...] = jnp.broadcast_to(y, y_out.shape)
    evaluate(
        y, lambda r: rate_above[r], lambda r: rate_below[r],
        up, low, least, most, upper, lower, bend, tallies, message,
    )


def last_kernel(
    arrived, y_ref, rate_above, rate_below, up, low, least, most, below, solid, material, out
):
    y = advance(arrived, y_ref[0:1, 0:1])
    for r in range(out.shape[0]):
        chosen = reached(rate_above[r], rate_below[r], y, up[r], low[r], least[r], most[r])[1]
        out[r] = jnp.where(material[r] == 1, below[r] + chosen, solid[r])


def with_place(kernel, rows_total, cols_total):
    def body(place_ref, *refs):
        kernel(rows_total, cols_total, (place_ref[0], place_ref[1]), *refs)

    return body


def placed_call(kernel, place, outs, args, scratch, totals):
    vmem = pl.BlockSpec(memory_space=pltpu.VMEM)
    return pl.pallas_call(
        with_place(kernel, *totals),
        out_shape=[jax.ShapeDtypeStruct(shape, f32) for shape in outs],
        in_specs=[pl.BlockSpec(memory_space=pltpu.SMEM)] + [vmem] * len(args),
        out_specs=[vmem] * len(outs),
        scratch_shapes=[pltpu.VMEM(shape, f32) for shape in scratch],
        compiler_params=pltpu.CompilerParams(vmem_limit_bytes=40 * 1024 * 1024),
    )(place, *args)


def launch_messages(density, material, source, prior, temp):
    rows, height, own = density.shape
    end = own // LANES - 1
    block, message = (rows, height, LANES), (12, height, own)
    first = pl.BlockSpec(block, lambda i: (0, 0, 0))
    last = pl.BlockSpec(block, lambda i: (0, 0, end))

    def layers(count, index):
        return pl.BlockSpec((count, height, own), lambda i: (index, 0, 0))

    strips = (density, material, source, prior, temp)
    layered = (density, prior, source, temp)
    return pl.pallas_call(
        launch_kernel,
        grid=(1,),
        out_shape=[jax.ShapeDtypeStruct(s, f32) for s in (block, block, message, message)],
        in_specs=[first] * 5 + [last] * 5
        + [layers(4, 0)] * 3 + [layers(1, 0)] + [layers(4, rows // 4 - 1)] * 3 + [layers(1, rows - 1)],
        out_specs=[pl.BlockSpec(s, lambda i: (0, 0, 0)) for s in (block, block, message, message)],
    )(*strips, *strips, *layered, *layered)


def on_device(
    solid_occupancy,
    newer_occupancy_shift,
    older_occupancy_shift,
    below_limit_spacing,
    above_limit_spacing,
    thermal_state,
    loss_state_derivative,
    prior_dual_state,
    cell_material,
):
    rows, height, own = solid_occupancy.shape
    deep, long = lax.axis_size("thick"), lax.axis_size("facade")
    totals = (rows * deep, own * long)
    place = jnp.stack(
        [lax.axis_index("thick") * rows, lax.axis_index("facade") * own]
    ).astype(jnp.int32)
    width = own + LANES
    whole = (rows, height, own)

    def turn(axis, size, step):
        pairs = [(i, (i + step) % size) for i in range(size)]
        return lambda value: lax.ppermute(value, axis, pairs)

    to_right, to_left = turn("facade", long, 1), turn("facade", long, -1)
    to_deeper, to_nearer = turn("thick", deep, 1), turn("thick", deep, -1)

    first_strips, last_strips, rows_up, rows_down = launch_messages(
        solid_occupancy, cell_material, loss_state_derivative, prior_dual_state, thermal_state
    )
    right, left = to_left(first_strips), to_right(last_strips)
    from_above, from_below = to_deeper(rows_up), to_nearer(rows_down)
    corner_above = to_deeper(jnp.concatenate([left[rows - 4:], right[rows - 4:]]))
    corner_below = to_nearer(jnp.concatenate([left[:4], right[:4]]))

    (below, above, up, low, least, most, upper, lower, bend, tallies) = call(
        lines_kernel,
        [whole] * 9 + [(2, height, LANES)],
        (
            solid_occupancy, newer_occupancy_shift, older_occupancy_shift,
            below_limit_spacing, above_limit_spacing, cell_material,
        ),
    )

    four = (4, height, width)
    rho, cond_first, cond_last = placed_call(
        rho_kernel, place,
        [(rows, height, width), four, four],
        (
            solid_occupancy, cell_material, from_above, from_below,
            corner_above, corner_below, left, right,
        ),
        [(BOTH_SIDES, height, width), (BOTH_SIDES - 4, height, width), (rows, height, width)],
        totals,
    )
    cond_above, cond_below = to_deeper(cond_last), to_nearer(cond_first)
    tall, own_wide, inner = (
        (BOTH_SIDES, height, width), (rows, height, width), (len(INNER), height, width),
    )
    prepared = call(
        prepare_kernel,
        [tall, tall, (rows + 2, height, width)] + [own_wide] * 9 + [inner] * 4,
        (
            cond_first, cond_last, prior_dual_state, loss_state_derivative, thermal_state,
            from_above, from_below, corner_above, corner_below, left, right,
        ),
    )
    dual_state, weighted_first, weighted_last = placed_call(
        sweep_kernel, place,
        [whole, four, four],
        (
            cond_above, cond_first, cond_last, cond_below, rho, cell_material, *prepared,
            left, right, tallies,
        ),
        [tall] * 8 + [(2, height, width)] * 2,
        totals,
    )
    weighted_above, weighted_below = to_deeper(weighted_last), to_nearer(weighted_first)
    count = deep * long
    note = (count, LANES)
    grad, message = placed_call(
        grad_kernel, place,
        [whole, note],
        (weighted_above, weighted_first, weighted_last, weighted_below, cell_material),
        [tall, (BOTH_SIDES - 4, height, width), (rows, height, width)],
        totals,
    )

    def everyone(rows_out):
        return lax.all_to_all(rows_out, AXES, 0, 0, tiled=True)

    fixed = (up, low, least, most, upper, lower, bend, tallies)
    message, rate_above, rate_below = call(
        first_kernel, [note, whole, whole], (everyone(message), grad) + fixed
    )
    y = jnp.ones((8, LANES), f32)
    for _ in range(NEWTON - 1):
        message, y = call(
            step_kernel, [note, (8, LANES)],
            (everyone(message), y, rate_above, rate_below) + fixed,
        )
    (density_new,) = call(
        last_kernel, [whole],
        (
            everyone(message), y, rate_above, rate_below, up, low, least, most, below,
            solid_occupancy, cell_material,
        ),
    )
    return (density_new, below, above, dual_state)


def solution(mesh):
    spec = P("thick", None, "facade")
    return jax.shard_map(
        on_device,
        mesh=mesh,
        in_specs=(spec,) * 9,
        out_specs=(spec,) * 4,
        check_vma=False,
    )
```

```python
import functools
import jax
import jax.numpy as jnp
from jax import lax
from jax.experimental import pallas as pl
from jax.experimental.pallas import tpu as pltpu
from jax.sharding import PartitionSpec as P

RADIUS = 4
SWEEPS = 3
NEWTON = 8

k_void = 0.03
k_frame = 160.0
k_glass = 1.0
k_anchor = 50.0
loss_rate = 0.05
spectrum_low = 0.05
spectrum_high = 2.0
solid_allowance = 0.35
curve_floor = 0.05
move_limit = 0.2
gamma_slope = 200.0

LANES = 128
STRIP = 16
above_weight = 1.001 + 1e-05
below_weight = 0.001 + 1e-05

f32 = jnp.float32
AXES = ("thick", "facade")
BOTH_SIDES = 16


def call(kernel, outs, args, scratch=()):
    vmem = pl.BlockSpec(memory_space=pltpu.VMEM)
    return pl.pallas_call(
        kernel,
        out_shape=[jax.ShapeDtypeStruct(shape, f32) for shape in outs],
        in_specs=[vmem] * len(args),
        out_specs=[vmem] * len(outs),
        scratch_shapes=[pltpu.VMEM(shape, f32) for shape in scratch],
        compiler_params=pltpu.CompilerParams(vmem_limit_bytes=40 * 1024 * 1024),
    )(*args)


def lane_iota(shape):
    return lax.broadcasted_iota(jnp.int32, shape, len(shape) - 1)


def sub_iota(shape):
    return lax.broadcasted_iota(jnp.int32, shape, len(shape) - 2)


def ahead(value, step, axis):
    return pltpu.roll(value, (value.shape[axis] - step) % value.shape[axis], axis)


def behind(value, step, axis):
    return pltpu.roll(value, step, axis)


def launch_kernel(*refs):
    firsts, lasts, nears, fars = refs[0:5], refs[5:10], refs[10:14], refs[14:18]
    to_left, to_right, rows_up, rows_down = refs[18:22]
    left_corners, right_corners = refs[22:24], refs[24:26]
    rows, height, _ = to_left.shape
    group = lane_iota((height, LANES)) // STRIP
    for row in range(rows):
        for source, target, corners, place in (
            (firsts, to_left, left_corners, 0), (lasts, to_right, right_corners, LANES - STRIP)
        ):
            packed = jnp.zeros((height, LANES), f32)
            for index, ref in enumerate(source):
                value = ref[row]
                if value.dtype != f32:
                    value = value.astype(f32) + 1.0
                shift = (STRIP * index - place) % LANES
                if shift:
                    value = pltpu.roll(value, shift, 1)
                packed = jnp.where(group == index, value, packed)
            target[row] = packed
            if row < 4:
                corners[0][row] = packed
            if row >= rows - 4:
                corners[1][row - rows + 4] = packed
    start = 0
    for near, far, count in zip(nears, fars, (4, 4, 3, 1)):
        for r in range(count):
            rows_down[start + r] = near[r]
            rows_up[start + r] = far[far.shape[0] - count + r]
        start += count


def halo_lanes(left, right, index):
    lane = lane_iota(left.shape)
    shift = (LANES - STRIP * index) % LANES
    after = pltpu.roll(right, shift, 1) if shift else right
    shift = (LANES - STRIP - STRIP * index) % LANES
    before = pltpu.roll(left, shift, 1) if shift else left
    return jnp.where(lane < STRIP, after, jnp.where(lane >= LANES - STRIP, before, 0.0))


def axis_weight(position, total):
    acc = jnp.zeros(position.shape, f32)
    for offset in range(-RADIUS, RADIUS + 1):
        weight = float(RADIUS + 1 - abs(offset))
        inside = (position + offset >= 0) & (position + offset < total)
        acc = acc + jnp.where(inside, weight, 0.0)
    return jnp.maximum(acc, 1.0)


def inverse_plane(height, own, cols_total, col_start):
    width = own + LANES
    lane = lane_iota((1, width))
    place = jnp.where(lane < own + LANES // 2, lane, lane - width) + col_start
    middle = axis_weight(sub_iota((height, 1)), height)
    return 1.0 / (middle * axis_weight(place, cols_total))


def row_weight(row, rows_total, row_start):
    return 1.0 / axis_weight(jnp.full((1, 1), row + row_start, jnp.int32), rows_total)


def filter_height(value):
    height = value.shape[0]
    level = sub_iota((height, 1))
    total = float(RADIUS + 1) * value
    for offset in range(1, RADIUS + 1):
        weight = float(RADIUS + 1 - offset)
        up = jnp.where(level < height - offset, weight, 0.0)
        down = jnp.where(level >= offset, weight, 0.0)
        total = total + up * ahead(value, offset, 0) + down * behind(value, offset, 0)
    return total


def filter_lanes(value):
    def box(v):
        pair = v + ahead(v, 1, 1)
        return pair + ahead(pair, 2, 1) + behind(v, 1, 1)

    def box_back(v):
        pair = v + behind(v, 1, 1)
        return pair + behind(pair, 2, 1) + ahead(v, 1, 1)

    return box_back(box(value))


def depth_filter(source, middle, target):
    count = source.shape[0]
    for r in range(count - 4):
        middle[r] = (source[r] + source[r + 1]) + (source[r + 2] + source[r + 3]) + source[r + 4]
    for r in range(count - 8):
        target[r] = (middle[r] + middle[r + 1]) + (middle[r + 2] + middle[r + 3]) + middle[r + 4]


def present(place, rows, own, rows_total, cols_total):
    row_start, col_start = place

    def flag(condition):
        return jnp.where(condition, 1.0, 0.0).astype(f32)

    return (
        flag(row_start > 0), flag(row_start + rows < rows_total),
        flag(col_start > 0), flag(col_start + own < cols_total),
    )


def corner(strips, row):
    return strips[0][row], strips[1][row]


def rho_kernel(
    rows_total, cols_total, place,
    density, material, from_above, from_below,
    above_left, above_right, below_left, below_right, left, right,
    rho_out, cond_first, cond_last,
    ext, middle, summed,
):
    corner_above, corner_below = (above_left, above_right), (below_left, below_right)
    rows, height, own = density.shape
    has_above, has_below, has_left, has_right = present(place, rows, own, rows_total, cols_total)

    def halo(strips, index):
        return halo_lanes(strips[0] * has_left, strips[1] * has_right, index)

    for r in range(4):
        ext[r, :, :own] = from_above[r] * has_above
        ext[r, :, own:] = halo(corner(corner_above, r), 0) * has_above
        ext[rows + 4 + r, :, :own] = from_below[r] * has_below
        ext[rows + 4 + r, :, own:] = halo(corner(corner_below, r), 0) * has_below
    for r in range(rows):
        ext[4 + r, :, :own] = density[r]
        ext[4 + r, :, own:] = halo((left[r], right[r]), 0)
    depth_filter(ext, middle, summed)
    plane = inverse_plane(height, own, cols_total, place[1])
    for r in range(rows):
        rho = filter_lanes(filter_height(summed[r])) * (
            plane * row_weight(r, rows_total, place[0])
        )
        code = jnp.concatenate(
            [material[r].astype(f32) + 1.0, halo((left[r], right[r]), 1)], axis=1
        )
        frame = k_void + (k_frame - k_void) * rho * rho * rho
        cond = jnp.where(code == 2.0, frame, jnp.where(code == 1.0, k_glass, k_anchor))
        cond = jnp.where(code == 0.0, 0.0, cond)
        rho_out[r] = rho
        if r < 4:
            cond_first[r] = cond
        else:
            cond_last[r - 4] = cond


centre_value = 0.5 * (spectrum_high + spectrum_low)
half_width = 0.5 * (spectrum_high - spectrum_low)
ratio_value = centre_value / half_width
INNER = range(5, 11)


class Rows:
    def __init__(self, ready, first, stop, rest):
        self.ready, self.first, self.stop, self.rest = ready, first, stop, rest

    def __getitem__(self, row):
        if self.first <= row < self.stop:
            return self.ready[row - self.first]
        return self.rest[row]


def face(one, other, store=None):
    inv = 1.0 / jnp.maximum(one + other, 1e-3)
    part = one * inv
    if store is not None:
        here, there, row = store
        rest = other * inv
        there[row] = part * part
        here[row] = rest * rest
    return 2.0 * part * other


def first_residual(value, before, after, load, deep_before, deep, tall, wide):
    inverse = 1.0 / (
        loss_rate + (deep + deep_before) + (tall + behind(tall, 1, 0)) + (wide + behind(wide, 1, 1))
    )
    left_over = load - operate(value, deep_before * (before - value), deep * (value - after), tall, wide)
    direction = left_over * inverse * (1.0 / centre_value)
    return inverse, left_over, direction


def operate(value, flux_before, flux, tall, wide):
    high = tall * (value - ahead(value, 1, 0))
    along = wide * (value - ahead(value, 1, 1))
    return (
        loss_rate * value + (flux - flux_before) + (high - behind(high, 1, 0))
        + (along - behind(along, 1, 1))
    )


def prepare_kernel(
    cond_first, cond_last, prior, source, temp,
    from_above, from_below, above_left, above_right, below_left, below_right, left, right,
    field, load, heat, depth_face, height_face, lane_face,
    depth_here, depth_there, height_here, height_there, lane_here, lane_there,
    inverse, residual, direction, dual,
):
    rows, height, own = prior.shape
    corner_above, corner_below = (above_left, above_right), (below_left, below_right)
    last_level = sub_iota((height, 1)) == height - 1

    def place_row(target, row, main, strips, index):
        target[row, :, :own] = main
        target[row, :, own:] = halo_lanes(strips[0], strips[1], index)

    for r in range(4):
        place_row(field, r, from_above[4 + r], corner(corner_above, r), 3)
        place_row(field, 12 + r, from_below[4 + r], corner(corner_below, r), 3)
    for r in range(3):
        place_row(load, 1 + r, from_above[8 + r], corner(corner_above, 1 + r), 2)
        place_row(load, 12 + r, from_below[8 + r], corner(corner_below, r), 2)
    load[0] = jnp.zeros(load.shape[1:], f32)
    load[15] = jnp.zeros(load.shape[1:], f32)
    place_row(heat, 0, from_above[11], corner(corner_above, 3), 4)
    place_row(heat, 9, from_below[11], corner(corner_below, 0), 4)
    for r in range(rows):
        strips = (left[r], right[r])
        place_row(field, 4 + r, prior[r], strips, 3)
        place_row(load, 4 + r, source[r], strips, 2)
        place_row(heat, 1 + r, temp[r], strips, 4)

    deep_before = None
    following = cond_first[0]
    for r in range(4, 12):
        i = r - 4
        here = following
        tall = jnp.where(
            last_level, 0.0, face(here, ahead(here, 1, 0), (height_here, height_there, i))
        )
        wide = face(here, ahead(here, 1, 1), (lane_here, lane_there, i))
        height_face[i] = tall
        lane_face[i] = wide
        if r < 11:
            following = cond_first[i + 1] if i < 3 else cond_last[i - 3]
            deep = face(here, following, (depth_here, depth_there, i))
            depth_face[i] = deep
        if r in INNER:
            value = field[r]
            one, two, three = first_residual(
                value, field[r - 1], field[r + 1], load[r], deep_before, deep, tall, wide
            )
            k = r - INNER.start
            inverse[k], residual[k], direction[k] = one, two, three
            dual[k] = value + three
        deep_before = deep


def sweep_kernel(
    rows_total, cols_total, place,
    cond_above, cond_first, cond_last, cond_below, rho, material,
    field, load, heat, own_depth_face, own_height_face, own_lane_face,
    own_depth_here, own_depth_there, height_here, height_there, lane_here, lane_there,
    own_inverse, own_residual, own_direction, own_dual, left, right, tallies,
    dual_out, weighted_first, weighted_last,
    depth_face, height_face, lane_face, inverse, residual, first_direction, next_direction, dual,
    edge_here, edge_there,
):
    rows, height, own = rho.shape[0], rho.shape[1], dual_out.shape[2]
    has_above, has_below, has_left, has_right = present(place, rows, own, rows_total, cols_total)
    last_level = sub_iota((height, 1)) == height - 1

    def cond(r):
        if r < 4:
            return cond_above[r] * has_above
        if r >= 12:
            return cond_below[r - 12] * has_below
        return cond_first[r - 4] if r < 8 else cond_last[r - 8]

    depth_faces = Rows(own_depth_face, 4, 11, depth_face)
    height_faces = Rows(own_height_face, 4, 12, height_face)
    lane_faces = Rows(own_lane_face, 4, 12, lane_face)
    inverses = Rows(own_inverse, INNER.start, INNER.stop, inverse)
    residuals = Rows(own_residual, INNER.start, INNER.stop, residual)
    directions = Rows(own_direction, INNER.start, INNER.stop, first_direction)
    duals = Rows(own_dual, INNER.start, INNER.stop, dual)

    following = cond(0)
    for r in range(15):
        if 4 <= r < 11:
            following = None
            continue
        here = cond(r) if following is None else following
        following = cond(r + 1)
        store = (edge_here, edge_there, 0 if r == 3 else 1) if r in (3, 11) else None
        depth_face[r] = face(here, following, store)
        if r in (1, 2, 3, 12, 13, 14):
            height_face[r] = jnp.where(last_level, 0.0, face(here, ahead(here, 1, 0)))
            lane_face[r] = face(here, ahead(here, 1, 1))
    for r in range(1, 15):
        if r in INNER:
            continue
        value = field[r]
        one, two, three = first_residual(
            value, field[r - 1], field[r + 1], load[r],
            depth_faces[r - 1], depth_faces[r], height_faces[r], lane_faces[r],
        )
        inverse[r], residual[r], first_direction[r] = one, two, three
        if 3 <= r < 13:
            dual[r] = value + three

    factor = 1.0 / ratio_value
    now = directions
    for sweep in range(SWEEPS - 1):
        factor_next = 1.0 / (2.0 * ratio_value - factor)
        keep, add = factor_next * factor, 2.0 * factor_next / half_width
        start, stop = 2 + sweep, 14 - sweep
        following = now[start]
        flux_before = depth_faces[start - 1] * (now[start - 1] - following)
        for r in range(start, stop):
            value, following = following, now[r + 1]
            flux = depth_faces[r] * (value - following)
            left_over = residuals[r] - operate(
                value, flux_before, flux, height_faces[r], lane_faces[r]
            )
            direction = keep * value + add * (left_over * inverses[r])
            if sweep < SWEEPS - 2:
                residual[r] = left_over
                next_direction[r] = direction
            if 3 <= r < 13:
                dual[r] = duals[r] + direction
            flux_before = flux
        factor = factor_next
        now, residuals, duals = next_direction, residual, dual

    depth_here = Rows(own_depth_here, 4, 11, {11: edge_here[1]})
    depth_there = Rows(own_depth_there, 4, 11, {3: edge_there[0], 11: edge_there[1]})
    plane = inverse_plane(height, own, cols_total, place[1])
    for r in range(rows):
        dual_out[r] = dual[4 + r, :, :own]
    a, t = dual[3], heat[0]
    a_next, t_next = dual[4], heat[1]
    deep_before = (a - a_next) * (t - t_next) * depth_there[3]
    for r in range(4, 4 + rows):
        row = r - 4
        a, t = a_next, t_next
        a_next, t_next = dual[r + 1], heat[r - 2]
        deep = (a - a_next) * (t - t_next)
        tall = (a - ahead(a, 1, 0)) * (t - ahead(t, 1, 0))
        tall = jnp.where(last_level, 0.0, tall)
        wide = (a - ahead(a, 1, 1)) * (t - ahead(t, 1, 1))
        total = (
            (deep * depth_here[r] + deep_before)
            + (tall * height_here[row] + behind(tall * height_there[row], 1, 0))
            + (wide * lane_here[row] + behind(wide * lane_there[row], 1, 1))
        )
        deep_before = deep * depth_there[r]
        strips = halo_lanes(left[row] * has_left, right[row] * has_right, 1)
        code = jnp.concatenate([material[row].astype(f32) + 1.0, strips], axis=1)
        thick_rho = rho[row]
        value = total * (thick_rho * thick_rho) * (
            plane * (row_weight(row, rows_total, place[0]) * (-6.0 * (k_frame - k_void)))
        )
        value = jnp.where(code == 2.0, value, 0.0)
        if row < 4:
            weighted_first[row] = value
        else:
            weighted_last[row - 4] = value


def grad_kernel(
    rows_total, cols_total, place,
    from_above, first, last, from_below, material, grad_out, message, ext, middle, summed,
):
    rows, height, own = grad_out.shape
    has_above, has_below, _, _ = present(place, rows, own, rows_total, cols_total)
    for r in range(4):
        ext[r] = from_above[r] * has_above
        ext[4 + r] = first[r]
        ext[8 + r] = last[r]
        ext[12 + r] = from_below[r] * has_below
    depth_filter(ext, middle, summed)
    largest = jnp.zeros((height, LANES), f32)
    for r in range(rows):
        grad = filter_lanes(filter_height(summed[r]))[:, :own]
        grad_out[r] = grad
        size = jnp.where(material[r] == 1, jnp.abs(grad), 0.0)
        for block in range(own // LANES):
            largest = jnp.maximum(largest, size[:, block * LANES:(block + 1) * LANES])
    message[...] = jnp.broadcast_to(jnp.max(largest, axis=0, keepdims=True), message.shape)


def lines_kernel(
    solid, newer, older, below_spacing, above_spacing, material,
    below_out, above_out, up_out, low_out, least_out, most_out, upper_out, lower_out, bend_out,
    tallies,
):
    rows, height, own = solid.shape
    base = jnp.zeros((height, LANES), f32)
    count = jnp.zeros((height, LANES), f32)
    for r in range(rows):
        x = solid[r]
        design = material[r] == 1
        gamma = 0.95 + 0.25 * jnp.tanh(gamma_slope * newer[r] * older[r])
        below = x - gamma * below_spacing[r]
        above = x + gamma * above_spacing[r]
        below_out[r] = below
        above_out[r] = above
        up = above - x
        low = x - below
        floor = jnp.maximum(jnp.maximum(0.0, below + 0.1 * low), x - move_limit)
        ceiling = jnp.minimum(jnp.minimum(1.0, above - 0.1 * up), x + move_limit)
        up_out[r] = up
        low_out[r] = low
        least_out[r] = floor - below
        most_out[r] = ceiling - below
        upper_out[r] = jnp.where(design, above_weight * up * up, 0.0)
        lower_out[r] = jnp.where(design, below_weight * low * low, 0.0)
        bend_out[r] = jnp.where(design, up * low / (2.0 * (up + low)), 0.0)
        term = jnp.where(
            design, x - solid_allowance - above_weight * up - below_weight * low, 0.0
        )
        one = jnp.where(design, curve_floor, 0.0)
        for block in range(own // LANES):
            base = base + term[:, block * LANES:(block + 1) * LANES]
            count = count + one[:, block * LANES:(block + 1) * LANES]
    tallies[0] = base
    tallies[1] = count


def reached(rate_above, rate_below, y, up, low, least, most):
    root_above = rate_above + y * above_weight
    root_below = rate_below + y * below_weight
    inv_above, inv_below = lax.rsqrt(root_above), lax.rsqrt(root_below)
    root_above, root_below = root_above * inv_above, root_below * inv_below
    width = up + low
    pull = low * root_below
    trial = width * pull / (up * root_above + pull)
    return trial, jnp.clip(trial, least, most), width, root_above, root_below, inv_above, inv_below


def sums_to_message(slope, curve, message):
    slope = jnp.sum(slope, axis=0, keepdims=True)
    curve = jnp.sum(curve, axis=0, keepdims=True)
    slope = slope + pltpu.roll(slope, LANES // 2, 1)
    curve = curve + pltpu.roll(curve, LANES // 2, 1)
    lane = lane_iota((1, LANES))
    message[...] = jnp.broadcast_to(jnp.where(lane < LANES // 2, slope, curve), message.shape)


def evaluate(y, rate_above, rate_below, up, low, least, most, upper, lower, bend, tallies, message):
    rows, height, own = up.shape
    slope_sum, curve_sum = tallies[0], tallies[1]
    for r in range(rows):
        trial, chosen, width, root_above, root_below, inv_above, inv_below = reached(
            rate_above(r), rate_below(r), y, up[r], low[r], least[r], most[r]
        )
        rest = width - chosen
        slope = (upper[r] * chosen + lower[r] * rest) / (rest * chosen)
        split = above_weight * (inv_above * inv_above) - below_weight * (inv_below * inv_below)
        curve = bend[r] * (root_above * root_below) * (split * split)
        free = (trial > least[r]) & (trial < most[r])
        curve = jnp.where(free, curve, 0.0)
        for block in range(own // LANES):
            slope_sum = slope_sum + slope[:, block * LANES:(block + 1) * LANES]
            curve_sum = curve_sum + curve[:, block * LANES:(block + 1) * LANES]
    sums_to_message(slope_sum, curve_sum, message)


def first_kernel(
    arrived, grad, up, low, least, most, upper, lower, bend, tallies,
    message, rate_above_out, rate_below_out,
):
    scale = jnp.max(jnp.max(arrived[...], axis=0, keepdims=True), axis=1, keepdims=True)
    inverse = 1.0 / (scale + 1e-06)

    def above(r):
        element = grad[r] * inverse
        value = jnp.maximum(1.001 * element, -0.001 * element) + 1e-05
        rate_above_out[r] = value
        return value

    def below(r):
        element = grad[r] * inverse
        value = jnp.maximum(0.001 * element, -1.001 * element) + 1e-05
        rate_below_out[r] = value
        return value

    evaluate(
        jnp.ones((1, 1), f32), above, below, up, low, least, most, upper, lower, bend, tallies, message
    )


def advance(arrived, y):
    total = jnp.sum(arrived[...], axis=0, keepdims=True)
    lane = lane_iota(total.shape)
    slope = jnp.sum(jnp.where(lane < LANES // 2, total, 0.0), axis=1, keepdims=True)
    curve = jnp.sum(jnp.where(lane < LANES // 2, 0.0, total), axis=1, keepdims=True)
    return jnp.maximum(0.0, y + slope / curve)


def step_kernel(
    arrived, y_ref, rate_above, rate_below, up, low, least, most, upper, lower, bend, tallies,
    message, y_out,
):
    y = advance(arrived, y_ref[0:1, 0:1])
    y_out[...] = jnp.broadcast_to(y, y_out.shape)
    evaluate(
        y, lambda r: rate_above[r], lambda r: rate_below[r],
        up, low, least, most, upper, lower, bend, tallies, message,
    )


def last_kernel(
    arrived, y_ref, rate_above, rate_below, up, low, least, most, below, solid, material, out
):
    y = advance(arrived, y_ref[0:1, 0:1])
    for r in range(out.shape[0]):
        chosen = reached(rate_above[r], rate_below[r], y, up[r], low[r], least[r], most[r])[1]
        out[r] = jnp.where(material[r] == 1, below[r] + chosen, solid[r])


def with_place(kernel, rows_total, cols_total):
    def body(place_ref, *refs):
        kernel(rows_total, cols_total, (place_ref[0], place_ref[1]), *refs)

    return body


def placed_call(kernel, place, outs, args, scratch, totals):
    vmem = pl.BlockSpec(memory_space=pltpu.VMEM)
    return pl.pallas_call(
        with_place(kernel, *totals),
        out_shape=[jax.ShapeDtypeStruct(shape, f32) for shape in outs],
        in_specs=[pl.BlockSpec(memory_space=pltpu.SMEM)] + [vmem] * len(args),
        out_specs=[vmem] * len(outs),
        scratch_shapes=[pltpu.VMEM(shape, f32) for shape in scratch],
        compiler_params=pltpu.CompilerParams(vmem_limit_bytes=40 * 1024 * 1024),
    )(place, *args)


def launch_messages(density, material, source, prior, temp):
    rows, height, own = density.shape
    end = own // LANES - 1
    block, message, half = (rows, height, LANES), (12, height, own), (4, height, LANES)
    outs = (block, block, message, message, half, half, half, half)
    first = pl.BlockSpec(block, lambda i: (0, 0, 0))
    last = pl.BlockSpec(block, lambda i: (0, 0, end))

    def layers(count, index):
        return pl.BlockSpec((count, height, own), lambda i: (index, 0, 0))

    strips = (density, material, source, prior, temp)
    layered = (density, prior, source, temp)
    return pl.pallas_call(
        launch_kernel,
        grid=(1,),
        out_shape=[jax.ShapeDtypeStruct(s, f32) for s in outs],
        in_specs=[first] * 5 + [last] * 5
        + [layers(4, 0)] * 3 + [layers(1, 0)] + [layers(4, rows // 4 - 1)] * 3 + [layers(1, rows - 1)],
        out_specs=[pl.BlockSpec(s, lambda i: (0, 0, 0)) for s in outs],
    )(*strips, *strips, *layered, *layered)


def on_device(
    solid_occupancy,
    newer_occupancy_shift,
    older_occupancy_shift,
    below_limit_spacing,
    above_limit_spacing,
    thermal_state,
    loss_state_derivative,
    prior_dual_state,
    cell_material,
):
    rows, height, own = solid_occupancy.shape
    deep, long = lax.axis_size("thick"), lax.axis_size("facade")
    totals = (rows * deep, own * long)
    place = jnp.stack(
        [lax.axis_index("thick") * rows, lax.axis_index("facade") * own]
    ).astype(jnp.int32)
    width = own + LANES
    whole = (rows, height, own)

    def turn(axis, size, step):
        pairs = [(i, (i + step) % size) for i in range(size)]
        return lambda value: lax.ppermute(value, axis, pairs)

    to_right, to_left = turn("facade", long, 1), turn("facade", long, -1)
    to_deeper, to_nearer = turn("thick", deep, 1), turn("thick", deep, -1)

    def diagonal(deeper, righter):
        pairs = [
            (i * long + j, (i + deeper) % deep * long + (j + righter) % long)
            for i in range(deep) for j in range(long)
        ]
        return lambda value: lax.ppermute(value, AXES, pairs)

    (
        first_strips, last_strips, rows_up, rows_down, first_near, first_far, last_near, last_far,
    ) = launch_messages(
        solid_occupancy, cell_material, loss_state_derivative, prior_dual_state, thermal_state
    )
    from_above, from_below = to_deeper(rows_up), to_nearer(rows_down)
    right, left = to_left(first_strips), to_right(last_strips)
    corners = (
        diagonal(1, 1)(last_far), diagonal(1, -1)(first_far),
        diagonal(-1, 1)(last_near), diagonal(-1, -1)(first_near),
    )

    (below, above, up, low, least, most, upper, lower, bend, tallies) = call(
        lines_kernel,
        [whole] * 9 + [(2, height, LANES)],
        (
            solid_occupancy, newer_occupancy_shift, older_occupancy_shift,
            below_limit_spacing, above_limit_spacing, cell_material,
        ),
    )

    four = (4, height, width)
    rho, cond_first, cond_last = placed_call(
        rho_kernel, place,
        [(rows, height, width), four, four],
        (
            solid_occupancy, cell_material, from_above, from_below, *corners, left, right,
        ),
        [(BOTH_SIDES, height, width), (BOTH_SIDES - 4, height, width), (rows, height, width)],
        totals,
    )
    cond_above, cond_below = to_deeper(cond_last), to_nearer(cond_first)
    tall, own_wide, inner = (
        (BOTH_SIDES, height, width), (rows, height, width), (len(INNER), height, width),
    )
    prepared = call(
        prepare_kernel,
        [tall, tall, (rows + 2, height, width)] + [own_wide] * 9 + [inner] * 4,
        (
            cond_first, cond_last, prior_dual_state, loss_state_derivative, thermal_state,
            from_above, from_below, *corners, left, right,
        ),
    )
    dual_state, weighted_first, weighted_last = placed_call(
        sweep_kernel, place,
        [whole, four, four],
        (
            cond_above, cond_first, cond_last, cond_below, rho, cell_material, *prepared,
            left, right, tallies,
        ),
        [tall] * 8 + [(2, height, width)] * 2,
        totals,
    )
    weighted_above, weighted_below = to_deeper(weighted_last), to_nearer(weighted_first)
    count = deep * long
    note = (count, LANES)
    grad, message = placed_call(
        grad_kernel, place,
        [whole, note],
        (weighted_above, weighted_first, weighted_last, weighted_below, cell_material),
        [tall, (BOTH_SIDES - 4, height, width), (rows, height, width)],
        totals,
    )

    def everyone(rows_out):
        return lax.all_to_all(rows_out, AXES, 0, 0, tiled=True)

    fixed = (up, low, least, most, upper, lower, bend, tallies)
    message, rate_above, rate_below = call(
        first_kernel, [note, whole, whole], (everyone(message), grad) + fixed
    )
    y = jnp.ones((8, LANES), f32)
    for _ in range(NEWTON - 1):
        message, y = call(
            step_kernel, [note, (8, LANES)],
            (everyone(message), y, rate_above, rate_below) + fixed,
        )
    (density_new,) = call(
        last_kernel, [whole],
        (
            everyone(message), y, rate_above, rate_below, up, low, least, most, below,
            solid_occupancy, cell_material,
        ),
    )
    return (density_new, below, above, dual_state)


def solution(mesh):
    spec = P("thick", None, "facade")
    return jax.shard_map(
        on_device,
        mesh=mesh,
        in_specs=(spec,) * 9,
        out_specs=(spec,) * 4,
        check_vma=False,
    )
```

```python
import functools
import jax
import jax.numpy as jnp
from jax import lax
from jax.experimental import pallas as pl
from jax.experimental.pallas import tpu as pltpu
from jax.sharding import PartitionSpec as P

RADIUS = 4
SWEEPS = 3
NEWTON = 8

k_void = 0.03
k_frame = 160.0
k_glass = 1.0
k_anchor = 50.0
loss_rate = 0.05
spectrum_low = 0.05
spectrum_high = 2.0
solid_allowance = 0.35
curve_floor = 0.05
move_limit = 0.2
gamma_slope = 200.0

LANES = 128
STRIP = 16
above_weight = 1.001 + 1e-05
below_weight = 0.001 + 1e-05

f32 = jnp.float32
AXES = ("thick", "facade")
BOTH_SIDES = 16


def call(kernel, outs, args, scratch=()):
    vmem = pl.BlockSpec(memory_space=pltpu.VMEM)
    return pl.pallas_call(
        kernel,
        out_shape=[jax.ShapeDtypeStruct(shape, f32) for shape in outs],
        in_specs=[vmem] * len(args),
        out_specs=[vmem] * len(outs),
        scratch_shapes=[pltpu.VMEM(shape, f32) for shape in scratch],
        compiler_params=pltpu.CompilerParams(vmem_limit_bytes=40 * 1024 * 1024),
    )(*args)


def lane_iota(shape):
    return lax.broadcasted_iota(jnp.int32, shape, len(shape) - 1)


def sub_iota(shape):
    return lax.broadcasted_iota(jnp.int32, shape, len(shape) - 2)


def ahead(value, step, axis):
    return pltpu.roll(value, (value.shape[axis] - step) % value.shape[axis], axis)


def behind(value, step, axis):
    return pltpu.roll(value, step, axis)


def launch_kernel(*refs):
    firsts, lasts, nears, fars = refs[0:5], refs[5:10], refs[10:13], refs[13:16]
    to_left, to_right, rows_up, rows_down = refs[16:]
    rows, height, _ = to_left.shape
    group = lane_iota((height, LANES)) // STRIP
    for row in range(rows):
        for source, target, place in ((firsts, to_left, 0), (lasts, to_right, LANES - STRIP)):
            packed = jnp.zeros((height, LANES), f32)
            for index, ref in enumerate(source):
                value = ref[row]
                if value.dtype != f32:
                    value = value.astype(f32) + 1.0
                shift = (STRIP * index - place) % LANES
                if shift:
                    value = pltpu.roll(value, shift, 1)
                packed = jnp.where(group == index, value, packed)
            target[row] = packed
    start = 0
    for near, far, count in zip(nears, fars, (4, 3, 1)):
        for r in range(count):
            rows_down[start + r] = near[r]
            rows_up[start + r] = far[far.shape[0] - count + r]
        start += count


def halo_lanes(left, right, index):
    lane = lane_iota(left.shape)
    shift = (LANES - STRIP * index) % LANES
    after = pltpu.roll(right, shift, 1) if shift else right
    shift = (LANES - STRIP - STRIP * index) % LANES
    before = pltpu.roll(left, shift, 1) if shift else left
    return jnp.where(lane < STRIP, after, jnp.where(lane >= LANES - STRIP, before, 0.0))


def axis_weight(position, total):
    acc = jnp.zeros(position.shape, f32)
    for offset in range(-RADIUS, RADIUS + 1):
        weight = float(RADIUS + 1 - abs(offset))
        inside = (position + offset >= 0) & (position + offset < total)
        acc = acc + jnp.where(inside, weight, 0.0)
    return jnp.maximum(acc, 1.0)


def inverse_plane(height, own, cols_total, col_start):
    width = own + LANES
    lane = lane_iota((1, width))
    place = jnp.where(lane < own + LANES // 2, lane, lane - width) + col_start
    middle = axis_weight(sub_iota((height, 1)), height)
    return 1.0 / (middle * axis_weight(place, cols_total))


def row_weight(row, rows_total, row_start):
    return 1.0 / axis_weight(jnp.full((1, 1), row + row_start, jnp.int32), rows_total)


def filter_height(value):
    height = value.shape[0]
    level = sub_iota((height, 1))
    total = float(RADIUS + 1) * value
    for offset in range(1, RADIUS + 1):
        weight = float(RADIUS + 1 - offset)
        up = jnp.where(level < height - offset, weight, 0.0)
        down = jnp.where(level >= offset, weight, 0.0)
        total = total + up * ahead(value, offset, 0) + down * behind(value, offset, 0)
    return total


def filter_lanes(value):
    def box(v):
        pair = v + ahead(v, 1, 1)
        return pair + ahead(pair, 2, 1) + behind(v, 1, 1)

    def box_back(v):
        pair = v + behind(v, 1, 1)
        return pair + behind(pair, 2, 1) + ahead(v, 1, 1)

    return box_back(box(value))


def depth_filter(source, middle, target):
    count = source.shape[0]
    for r in range(count - 4):
        middle[r] = (source[r] + source[r + 1]) + (source[r + 2] + source[r + 3]) + source[r + 4]
    for r in range(count - 8):
        target[r] = (middle[r] + middle[r + 1]) + (middle[r + 2] + middle[r + 3]) + middle[r + 4]


def present(place, rows, own, rows_total, cols_total):
    row_start, col_start = place

    def flag(condition):
        return jnp.where(condition, 1.0, 0.0).astype(f32)

    return (
        flag(row_start > 0), flag(row_start + rows < rows_total),
        flag(col_start > 0), flag(col_start + own < cols_total),
    )


def corner(message, row):
    lanes = slice(row * LANES, (row + 1) * LANES)
    return message[4, :, lanes], message[5, :, lanes]


def rho_kernel(
    rows_total, cols_total, place,
    density, material, density_above, density_below, left, right,
    rho_out, cond_first, cond_last,
    ext, middle, summed,
):
    rows, height, own = density.shape
    has_above, has_below, has_left, has_right = present(place, rows, own, rows_total, cols_total)

    def halo(strips, index):
        return halo_lanes(strips[0] * has_left, strips[1] * has_right, index)

    for r in range(4):
        ext[r, :, :own] = density_above[r] * has_above
        ext[r, :, own:] = halo(corner(density_above, r), 0) * has_above
        ext[rows + 4 + r, :, :own] = density_below[r] * has_below
        ext[rows + 4 + r, :, own:] = halo(corner(density_below, r), 0) * has_below
    for r in range(rows):
        ext[4 + r, :, :own] = density[r]
        ext[4 + r, :, own:] = halo((left[r], right[r]), 0)
    depth_filter(ext, middle, summed)
    plane = inverse_plane(height, own, cols_total, place[1])
    for r in range(rows):
        rho = filter_lanes(filter_height(summed[r])) * (
            plane * row_weight(r, rows_total, place[0])
        )
        code = jnp.concatenate(
            [material[r].astype(f32) + 1.0, halo((left[r], right[r]), 1)], axis=1
        )
        frame = k_void + (k_frame - k_void) * rho * rho * rho
        cond = jnp.where(code == 2.0, frame, jnp.where(code == 1.0, k_glass, k_anchor))
        cond = jnp.where(code == 0.0, 0.0, cond)
        rho_out[r] = rho
        if r < 4:
            cond_first[r] = cond
        else:
            cond_last[r - 4] = cond


centre_value = 0.5 * (spectrum_high + spectrum_low)
half_width = 0.5 * (spectrum_high - spectrum_low)
ratio_value = centre_value / half_width
INNER = range(5, 11)


class Rows:
    def __init__(self, ready, first, stop, rest):
        self.ready, self.first, self.stop, self.rest = ready, first, stop, rest

    def __getitem__(self, row):
        if self.first <= row < self.stop:
            return self.ready[row - self.first]
        return self.rest[row]


def face(one, other, store=None):
    inv = 1.0 / jnp.maximum(one + other, 1e-3)
    part = one * inv
    if store is not None:
        here, there, row = store
        rest = other * inv
        there[row] = part * part
        here[row] = rest * rest
    return 2.0 * part * other


def first_residual(value, before, after, load, deep_before, deep, tall, wide):
    inverse = 1.0 / (
        loss_rate + (deep + deep_before) + (tall + behind(tall, 1, 0)) + (wide + behind(wide, 1, 1))
    )
    left_over = load - operate(value, deep_before * (before - value), deep * (value - after), tall, wide)
    direction = left_over * inverse * (1.0 / centre_value)
    return inverse, left_over, direction


def operate(value, flux_before, flux, tall, wide):
    high = tall * (value - ahead(value, 1, 0))
    along = wide * (value - ahead(value, 1, 1))
    return (
        loss_rate * value + (flux - flux_before) + (high - behind(high, 1, 0))
        + (along - behind(along, 1, 1))
    )


def prepare_kernel(
    cond_first, cond_last, prior, source, temp,
    from_above, from_below, density_above, density_below, left, right,
    field, load, heat, depth_face, height_face, lane_face,
    depth_here, depth_there, height_here, height_there, lane_here, lane_there,
    inverse, residual, direction, dual,
):
    rows, height, own = prior.shape
    last_level = sub_iota((height, 1)) == height - 1

    def place_row(target, row, main, strips, index):
        target[row, :, :own] = main
        target[row, :, own:] = halo_lanes(strips[0], strips[1], index)

    for r in range(4):
        place_row(field, r, from_above[r], corner(density_above, r), 3)
        place_row(field, 12 + r, from_below[r], corner(density_below, r), 3)
    for r in range(3):
        place_row(load, 1 + r, from_above[4 + r], corner(density_above, 1 + r), 2)
        place_row(load, 12 + r, from_below[4 + r], corner(density_below, r), 2)
    load[0] = jnp.zeros(load.shape[1:], f32)
    load[15] = jnp.zeros(load.shape[1:], f32)
    place_row(heat, 0, from_above[7], corner(density_above, 3), 4)
    place_row(heat, 9, from_below[7], corner(density_below, 0), 4)
    for r in range(rows):
        strips = (left[r], right[r])
        place_row(field, 4 + r, prior[r], strips, 3)
        place_row(load, 4 + r, source[r], strips, 2)
        place_row(heat, 1 + r, temp[r], strips, 4)

    deep_before = None
    following = cond_first[0]
    for r in range(4, 12):
        i = r - 4
        here = following
        tall = jnp.where(
            last_level, 0.0, face(here, ahead(here, 1, 0), (height_here, height_there, i))
        )
        wide = face(here, ahead(here, 1, 1), (lane_here, lane_there, i))
        height_face[i] = tall
        lane_face[i] = wide
        if r < 11:
            following = cond_first[i + 1] if i < 3 else cond_last[i - 3]
            deep = face(here, following, (depth_here, depth_there, i))
            depth_face[i] = deep
        if r in INNER:
            value = field[r]
            one, two, three = first_residual(
                value, field[r - 1], field[r + 1], load[r], deep_before, deep, tall, wide
            )
            k = r - INNER.start
            inverse[k], residual[k], direction[k] = one, two, three
            dual[k] = value + three
        deep_before = deep


def sweep_kernel(
    rows_total, cols_total, place,
    cond_above, cond_first, cond_last, cond_below, rho, material,
    field, load, heat, own_depth_face, own_height_face, own_lane_face,
    own_depth_here, own_depth_there, height_here, height_there, lane_here, lane_there,
    own_inverse, own_residual, own_direction, own_dual, left, right, tallies,
    dual_out, weighted_first, weighted_last,
    depth_face, height_face, lane_face, inverse, residual, first_direction, next_direction, dual,
    edge_here, edge_there,
):
    rows, height, own = rho.shape[0], rho.shape[1], dual_out.shape[2]
    has_above, has_below, has_left, has_right = present(place, rows, own, rows_total, cols_total)
    last_level = sub_iota((height, 1)) == height - 1

    def cond(r):
        if r < 4:
            return cond_above[r] * has_above
        if r >= 12:
            return cond_below[r - 12] * has_below
        return cond_first[r - 4] if r < 8 else cond_last[r - 8]

    depth_faces = Rows(own_depth_face, 4, 11, depth_face)
    height_faces = Rows(own_height_face, 4, 12, height_face)
    lane_faces = Rows(own_lane_face, 4, 12, lane_face)
    inverses = Rows(own_inverse, INNER.start, INNER.stop, inverse)
    residuals = Rows(own_residual, INNER.start, INNER.stop, residual)
    directions = Rows(own_direction, INNER.start, INNER.stop, first_direction)
    duals = Rows(own_dual, INNER.start, INNER.stop, dual)

    following = cond(0)
    for r in range(15):
        if 4 <= r < 11:
            following = None
            continue
        here = cond(r) if following is None else following
        following = cond(r + 1)
        store = (edge_here, edge_there, 0 if r == 3 else 1) if r in (3, 11) else None
        depth_face[r] = face(here, following, store)
        if r in (1, 2, 3, 12, 13, 14):
            height_face[r] = jnp.where(last_level, 0.0, face(here, ahead(here, 1, 0)))
            lane_face[r] = face(here, ahead(here, 1, 1))
    for r in range(1, 15):
        if r in INNER:
            continue
        value = field[r]
        one, two, three = first_residual(
            value, field[r - 1], field[r + 1], load[r],
            depth_faces[r - 1], depth_faces[r], height_faces[r], lane_faces[r],
        )
        inverse[r], residual[r], first_direction[r] = one, two, three
        if 3 <= r < 13:
            dual[r] = value + three

    factor = 1.0 / ratio_value
    now = directions
    for sweep in range(SWEEPS - 1):
        factor_next = 1.0 / (2.0 * ratio_value - factor)
        keep, add = factor_next * factor, 2.0 * factor_next / half_width
        start, stop = 2 + sweep, 14 - sweep
        following = now[start]
        flux_before = depth_faces[start - 1] * (now[start - 1] - following)
        for r in range(start, stop):
            value, following = following, now[r + 1]
            flux = depth_faces[r] * (value - following)
            left_over = residuals[r] - operate(
                value, flux_before, flux, height_faces[r], lane_faces[r]
            )
            direction = keep * value + add * (left_over * inverses[r])
            if sweep < SWEEPS - 2:
                residual[r] = left_over
                next_direction[r] = direction
            if 3 <= r < 13:
                dual[r] = duals[r] + direction
            flux_before = flux
        factor = factor_next
        now, residuals, duals = next_direction, residual, dual

    depth_here = Rows(own_depth_here, 4, 11, {11: edge_here[1]})
    depth_there = Rows(own_depth_there, 4, 11, {3: edge_there[0], 11: edge_there[1]})
    plane = inverse_plane(height, own, cols_total, place[1])
    for r in range(rows):
        dual_out[r] = dual[4 + r, :, :own]
    a, t = dual[3], heat[0]
    a_next, t_next = dual[4], heat[1]
    deep_before = (a - a_next) * (t - t_next) * depth_there[3]
    for r in range(4, 4 + rows):
        row = r - 4
        a, t = a_next, t_next
        a_next, t_next = dual[r + 1], heat[r - 2]
        deep = (a - a_next) * (t - t_next)
        tall = (a - ahead(a, 1, 0)) * (t - ahead(t, 1, 0))
        tall = jnp.where(last_level, 0.0, tall)
        wide = (a - ahead(a, 1, 1)) * (t - ahead(t, 1, 1))
        total = (
            (deep * depth_here[r] + deep_before)
            + (tall * height_here[row] + behind(tall * height_there[row], 1, 0))
            + (wide * lane_here[row] + behind(wide * lane_there[row], 1, 1))
        )
        deep_before = deep * depth_there[r]
        strips = halo_lanes(left[row] * has_left, right[row] * has_right, 1)
        code = jnp.concatenate([material[row].astype(f32) + 1.0, strips], axis=1)
        thick_rho = rho[row]
        value = total * (thick_rho * thick_rho) * (
            plane * (row_weight(row, rows_total, place[0]) * (-6.0 * (k_frame - k_void)))
        )
        value = jnp.where(code == 2.0, value, 0.0)
        if row < 4:
            weighted_first[row] = value
        else:
            weighted_last[row - 4] = value


def grad_kernel(
    rows_total, cols_total, place,
    from_above, first, last, from_below, material, grad_out, message, ext, middle, summed,
):
    rows, height, own = grad_out.shape
    has_above, has_below, _, _ = present(place, rows, own, rows_total, cols_total)
    for r in range(4):
        ext[r] = from_above[r] * has_above
        ext[4 + r] = first[r]
        ext[8 + r] = last[r]
        ext[12 + r] = from_below[r] * has_below
    depth_filter(ext, middle, summed)
    largest = jnp.zeros((height, LANES), f32)
    for r in range(rows):
        grad = filter_lanes(filter_height(summed[r]))[:, :own]
        grad_out[r] = grad
        size = jnp.where(material[r] == 1, jnp.abs(grad), 0.0)
        for block in range(own // LANES):
            largest = jnp.maximum(largest, size[:, block * LANES:(block + 1) * LANES])
    message[...] = jnp.broadcast_to(jnp.max(largest, axis=0, keepdims=True), message.shape)


def lines_kernel(
    solid, newer, older, below_spacing, above_spacing, material,
    below_out, above_out, up_out, low_out, least_out, most_out, upper_out, lower_out, bend_out,
    tallies,
):
    rows, height, own = solid.shape
    base = jnp.zeros((height, LANES), f32)
    count = jnp.zeros((height, LANES), f32)
    for r in range(rows):
        x = solid[r]
        design = material[r] == 1
        gamma = 0.95 + 0.25 * jnp.tanh(gamma_slope * newer[r] * older[r])
        below = x - gamma * below_spacing[r]
        above = x + gamma * above_spacing[r]
        below_out[r] = below
        above_out[r] = above
        up = above - x
        low = x - below
        floor = jnp.maximum(jnp.maximum(0.0, below + 0.1 * low), x - move_limit)
        ceiling = jnp.minimum(jnp.minimum(1.0, above - 0.1 * up), x + move_limit)
        up_out[r] = up
        low_out[r] = low
        least_out[r] = floor - below
        most_out[r] = ceiling - below
        upper_out[r] = jnp.where(design, above_weight * up * up, 0.0)
        lower_out[r] = jnp.where(design, below_weight * low * low, 0.0)
        bend_out[r] = jnp.where(design, up * low / (2.0 * (up + low)), 0.0)
        term = jnp.where(
            design, x - solid_allowance - above_weight * up - below_weight * low, 0.0
        )
        one = jnp.where(design, curve_floor, 0.0)
        for block in range(own // LANES):
            base = base + term[:, block * LANES:(block + 1) * LANES]
            count = count + one[:, block * LANES:(block + 1) * LANES]
    tallies[0] = base
    tallies[1] = count


def reached(rate_above, rate_below, y, up, low, least, most):
    root_above = rate_above + y * above_weight
    root_below = rate_below + y * below_weight
    inv_above, inv_below = lax.rsqrt(root_above), lax.rsqrt(root_below)
    root_above, root_below = root_above * inv_above, root_below * inv_below
    width = up + low
    pull = low * root_below
    trial = width * pull / (up * root_above + pull)
    return trial, jnp.clip(trial, least, most), width, root_above, root_below, inv_above, inv_below


def sums_to_message(slope, curve, message):
    slope = jnp.sum(slope, axis=0, keepdims=True)
    curve = jnp.sum(curve, axis=0, keepdims=True)
    slope = slope + pltpu.roll(slope, LANES // 2, 1)
    curve = curve + pltpu.roll(curve, LANES // 2, 1)
    lane = lane_iota((1, LANES))
    message[...] = jnp.broadcast_to(jnp.where(lane < LANES // 2, slope, curve), message.shape)


def evaluate(y, rate_above, rate_below, up, low, least, most, upper, lower, bend, tallies, message):
    rows, height, own = up.shape
    slope_sum, curve_sum = tallies[0], tallies[1]
    for r in range(rows):
        trial, chosen, width, root_above, root_below, inv_above, inv_below = reached(
            rate_above(r), rate_below(r), y, up[r], low[r], least[r], most[r]
        )
        rest = width - chosen
        slope = (upper[r] * chosen + lower[r] * rest) / (rest * chosen)
        split = above_weight * (inv_above * inv_above) - below_weight * (inv_below * inv_below)
        curve = bend[r] * (root_above * root_below) * (split * split)
        free = (trial > least[r]) & (trial < most[r])
        curve = jnp.where(free, curve, 0.0)
        for block in range(own // LANES):
            slope_sum = slope_sum + slope[:, block * LANES:(block + 1) * LANES]
            curve_sum = curve_sum + curve[:, block * LANES:(block + 1) * LANES]
    sums_to_message(slope_sum, curve_sum, message)


def first_kernel(
    arrived, grad, up, low, least, most, upper, lower, bend, tallies,
    message, rate_above_out, rate_below_out,
):
    scale = jnp.max(jnp.max(arrived[...], axis=0, keepdims=True), axis=1, keepdims=True)
    inverse = 1.0 / (scale + 1e-06)

    def above(r):
        element = grad[r] * inverse
        value = jnp.maximum(1.001 * element, -0.001 * element) + 1e-05
        rate_above_out[r] = value
        return value

    def below(r):
        element = grad[r] * inverse
        value = jnp.maximum(0.001 * element, -1.001 * element) + 1e-05
        rate_below_out[r] = value
        return value

    evaluate(
        jnp.ones((1, 1), f32), above, below, up, low, least, most, upper, lower, bend, tallies, message
    )


def advance(arrived, y):
    total = jnp.sum(arrived[...], axis=0, keepdims=True)
    lane = lane_iota(total.shape)
    slope = jnp.sum(jnp.where(lane < LANES // 2, total, 0.0), axis=1, keepdims=True)
    curve = jnp.sum(jnp.where(lane < LANES // 2, 0.0, total), axis=1, keepdims=True)
    return jnp.maximum(0.0, y + slope / curve)


def step_kernel(
    arrived, y_ref, rate_above, rate_below, up, low, least, most, upper, lower, bend, tallies,
    message, y_out,
):
    y = advance(arrived, y_ref[0:1, 0:1])
    y_out[...] = jnp.broadcast_to(y, y_out.shape)
    evaluate(
        y, lambda r: rate_above[r], lambda r: rate_below[r],
        up, low, least, most, upper, lower, bend, tallies, message,
    )


def last_kernel(
    arrived, y_ref, rate_above, rate_below, up, low, least, most, below, solid, material, out
):
    y = advance(arrived, y_ref[0:1, 0:1])
    for r in range(out.shape[0]):
        chosen = reached(rate_above[r], rate_below[r], y, up[r], low[r], least[r], most[r])[1]
        out[r] = jnp.where(material[r] == 1, below[r] + chosen, solid[r])


def with_place(kernel, rows_total, cols_total):
    def body(place_ref, *refs):
        kernel(rows_total, cols_total, (place_ref[0], place_ref[1]), *refs)

    return body


def placed_call(kernel, place, outs, args, scratch, totals):
    vmem = pl.BlockSpec(memory_space=pltpu.VMEM)
    return pl.pallas_call(
        with_place(kernel, *totals),
        out_shape=[jax.ShapeDtypeStruct(shape, f32) for shape in outs],
        in_specs=[pl.BlockSpec(memory_space=pltpu.SMEM)] + [vmem] * len(args),
        out_specs=[vmem] * len(outs),
        scratch_shapes=[pltpu.VMEM(shape, f32) for shape in scratch],
        compiler_params=pltpu.CompilerParams(vmem_limit_bytes=40 * 1024 * 1024),
    )(place, *args)


def launch_messages(density, material, source, prior, temp):
    rows, height, own = density.shape
    end = own // LANES - 1
    block, message = (rows, height, LANES), (8, height, own)
    first = pl.BlockSpec(block, lambda i: (0, 0, 0))
    last = pl.BlockSpec(block, lambda i: (0, 0, end))

    def layers(count, index):
        return pl.BlockSpec((count, height, own), lambda i: (index, 0, 0))

    strips = (density, material, source, prior, temp)
    layered = (prior, source, temp)
    return pl.pallas_call(
        launch_kernel,
        grid=(1,),
        out_shape=[jax.ShapeDtypeStruct(s, f32) for s in (block, block, message, message)],
        in_specs=[first] * 5 + [last] * 5
        + [layers(4, 0)] * 2 + [layers(1, 0)] + [layers(4, rows // 4 - 1)] * 2 + [layers(1, rows - 1)],
        out_specs=[pl.BlockSpec(s, lambda i: (0, 0, 0)) for s in (block, block, message, message)],
    )(*strips, *strips, *layered, *layered)


def on_device(
    solid_occupancy,
    newer_occupancy_shift,
    older_occupancy_shift,
    below_limit_spacing,
    above_limit_spacing,
    thermal_state,
    loss_state_derivative,
    prior_dual_state,
    cell_material,
):
    rows, height, own = solid_occupancy.shape
    deep, long = lax.axis_size("thick"), lax.axis_size("facade")
    totals = (rows * deep, own * long)
    place = jnp.stack(
        [lax.axis_index("thick") * rows, lax.axis_index("facade") * own]
    ).astype(jnp.int32)
    width = own + LANES
    whole = (rows, height, own)

    def turn(axis, size, step):
        pairs = [(i, (i + step) % size) for i in range(size)]
        return lambda value: lax.ppermute(value, axis, pairs)

    to_right, to_left = turn("facade", long, 1), turn("facade", long, -1)
    to_deeper, to_nearer = turn("thick", deep, 1), turn("thick", deep, -1)

    first_strips, last_strips, rows_up, rows_down = launch_messages(
        solid_occupancy, cell_material, loss_state_derivative, prior_dual_state, thermal_state
    )
    right, left = to_left(first_strips), to_right(last_strips)

    def side_by_side(strips, start):
        return jnp.concatenate([strips[start + r] for r in range(4)], axis=1)[None]

    def density_message(start):
        return jnp.concatenate(
            [
                solid_occupancy[start:start + 4],
                side_by_side(left, start), side_by_side(right, start),
            ]
        )

    density_up, density_down, rows_up, rows_down = lax.optimization_barrier(
        (density_message(rows - 4), density_message(0), rows_up, rows_down)
    )
    density_above, density_below = to_deeper(density_up), to_nearer(density_down)
    from_above, from_below = to_deeper(rows_up), to_nearer(rows_down)

    (below, above, up, low, least, most, upper, lower, bend, tallies) = call(
        lines_kernel,
        [whole] * 9 + [(2, height, LANES)],
        (
            solid_occupancy, newer_occupancy_shift, older_occupancy_shift,
            below_limit_spacing, above_limit_spacing, cell_material,
        ),
    )

    four = (4, height, width)
    rho, cond_first, cond_last = placed_call(
        rho_kernel, place,
        [(rows, height, width), four, four],
        (
            solid_occupancy, cell_material, density_above, density_below, left, right,
        ),
        [(BOTH_SIDES, height, width), (BOTH_SIDES - 4, height, width), (rows, height, width)],
        totals,
    )
    cond_above, cond_below = to_deeper(cond_last), to_nearer(cond_first)
    tall, own_wide, inner = (
        (BOTH_SIDES, height, width), (rows, height, width), (len(INNER), height, width),
    )
    prepared = call(
        prepare_kernel,
        [tall, tall, (rows + 2, height, width)] + [own_wide] * 9 + [inner] * 4,
        (
            cond_first, cond_last, prior_dual_state, loss_state_derivative, thermal_state,
            from_above, from_below, density_above, density_below, left, right,
        ),
    )
    dual_state, weighted_first, weighted_last = placed_call(
        sweep_kernel, place,
        [whole, four, four],
        (
            cond_above, cond_first, cond_last, cond_below, rho, cell_material, *prepared,
            left, right, tallies,
        ),
        [tall] * 8 + [(2, height, width)] * 2,
        totals,
    )
    weighted_above, weighted_below = to_deeper(weighted_last), to_nearer(weighted_first)
    count = deep * long
    note = (count, LANES)
    grad, message = placed_call(
        grad_kernel, place,
        [whole, note],
        (weighted_above, weighted_first, weighted_last, weighted_below, cell_material),
        [tall, (BOTH_SIDES - 4, height, width), (rows, height, width)],
        totals,
    )

    def everyone(rows_out):
        return lax.all_to_all(rows_out, AXES, 0, 0, tiled=True)

    fixed = (up, low, least, most, upper, lower, bend, tallies)
    message, rate_above, rate_below = call(
        first_kernel, [note, whole, whole], (everyone(message), grad) + fixed
    )
    y = jnp.ones((8, LANES), f32)
    for _ in range(NEWTON - 1):
        message, y = call(
            step_kernel, [note, (8, LANES)],
            (everyone(message), y, rate_above, rate_below) + fixed,
        )
    (density_new,) = call(
        last_kernel, [whole],
        (
            everyone(message), y, rate_above, rate_below, up, low, least, most, below,
            solid_occupancy, cell_material,
        ),
    )
    return (density_new, below, above, dual_state)


def solution(mesh):
    spec = P("thick", None, "facade")
    return jax.shard_map(
        on_device,
        mesh=mesh,
        in_specs=(spec,) * 9,
        out_specs=(spec,) * 4,
        check_vma=False,
    )
```

```python
import functools
import jax
import jax.numpy as jnp
from jax import lax
from jax.experimental import pallas as pl
from jax.experimental.pallas import tpu as pltpu
from jax.sharding import PartitionSpec as P

RADIUS = 4
SWEEPS = 3
NEWTON = 8

k_void = 0.03
k_frame = 160.0
k_glass = 1.0
k_anchor = 50.0
loss_rate = 0.05
spectrum_low = 0.05
spectrum_high = 2.0
solid_allowance = 0.35
curve_floor = 0.05
move_limit = 0.2
gamma_slope = 200.0

LANES = 128
STRIP = 16
above_weight = 1.001 + 1e-05
below_weight = 0.001 + 1e-05

f32 = jnp.float32
AXES = ("thick", "facade")
BOTH_SIDES = 16


def call(kernel, outs, args, scratch=()):
    vmem = pl.BlockSpec(memory_space=pltpu.VMEM)
    return pl.pallas_call(
        kernel,
        out_shape=[jax.ShapeDtypeStruct(shape, f32) for shape in outs],
        in_specs=[vmem] * len(args),
        out_specs=[vmem] * len(outs),
        scratch_shapes=[pltpu.VMEM(shape, f32) for shape in scratch],
        compiler_params=pltpu.CompilerParams(vmem_limit_bytes=40 * 1024 * 1024),
    )(*args)


def lane_iota(shape):
    return lax.broadcasted_iota(jnp.int32, shape, len(shape) - 1)


def sub_iota(shape):
    return lax.broadcasted_iota(jnp.int32, shape, len(shape) - 2)


def ahead(value, step, axis):
    return pltpu.roll(value, (value.shape[axis] - step) % value.shape[axis], axis)


def behind(value, step, axis):
    return pltpu.roll(value, step, axis)


def launch_kernel(*refs):
    firsts, lasts, nears, fars = refs[0:5], refs[5:10], refs[10:13], refs[13:16]
    to_left, to_right, rows_up, rows_down = refs[16:]
    rows, height, _ = to_left.shape
    group = lane_iota((height, LANES)) // STRIP
    for row in range(rows):
        for source, target, place in ((firsts, to_left, 0), (lasts, to_right, LANES - STRIP)):
            packed = jnp.zeros((height, LANES), f32)
            for index, ref in enumerate(source):
                value = ref[row]
                if value.dtype != f32:
                    value = value.astype(f32) + 1.0
                shift = (STRIP * index - place) % LANES
                if shift:
                    value = pltpu.roll(value, shift, 1)
                packed = jnp.where(group == index, value, packed)
            target[row] = packed
    start = 0
    for near, far, count in zip(nears, fars, (4, 3, 1)):
        for r in range(count):
            rows_down[start + r] = near[r]
            rows_up[start + r] = far[far.shape[0] - count + r]
        start += count


def halo_lanes(left, right, index):
    lane = lane_iota(left.shape)
    shift = (LANES - STRIP * index) % LANES
    after = pltpu.roll(right, shift, 1) if shift else right
    shift = (LANES - STRIP - STRIP * index) % LANES
    before = pltpu.roll(left, shift, 1) if shift else left
    return jnp.where(lane < STRIP, after, jnp.where(lane >= LANES - STRIP, before, 0.0))


def axis_weight(position, total):
    acc = jnp.zeros(position.shape, f32)
    for offset in range(-RADIUS, RADIUS + 1):
        weight = float(RADIUS + 1 - abs(offset))
        inside = (position + offset >= 0) & (position + offset < total)
        acc = acc + jnp.where(inside, weight, 0.0)
    return jnp.maximum(acc, 1.0)


def inverse_plane(height, own, cols_total, col_start):
    width = own + LANES
    lane = lane_iota((1, width))
    place = jnp.where(lane < own + LANES // 2, lane, lane - width) + col_start
    middle = axis_weight(sub_iota((height, 1)), height)
    return 1.0 / (middle * axis_weight(place, cols_total))


def row_weight(row, rows_total, row_start):
    return 1.0 / axis_weight(jnp.full((1, 1), row + row_start, jnp.int32), rows_total)


def filter_height(value):
    height = value.shape[0]
    level = sub_iota((height, 1))
    total = float(RADIUS + 1) * value
    for offset in range(1, RADIUS + 1):
        weight = float(RADIUS + 1 - offset)
        up = jnp.where(level < height - offset, weight, 0.0)
        down = jnp.where(level >= offset, weight, 0.0)
        total = total + up * ahead(value, offset, 0) + down * behind(value, offset, 0)
    return total


def filter_lanes(value):
    def box(v):
        pair = v + ahead(v, 1, 1)
        return pair + ahead(pair, 2, 1) + behind(v, 1, 1)

    def box_back(v):
        pair = v + behind(v, 1, 1)
        return pair + behind(pair, 2, 1) + ahead(v, 1, 1)

    return box_back(box(value))


def depth_filter(source, middle, target):
    count = source.shape[0]
    for r in range(count - 4):
        middle[r] = (source[r] + source[r + 1]) + (source[r + 2] + source[r + 3]) + source[r + 4]
    for r in range(count - 8):
        target[r] = (middle[r] + middle[r + 1]) + (middle[r + 2] + middle[r + 3]) + middle[r + 4]


def present(place, rows, own, rows_total, cols_total):
    row_start, col_start = place

    def flag(condition):
        return jnp.where(condition, 1.0, 0.0).astype(f32)

    return (
        flag(row_start > 0), flag(row_start + rows < rows_total),
        flag(col_start > 0), flag(col_start + own < cols_total),
    )


def corner(message, row):
    lanes = slice(row * LANES, (row + 1) * LANES)
    return message[4, :, lanes], message[5, :, lanes]


def rho_kernel(
    rows_total, cols_total, place,
    density, material, density_above, density_below, left, right,
    rho_out, cond_first, cond_last,
    ext, middle, summed,
):
    rows, height, own = density.shape
    has_above, has_below, has_left, has_right = present(place, rows, own, rows_total, cols_total)

    def halo(strips, index):
        return halo_lanes(strips[0] * has_left, strips[1] * has_right, index)

    for r in range(4):
        ext[r, :, :own] = density_above[r] * has_above
        ext[r, :, own:] = halo(corner(density_above, r), 0) * has_above
        ext[rows + 4 + r, :, :own] = density_below[r] * has_below
        ext[rows + 4 + r, :, own:] = halo(corner(density_below, r), 0) * has_below
    for r in range(rows):
        ext[4 + r, :, :own] = density[r]
        ext[4 + r, :, own:] = halo((left[r], right[r]), 0)
    depth_filter(ext, middle, summed)
    plane = inverse_plane(height, own, cols_total, place[1])
    for r in range(rows):
        rho = filter_lanes(filter_height(summed[r])) * (
            plane * row_weight(r, rows_total, place[0])
        )
        code = jnp.concatenate(
            [material[r].astype(f32) + 1.0, halo((left[r], right[r]), 1)], axis=1
        )
        frame = k_void + (k_frame - k_void) * rho * rho * rho
        cond = jnp.where(code == 2.0, frame, jnp.where(code == 1.0, k_glass, k_anchor))
        cond = jnp.where(code == 0.0, 0.0, cond)
        rho_out[r] = rho
        if r < 4:
            cond_first[r] = cond
        else:
            cond_last[r - 4] = cond


centre_value = 0.5 * (spectrum_high + spectrum_low)
half_width = 0.5 * (spectrum_high - spectrum_low)
ratio_value = centre_value / half_width
INNER = range(5, 11)


class Rows:
    def __init__(self, ready, first, stop, rest):
        self.ready, self.first, self.stop, self.rest = ready, first, stop, rest

    def __getitem__(self, row):
        if self.first <= row < self.stop:
            return self.ready[row - self.first]
        return self.rest[row]


def face(one, other, store=None):
    inv = 1.0 / jnp.maximum(one + other, 1e-3)
    part = one * inv
    if store is not None:
        here, there, row = store
        rest = other * inv
        there[row] = part * part
        here[row] = rest * rest
    return 2.0 * part * other


def first_residual(value, before, after, load, deep_before, deep, tall, wide):
    inverse = 1.0 / (
        loss_rate + (deep + deep_before) + (tall + behind(tall, 1, 0)) + (wide + behind(wide, 1, 1))
    )
    left_over = load - operate(value, deep_before * (before - value), deep * (value - after), tall, wide)
    direction = left_over * inverse * (1.0 / centre_value)
    return inverse, left_over, direction


def operate(value, flux_before, flux, tall, wide):
    high = tall * (value - ahead(value, 1, 0))
    along = wide * (value - ahead(value, 1, 1))
    return (
        loss_rate * value + (flux - flux_before) + (high - behind(high, 1, 0))
        + (along - behind(along, 1, 1))
    )


def prepare_kernel(
    cond_first, cond_last, prior, source, temp,
    from_above, from_below, density_above, density_below, left, right,
    field, load, heat, depth_face, height_face, lane_face,
    depth_here, depth_there, height_here, height_there, lane_here, lane_there,
    inverse, residual, direction, dual,
):
    rows, height, own = prior.shape
    last_level = sub_iota((height, 1)) == height - 1

    def place_row(target, row, main, strips, index):
        target[row, :, :own] = main
        target[row, :, own:] = halo_lanes(strips[0], strips[1], index)

    for r in range(4):
        place_row(field, r, from_above[r], corner(density_above, r), 3)
        place_row(field, 12 + r, from_below[r], corner(density_below, r), 3)
    for r in range(3):
        place_row(load, 1 + r, from_above[4 + r], corner(density_above, 1 + r), 2)
        place_row(load, 12 + r, from_below[4 + r], corner(density_below, r), 2)
    load[0] = jnp.zeros(load.shape[1:], f32)
    load[15] = jnp.zeros(load.shape[1:], f32)
    place_row(heat, 0, from_above[7], corner(density_above, 3), 4)
    place_row(heat, 9, from_below[7], corner(density_below, 0), 4)
    for r in range(rows):
        strips = (left[r], right[r])
        place_row(field, 4 + r, prior[r], strips, 3)
        place_row(load, 4 + r, source[r], strips, 2)
        place_row(heat, 1 + r, temp[r], strips, 4)

    deep_before = None
    following = cond_first[0]
    for r in range(4, 12):
        i = r - 4
        here = following
        tall = jnp.where(
            last_level, 0.0, face(here, ahead(here, 1, 0), (height_here, height_there, i))
        )
        wide = face(here, ahead(here, 1, 1), (lane_here, lane_there, i))
        height_face[i] = tall
        lane_face[i] = wide
        if r < 11:
            following = cond_first[i + 1] if i < 3 else cond_last[i - 3]
            deep = face(here, following, (depth_here, depth_there, i))
            depth_face[i] = deep
        if r in INNER:
            value = field[r]
            one, two, three = first_residual(
                value, field[r - 1], field[r + 1], load[r], deep_before, deep, tall, wide
            )
            k = r - INNER.start
            inverse[k], residual[k], direction[k] = one, two, three
            dual[k] = value + three
        deep_before = deep


def sweep_kernel(
    rows_total, cols_total, place,
    cond_above, cond_first, cond_last, cond_below, rho, material,
    field, load, heat, own_depth_face, own_height_face, own_lane_face,
    own_depth_here, own_depth_there, height_here, height_there, lane_here, lane_there,
    own_inverse, own_residual, own_direction, own_dual, left, right, tallies,
    dual_out, weighted_first, weighted_last,
    depth_face, height_face, lane_face, inverse, residual, first_direction, next_direction, dual,
    edge_here, edge_there,
):
    rows, height, own = rho.shape[0], rho.shape[1], dual_out.shape[2]
    has_above, has_below, has_left, has_right = present(place, rows, own, rows_total, cols_total)
    last_level = sub_iota((height, 1)) == height - 1

    def cond(r):
        if r < 4:
            return cond_above[r] * has_above
        if r >= 12:
            return cond_below[r - 12] * has_below
        return cond_first[r - 4] if r < 8 else cond_last[r - 8]

    depth_faces = Rows(own_depth_face, 4, 11, depth_face)
    height_faces = Rows(own_height_face, 4, 12, height_face)
    lane_faces = Rows(own_lane_face, 4, 12, lane_face)
    inverses = Rows(own_inverse, INNER.start, INNER.stop, inverse)
    residuals = Rows(own_residual, INNER.start, INNER.stop, residual)
    directions = Rows(own_direction, INNER.start, INNER.stop, first_direction)
    duals = Rows(own_dual, INNER.start, INNER.stop, dual)

    following = cond(0)
    for r in range(15):
        if 4 <= r < 11:
            following = None
            continue
        here = cond(r) if following is None else following
        following = cond(r + 1)
        store = (edge_here, edge_there, 0 if r == 3 else 1) if r in (3, 11) else None
        depth_face[r] = face(here, following, store)
        if r in (1, 2, 3, 12, 13, 14):
            height_face[r] = jnp.where(last_level, 0.0, face(here, ahead(here, 1, 0)))
            lane_face[r] = face(here, ahead(here, 1, 1))
    for r in range(1, 15):
        if r in INNER:
            continue
        value = field[r]
        one, two, three = first_residual(
            value, field[r - 1], field[r + 1], load[r],
            depth_faces[r - 1], depth_faces[r], height_faces[r], lane_faces[r],
        )
        inverse[r], residual[r], first_direction[r] = one, two, three
        if 3 <= r < 13:
            dual[r] = value + three

    factor = 1.0 / ratio_value
    now = directions
    for sweep in range(SWEEPS - 1):
        factor_next = 1.0 / (2.0 * ratio_value - factor)
        keep, add = factor_next * factor, 2.0 * factor_next / half_width
        start, stop = 2 + sweep, 14 - sweep
        following = now[start]
        flux_before = depth_faces[start - 1] * (now[start - 1] - following)
        for r in range(start, stop):
            value, following = following, now[r + 1]
            flux = depth_faces[r] * (value - following)
            left_over = residuals[r] - operate(
                value, flux_before, flux, height_faces[r], lane_faces[r]
            )
            direction = keep * value + add * (left_over * inverses[r])
            if sweep < SWEEPS - 2:
                residual[r] = left_over
                next_direction[r] = direction
            if 3 <= r < 13:
                dual[r] = duals[r] + direction
            flux_before = flux
        factor = factor_next
        now, residuals, duals = next_direction, residual, dual

    depth_here = Rows(own_depth_here, 4, 11, {11: edge_here[1]})
    depth_there = Rows(own_depth_there, 4, 11, {3: edge_there[0], 11: edge_there[1]})
    plane = inverse_plane(height, own, cols_total, place[1])
    for r in range(rows):
        dual_out[r] = dual[4 + r, :, :own]
    a, t = dual[3], heat[0]
    a_next, t_next = dual[4], heat[1]
    deep_before = (a - a_next) * (t - t_next) * depth_there[3]
    for r in range(4, 4 + rows):
        row = r - 4
        a, t = a_next, t_next
        a_next, t_next = dual[r + 1], heat[r - 2]
        deep = (a - a_next) * (t - t_next)
        tall = (a - ahead(a, 1, 0)) * (t - ahead(t, 1, 0))
        tall = jnp.where(last_level, 0.0, tall)
        wide = (a - ahead(a, 1, 1)) * (t - ahead(t, 1, 1))
        total = (
            (deep * depth_here[r] + deep_before)
            + (tall * height_here[row] + behind(tall * height_there[row], 1, 0))
            + (wide * lane_here[row] + behind(wide * lane_there[row], 1, 1))
        )
        deep_before = deep * depth_there[r]
        strips = halo_lanes(left[row] * has_left, right[row] * has_right, 1)
        code = jnp.concatenate([material[row].astype(f32) + 1.0, strips], axis=1)
        thick_rho = rho[row]
        value = total * (thick_rho * thick_rho) * (
            plane * (row_weight(row, rows_total, place[0]) * (-6.0 * (k_frame - k_void)))
        )
        value = jnp.where(code == 2.0, value, 0.0)
        if row < 4:
            weighted_first[row] = value
        else:
            weighted_last[row - 4] = value


def grad_kernel(
    rows_total, cols_total, place,
    from_above, first, last, from_below, material, grad_out, message, ext, middle, summed,
):
    rows, height, own = grad_out.shape
    has_above, has_below, _, _ = present(place, rows, own, rows_total, cols_total)
    for r in range(4):
        ext[r] = from_above[r] * has_above
        ext[4 + r] = first[r]
        ext[8 + r] = last[r]
        ext[12 + r] = from_below[r] * has_below
    depth_filter(ext, middle, summed)
    largest = jnp.zeros((height, LANES), f32)
    for r in range(rows):
        grad = filter_lanes(filter_height(summed[r]))[:, :own]
        grad_out[r] = grad
        size = jnp.where(material[r] == 1, jnp.abs(grad), 0.0)
        for block in range(own // LANES):
            largest = jnp.maximum(largest, size[:, block * LANES:(block + 1) * LANES])
    message[...] = jnp.broadcast_to(jnp.max(largest, axis=0, keepdims=True), message.shape)


def lines_kernel(
    solid, newer, older, below_spacing, above_spacing, material,
    below_out, above_out, up_out, low_out, least_out, most_out, upper_out, lower_out, bend_out,
    tallies,
):
    rows, height, own = solid.shape
    base = jnp.zeros((height, LANES), f32)
    count = jnp.zeros((height, LANES), f32)
    for r in range(rows):
        x = solid[r]
        design = material[r] == 1
        gamma = 0.95 + 0.25 * jnp.tanh(gamma_slope * newer[r] * older[r])
        below = x - gamma * below_spacing[r]
        above = x + gamma * above_spacing[r]
        below_out[r] = below
        above_out[r] = above
        up = above - x
        low = x - below
        floor = jnp.maximum(jnp.maximum(0.0, below + 0.1 * low), x - move_limit)
        ceiling = jnp.minimum(jnp.minimum(1.0, above - 0.1 * up), x + move_limit)
        up_out[r] = up
        low_out[r] = low
        least_out[r] = floor - below
        most_out[r] = ceiling - below
        upper_out[r] = jnp.where(design, above_weight * up * up, 0.0)
        lower_out[r] = jnp.where(design, below_weight * low * low, 0.0)
        bend_out[r] = jnp.where(design, up * low / (2.0 * (up + low)), 0.0)
        term = jnp.where(
            design, x - solid_allowance - above_weight * up - below_weight * low, 0.0
        )
        one = jnp.where(design, curve_floor, 0.0)
        for block in range(own // LANES):
            base = base + term[:, block * LANES:(block + 1) * LANES]
            count = count + one[:, block * LANES:(block + 1) * LANES]
    tallies[0] = base
    tallies[1] = count


def reached(rate_above, rate_below, y, up, low, least, most):
    root_above = rate_above + y * above_weight
    root_below = rate_below + y * below_weight
    inv_above, inv_below = lax.rsqrt(root_above), lax.rsqrt(root_below)
    root_above, root_below = root_above * inv_above, root_below * inv_below
    width = up + low
    pull = low * root_below
    trial = width * pull / (up * root_above + pull)
    return trial, jnp.clip(trial, least, most), width, root_above, root_below, inv_above, inv_below


def sums_to_message(slope, curve, message):
    slope = jnp.sum(slope, axis=0, keepdims=True)
    curve = jnp.sum(curve, axis=0, keepdims=True)
    slope = slope + pltpu.roll(slope, LANES // 2, 1)
    curve = curve + pltpu.roll(curve, LANES // 2, 1)
    lane = lane_iota((1, LANES))
    message[...] = jnp.broadcast_to(jnp.where(lane < LANES // 2, slope, curve), message.shape)


def evaluate(y, rate_above, rate_below, up, low, least, most, upper, lower, bend, tallies, message):
    rows, height, own = up.shape
    slope_sum, curve_sum = tallies[0], tallies[1]
    for r in range(rows):
        trial, chosen, width, root_above, root_below, inv_above, inv_below = reached(
            rate_above(r), rate_below(r), y, up[r], low[r], least[r], most[r]
        )
        rest = width - chosen
        slope = (upper[r] * chosen + lower[r] * rest) / (rest * chosen)
        split = above_weight * (inv_above * inv_above) - below_weight * (inv_below * inv_below)
        curve = bend[r] * (root_above * root_below) * (split * split)
        free = (trial > least[r]) & (trial < most[r])
        curve = jnp.where(free, curve, 0.0)
        for block in range(own // LANES):
            slope_sum = slope_sum + slope[:, block * LANES:(block + 1) * LANES]
            curve_sum = curve_sum + curve[:, block * LANES:(block + 1) * LANES]
    sums_to_message(slope_sum, curve_sum, message)


def first_kernel(
    arrived, grad, up, low, least, most, upper, lower, bend, tallies,
    message, rate_above_out, rate_below_out,
):
    scale = jnp.max(jnp.max(arrived[...], axis=0, keepdims=True), axis=1, keepdims=True)
    inverse = 1.0 / (scale + 1e-06)

    def above(r):
        element = grad[r] * inverse
        value = jnp.maximum(1.001 * element, -0.001 * element) + 1e-05
        rate_above_out[r] = value
        return value

    def below(r):
        element = grad[r] * inverse
        value = jnp.maximum(0.001 * element, -1.001 * element) + 1e-05
        rate_below_out[r] = value
        return value

    evaluate(
        jnp.ones((1, 1), f32), above, below, up, low, least, most, upper, lower, bend, tallies, message
    )


def advance(arrived, y):
    total = jnp.sum(arrived[...], axis=0, keepdims=True)
    lane = lane_iota(total.shape)
    slope = jnp.sum(jnp.where(lane < LANES // 2, total, 0.0), axis=1, keepdims=True)
    curve = jnp.sum(jnp.where(lane < LANES // 2, 0.0, total), axis=1, keepdims=True)
    return jnp.maximum(0.0, y + slope / curve)


def step_kernel(
    arrived, y_ref, rate_above, rate_below, up, low, least, most, upper, lower, bend, tallies,
    message, y_out,
):
    y = advance(arrived, y_ref[0:1, 0:1])
    y_out[...] = jnp.broadcast_to(y, y_out.shape)
    evaluate(
        y, lambda r: rate_above[r], lambda r: rate_below[r],
        up, low, least, most, upper, lower, bend, tallies, message,
    )


def last_kernel(
    arrived, y_ref, rate_above, rate_below, up, low, least, most, below, solid, material, out
):
    y = advance(arrived, y_ref[0:1, 0:1])
    for r in range(out.shape[0]):
        chosen = reached(rate_above[r], rate_below[r], y, up[r], low[r], least[r], most[r])[1]
        out[r] = jnp.where(material[r] == 1, below[r] + chosen, solid[r])


def with_place(kernel, rows_total, cols_total):
    def body(place_ref, *refs):
        kernel(rows_total, cols_total, (place_ref[0], place_ref[1]), *refs)

    return body


def placed_call(kernel, place, outs, args, scratch, totals):
    vmem = pl.BlockSpec(memory_space=pltpu.VMEM)
    return pl.pallas_call(
        with_place(kernel, *totals),
        out_shape=[jax.ShapeDtypeStruct(shape, f32) for shape in outs],
        in_specs=[pl.BlockSpec(memory_space=pltpu.SMEM)] + [vmem] * len(args),
        out_specs=[vmem] * len(outs),
        scratch_shapes=[pltpu.VMEM(shape, f32) for shape in scratch],
        compiler_params=pltpu.CompilerParams(vmem_limit_bytes=40 * 1024 * 1024),
    )(place, *args)


def launch_messages(density, material, source, prior, temp):
    rows, height, own = density.shape
    end = own // LANES - 1
    block, message = (rows, height, LANES), (8, height, own)
    first = pl.BlockSpec(block, lambda i: (0, 0, 0))
    last = pl.BlockSpec(block, lambda i: (0, 0, end))

    def layers(count, index):
        return pl.BlockSpec((count, height, own), lambda i: (index, 0, 0))

    strips = (density, material, source, prior, temp)
    layered = (prior, source, temp)
    return pl.pallas_call(
        launch_kernel,
        grid=(1,),
        out_shape=[jax.ShapeDtypeStruct(s, f32) for s in (block, block, message, message)],
        in_specs=[first] * 5 + [last] * 5
        + [layers(4, 0)] * 2 + [layers(1, 0)] + [layers(4, rows // 4 - 1)] * 2 + [layers(1, rows - 1)],
        out_specs=[pl.BlockSpec(s, lambda i: (0, 0, 0)) for s in (block, block, message, message)],
    )(*strips, *strips, *layered, *layered)


def on_device(
    solid_occupancy,
    newer_occupancy_shift,
    older_occupancy_shift,
    below_limit_spacing,
    above_limit_spacing,
    thermal_state,
    loss_state_derivative,
    prior_dual_state,
    cell_material,
):
    rows, height, own = solid_occupancy.shape
    deep, long = lax.axis_size("thick"), lax.axis_size("facade")
    totals = (rows * deep, own * long)
    place = jnp.stack(
        [lax.axis_index("thick") * rows, lax.axis_index("facade") * own]
    ).astype(jnp.int32)
    width = own + LANES
    whole = (rows, height, own)

    def turn(axis, size, step):
        pairs = [(i, (i + step) % size) for i in range(size)]
        return lambda value: lax.ppermute(value, axis, pairs)

    to_right, to_left = turn("facade", long, 1), turn("facade", long, -1)
    to_deeper, to_nearer = turn("thick", deep, 1), turn("thick", deep, -1)

    first_strips, last_strips, rows_up, rows_down = launch_messages(
        solid_occupancy, cell_material, loss_state_derivative, prior_dual_state, thermal_state
    )
    right, left = to_left(first_strips), to_right(last_strips)

    def side_by_side(strips, start):
        return jnp.concatenate([strips[start + r] for r in range(4)], axis=1)[None]

    def density_message(start):
        return jnp.concatenate(
            [
                solid_occupancy[start:start + 4],
                side_by_side(left, start), side_by_side(right, start),
            ]
        )

    density_up, density_down, rows_up, rows_down = lax.optimization_barrier(
        (density_message(rows - 4), density_message(0), rows_up, rows_down)
    )
    density_above, density_below = to_deeper(density_up), to_nearer(density_down)
    from_above, from_below = to_deeper(rows_up), to_nearer(rows_down)

    (below, above, up, low, least, most, upper, lower, bend, tallies) = call(
        lines_kernel,
        [whole] * 9 + [(2, height, LANES)],
        (
            solid_occupancy, newer_occupancy_shift, older_occupancy_shift,
            below_limit_spacing, above_limit_spacing, cell_material,
        ),
    )

    four = (4, height, width)
    rho, cond_first, cond_last = placed_call(
        rho_kernel, place,
        [(rows, height, width), four, four],
        (
            solid_occupancy, cell_material, density_above, density_below, left, right,
        ),
        [(BOTH_SIDES, height, width), (BOTH_SIDES - 4, height, width), (rows, height, width)],
        totals,
    )
    cond_above, cond_below = to_deeper(cond_last), to_nearer(cond_first)
    tall, own_wide, inner = (
        (BOTH_SIDES, height, width), (rows, height, width), (len(INNER), height, width),
    )
    prepared = call(
        prepare_kernel,
        [tall, tall, (rows + 2, height, width)] + [own_wide] * 9 + [inner] * 4,
        (
            cond_first, cond_last, prior_dual_state, loss_state_derivative, thermal_state,
            from_above, from_below, density_above, density_below, left, right,
        ),
    )
    dual_state, weighted_first, weighted_last = placed_call(
        sweep_kernel, place,
        [whole, four, four],
        (
            cond_above, cond_first, cond_last, cond_below, rho, cell_material, *prepared,
            left, right, tallies,
        ),
        [tall] * 8 + [(2, height, width)] * 2,
        totals,
    )
    weighted_above, weighted_below = to_deeper(weighted_last), to_nearer(weighted_first)
    count = deep * long
    note = (count, LANES)
    grad, message = placed_call(
        grad_kernel, place,
        [whole, note],
        (weighted_above, weighted_first, weighted_last, weighted_below, cell_material),
        [tall, (BOTH_SIDES - 4, height, width), (rows, height, width)],
        totals,
    )

    def everyone(rows_out):
        return lax.all_to_all(rows_out, AXES, 0, 0, tiled=True)

    partners = [(i, i ^ 1) for i in range(long)]
    alike = [[i for i in range(count) if i % 2 == core] for core in (0, 1)]

    def halves(row):
        both = row + lax.ppermute(row, "facade", partners)
        return lax.all_to_all(
            jnp.broadcast_to(both, (count // 2, LANES)), AXES, 0, 0, axis_index_groups=alike, tiled=True
        )

    fixed = (up, low, least, most, upper, lower, bend, tallies)
    line = (1, LANES)
    message, rate_above, rate_below = call(
        first_kernel, [line, whole, whole], (everyone(message), grad) + fixed
    )
    y = jnp.ones((8, LANES), f32)
    for _ in range(NEWTON - 1):
        message, y = call(
            step_kernel, [line, (8, LANES)],
            (halves(message), y, rate_above, rate_below) + fixed,
        )
    (density_new,) = call(
        last_kernel, [whole],
        (
            halves(message), y, rate_above, rate_below, up, low, least, most, below,
            solid_occupancy, cell_material,
        ),
    )
    return (density_new, below, above, dual_state)


def solution(mesh):
    spec = P("thick", None, "facade")
    return jax.shard_map(
        on_device,
        mesh=mesh,
        in_specs=(spec,) * 9,
        out_specs=(spec,) * 4,
        check_vma=False,
    )
```

```python
import functools
import jax
import jax.numpy as jnp
from jax import lax
from jax.experimental import pallas as pl
from jax.experimental.pallas import tpu as pltpu
from jax.sharding import PartitionSpec as P

RADIUS = 4
SWEEPS = 3
NEWTON = 8

k_void = 0.03
k_frame = 160.0
k_glass = 1.0
k_anchor = 50.0
loss_rate = 0.05
spectrum_low = 0.05
spectrum_high = 2.0
solid_allowance = 0.35
curve_floor = 0.05
move_limit = 0.2
gamma_slope = 200.0

LANES = 128
STRIP = 16
above_weight = 1.001 + 1e-05
below_weight = 0.001 + 1e-05

f32 = jnp.float32
AXES = ("thick", "facade")
BOTH_SIDES = 16


def call(kernel, outs, args, scratch=()):
    vmem = pl.BlockSpec(memory_space=pltpu.VMEM)
    return pl.pallas_call(
        kernel,
        out_shape=[jax.ShapeDtypeStruct(shape, f32) for shape in outs],
        in_specs=[vmem] * len(args),
        out_specs=[vmem] * len(outs),
        scratch_shapes=[pltpu.VMEM(shape, f32) for shape in scratch],
        compiler_params=pltpu.CompilerParams(vmem_limit_bytes=40 * 1024 * 1024),
    )(*args)


def lane_iota(shape):
    return lax.broadcasted_iota(jnp.int32, shape, len(shape) - 1)


def sub_iota(shape):
    return lax.broadcasted_iota(jnp.int32, shape, len(shape) - 2)


def ahead(value, step, axis):
    return pltpu.roll(value, (value.shape[axis] - step) % value.shape[axis], axis)


def behind(value, step, axis):
    return pltpu.roll(value, step, axis)


def launch_kernel(*refs):
    firsts, lasts, to_left, to_right = refs[0:5], refs[5:10], refs[10], refs[11]
    rows, height, _ = to_left.shape
    group = lane_iota((height, LANES)) // STRIP
    for row in range(rows):
        for source, target, place in ((firsts, to_left, 0), (lasts, to_right, LANES - STRIP)):
            packed = jnp.zeros((height, LANES), f32)
            for index, ref in enumerate(source):
                value = ref[row]
                if value.dtype != f32:
                    value = value.astype(f32) + 1.0
                shift = (STRIP * index - place) % LANES
                if shift:
                    value = pltpu.roll(value, shift, 1)
                packed = jnp.where(group == index, value, packed)
            target[row] = packed


def rows_kernel(*refs):
    nears, fars, rows_up, rows_down = refs[0:3], refs[3:6], refs[6], refs[7]
    start = 0
    for near, far, count in zip(nears, fars, (4, 3, 1)):
        for r in range(count):
            rows_down[start + r] = near[r]
            rows_up[start + r] = far[far.shape[0] - count + r]
        start += count


def halo_lanes(left, right, index):
    lane = lane_iota(left.shape)
    shift = (LANES - STRIP * index) % LANES
    after = pltpu.roll(right, shift, 1) if shift else right
    shift = (LANES - STRIP - STRIP * index) % LANES
    before = pltpu.roll(left, shift, 1) if shift else left
    return jnp.where(lane < STRIP, after, jnp.where(lane >= LANES - STRIP, before, 0.0))


def axis_weight(position, total):
    acc = jnp.zeros(position.shape, f32)
    for offset in range(-RADIUS, RADIUS + 1):
        weight = float(RADIUS + 1 - abs(offset))
        inside = (position + offset >= 0) & (position + offset < total)
        acc = acc + jnp.where(inside, weight, 0.0)
    return jnp.maximum(acc, 1.0)


def inverse_plane(height, own, cols_total, col_start):
    width = own + LANES
    lane = lane_iota((1, width))
    place = jnp.where(lane < own + LANES // 2, lane, lane - width) + col_start
    middle = axis_weight(sub_iota((height, 1)), height)
    return 1.0 / (middle * axis_weight(place, cols_total))


def row_weight(row, rows_total, row_start):
    return 1.0 / axis_weight(jnp.full((1, 1), row + row_start, jnp.int32), rows_total)


def filter_height(value):
    height = value.shape[0]
    level = sub_iota((height, 1))
    total = float(RADIUS + 1) * value
    for offset in range(1, RADIUS + 1):
        weight = float(RADIUS + 1 - offset)
        up = jnp.where(level < height - offset, weight, 0.0)
        down = jnp.where(level >= offset, weight, 0.0)
        total = total + up * ahead(value, offset, 0) + down * behind(value, offset, 0)
    return total


def filter_lanes(value):
    def box(v):
        pair = v + ahead(v, 1, 1)
        return pair + ahead(pair, 2, 1) + behind(v, 1, 1)

    def box_back(v):
        pair = v + behind(v, 1, 1)
        return pair + behind(pair, 2, 1) + ahead(v, 1, 1)

    return box_back(box(value))


def depth_filter(source, middle, target):
    count = source.shape[0]
    for r in range(count - 4):
        middle[r] = (source[r] + source[r + 1]) + (source[r + 2] + source[r + 3]) + source[r + 4]
    for r in range(count - 8):
        target[r] = (middle[r] + middle[r + 1]) + (middle[r + 2] + middle[r + 3]) + middle[r + 4]


def present(place, rows, own, rows_total, cols_total):
    row_start, col_start = place

    def flag(condition):
        return jnp.where(condition, 1.0, 0.0).astype(f32)

    return (
        flag(row_start > 0), flag(row_start + rows < rows_total),
        flag(col_start > 0), flag(col_start + own < cols_total),
    )


def corner(message, row):
    lanes = slice(row * LANES, (row + 1) * LANES)
    return message[4, :, lanes], message[5, :, lanes]


def rho_kernel(
    rows_total, cols_total, place,
    density, material, density_above, density_below, left, right,
    rho_out, cond_first, cond_last,
    ext, middle, summed,
):
    rows, height, own = density.shape
    has_above, has_below, has_left, has_right = present(place, rows, own, rows_total, cols_total)

    def halo(strips, index):
        return halo_lanes(strips[0] * has_left, strips[1] * has_right, index)

    for r in range(4):
        ext[r, :, :own] = density_above[r] * has_above
        ext[r, :, own:] = halo(corner(density_above, r), 0) * has_above
        ext[rows + 4 + r, :, :own] = density_below[r] * has_below
        ext[rows + 4 + r, :, own:] = halo(corner(density_below, r), 0) * has_below
    for r in range(rows):
        ext[4 + r, :, :own] = density[r]
        ext[4 + r, :, own:] = halo((left[r], right[r]), 0)
    depth_filter(ext, middle, summed)
    plane = inverse_plane(height, own, cols_total, place[1])
    for r in range(rows):
        rho = filter_lanes(filter_height(summed[r])) * (
            plane * row_weight(r, rows_total, place[0])
        )
        code = jnp.concatenate(
            [material[r].astype(f32) + 1.0, halo((left[r], right[r]), 1)], axis=1
        )
        frame = k_void + (k_frame - k_void) * rho * rho * rho
        cond = jnp.where(code == 2.0, frame, jnp.where(code == 1.0, k_glass, k_anchor))
        cond = jnp.where(code == 0.0, 0.0, cond)
        rho_out[r] = rho
        if r < 4:
            cond_first[r] = cond
        else:
            cond_last[r - 4] = cond


centre_value = 0.5 * (spectrum_high + spectrum_low)
half_width = 0.5 * (spectrum_high - spectrum_low)
ratio_value = centre_value / half_width
INNER = range(5, 11)


class Rows:
    def __init__(self, ready, first, stop, rest):
        self.ready, self.first, self.stop, self.rest = ready, first, stop, rest

    def __getitem__(self, row):
        if self.first <= row < self.stop:
            return self.ready[row - self.first]
        return self.rest[row]


def face(one, other, store=None):
    inv = 1.0 / jnp.maximum(one + other, 1e-3)
    part = one * inv
    if store is not None:
        here, there, row = store
        rest = other * inv
        there[row] = part * part
        here[row] = rest * rest
    return 2.0 * part * other


def first_residual(value, before, after, load, deep_before, deep, tall, wide):
    inverse = 1.0 / (
        loss_rate + (deep + deep_before) + (tall + behind(tall, 1, 0)) + (wide + behind(wide, 1, 1))
    )
    left_over = load - operate(value, deep_before * (before - value), deep * (value - after), tall, wide)
    direction = left_over * inverse * (1.0 / centre_value)
    return inverse, left_over, direction


def operate(value, flux_before, flux, tall, wide):
    high = tall * (value - ahead(value, 1, 0))
    along = wide * (value - ahead(value, 1, 1))
    return (
        loss_rate * value + (flux - flux_before) + (high - behind(high, 1, 0))
        + (along - behind(along, 1, 1))
    )


def prepare_kernel(
    cond_first, cond_last, prior, source, temp,
    from_above, from_below, density_above, density_below, left, right,
    field, load, heat, depth_face, height_face, lane_face,
    depth_here, depth_there, height_here, height_there, lane_here, lane_there,
    inverse, residual, direction, dual,
):
    rows, height, own = prior.shape
    last_level = sub_iota((height, 1)) == height - 1

    def place_row(target, row, main, strips, index):
        target[row, :, :own] = main
        target[row, :, own:] = halo_lanes(strips[0], strips[1], index)

    for r in range(4):
        place_row(field, r, from_above[r], corner(density_above, r), 3)
        place_row(field, 12 + r, from_below[r], corner(density_below, r), 3)
    for r in range(3):
        place_row(load, 1 + r, from_above[4 + r], corner(density_above, 1 + r), 2)
        place_row(load, 12 + r, from_below[4 + r], corner(density_below, r), 2)
    load[0] = jnp.zeros(load.shape[1:], f32)
    load[15] = jnp.zeros(load.shape[1:], f32)
    place_row(heat, 0, from_above[7], corner(density_above, 3), 4)
    place_row(heat, 9, from_below[7], corner(density_below, 0), 4)
    for r in range(rows):
        strips = (left[r], right[r])
        place_row(field, 4 + r, prior[r], strips, 3)
        place_row(load, 4 + r, source[r], strips, 2)
        place_row(heat, 1 + r, temp[r], strips, 4)

    deep_before = None
    following = cond_first[0]
    for r in range(4, 12):
        i = r - 4
        here = following
        tall = jnp.where(
            last_level, 0.0, face(here, ahead(here, 1, 0), (height_here, height_there, i))
        )
        wide = face(here, ahead(here, 1, 1), (lane_here, lane_there, i))
        height_face[i] = tall
        lane_face[i] = wide
        if r < 11:
            following = cond_first[i + 1] if i < 3 else cond_last[i - 3]
            deep = face(here, following, (depth_here, depth_there, i))
            depth_face[i] = deep
        if r in INNER:
            value = field[r]
            one, two, three = first_residual(
                value, field[r - 1], field[r + 1], load[r], deep_before, deep, tall, wide
            )
            k = r - INNER.start
            inverse[k], residual[k], direction[k] = one, two, three
            dual[k] = value + three
        deep_before = deep


def sweep_kernel(
    rows_total, cols_total, place,
    cond_above, cond_first, cond_last, cond_below, rho, material,
    field, load, heat, own_depth_face, own_height_face, own_lane_face,
    own_depth_here, own_depth_there, height_here, height_there, lane_here, lane_there,
    own_inverse, own_residual, own_direction, own_dual, left, right, tallies,
    dual_out, weighted_first, weighted_last,
    depth_face, height_face, lane_face, inverse, residual, first_direction, next_direction, dual,
    edge_here, edge_there,
):
    rows, height, own = rho.shape[0], rho.shape[1], dual_out.shape[2]
    has_above, has_below, has_left, has_right = present(place, rows, own, rows_total, cols_total)
    last_level = sub_iota((height, 1)) == height - 1

    def cond(r):
        if r < 4:
            return cond_above[r] * has_above
        if r >= 12:
            return cond_below[r - 12] * has_below
        return cond_first[r - 4] if r < 8 else cond_last[r - 8]

    depth_faces = Rows(own_depth_face, 4, 11, depth_face)
    height_faces = Rows(own_height_face, 4, 12, height_face)
    lane_faces = Rows(own_lane_face, 4, 12, lane_face)
    inverses = Rows(own_inverse, INNER.start, INNER.stop, inverse)
    residuals = Rows(own_residual, INNER.start, INNER.stop, residual)
    directions = Rows(own_direction, INNER.start, INNER.stop, first_direction)
    duals = Rows(own_dual, INNER.start, INNER.stop, dual)

    following = cond(0)
    for r in range(15):
        if 4 <= r < 11:
            following = None
            continue
        here = cond(r) if following is None else following
        following = cond(r + 1)
        store = (edge_here, edge_there, 0 if r == 3 else 1) if r in (3, 11) else None
        depth_face[r] = face(here, following, store)
        if r in (1, 2, 3, 12, 13, 14):
            height_face[r] = jnp.where(last_level, 0.0, face(here, ahead(here, 1, 0)))
            lane_face[r] = face(here, ahead(here, 1, 1))
    for r in range(1, 15):
        if r in INNER:
            continue
        value = field[r]
        one, two, three = first_residual(
            value, field[r - 1], field[r + 1], load[r],
            depth_faces[r - 1], depth_faces[r], height_faces[r], lane_faces[r],
        )
        inverse[r], residual[r], first_direction[r] = one, two, three
        if 3 <= r < 13:
            dual[r] = value + three

    factor = 1.0 / ratio_value
    now = directions
    for sweep in range(SWEEPS - 1):
        factor_next = 1.0 / (2.0 * ratio_value - factor)
        keep, add = factor_next * factor, 2.0 * factor_next / half_width
        start, stop = 2 + sweep, 14 - sweep
        following = now[start]
        flux_before = depth_faces[start - 1] * (now[start - 1] - following)
        for r in range(start, stop):
            value, following = following, now[r + 1]
            flux = depth_faces[r] * (value - following)
            left_over = residuals[r] - operate(
                value, flux_before, flux, height_faces[r], lane_faces[r]
            )
            direction = keep * value + add * (left_over * inverses[r])
            if sweep < SWEEPS - 2:
                residual[r] = left_over
                next_direction[r] = direction
            if 3 <= r < 13:
                dual[r] = duals[r] + direction
            flux_before = flux
        factor = factor_next
        now, residuals, duals = next_direction, residual, dual

    depth_here = Rows(own_depth_here, 4, 11, {11: edge_here[1]})
    depth_there = Rows(own_depth_there, 4, 11, {3: edge_there[0], 11: edge_there[1]})
    plane = inverse_plane(height, own, cols_total, place[1])
    for r in range(rows):
        dual_out[r] = dual[4 + r, :, :own]
    a, t = dual[3], heat[0]
    a_next, t_next = dual[4], heat[1]
    deep_before = (a - a_next) * (t - t_next) * depth_there[3]
    for r in range(4, 4 + rows):
        row = r - 4
        a, t = a_next, t_next
        a_next, t_next = dual[r + 1], heat[r - 2]
        deep = (a - a_next) * (t - t_next)
        tall = (a - ahead(a, 1, 0)) * (t - ahead(t, 1, 0))
        tall = jnp.where(last_level, 0.0, tall)
        wide = (a - ahead(a, 1, 1)) * (t - ahead(t, 1, 1))
        total = (
            (deep * depth_here[r] + deep_before)
            + (tall * height_here[row] + behind(tall * height_there[row], 1, 0))
            + (wide * lane_here[row] + behind(wide * lane_there[row], 1, 1))
        )
        deep_before = deep * depth_there[r]
        strips = halo_lanes(left[row] * has_left, right[row] * has_right, 1)
        code = jnp.concatenate([material[row].astype(f32) + 1.0, strips], axis=1)
        thick_rho = rho[row]
        value = total * (thick_rho * thick_rho) * (
            plane * (row_weight(row, rows_total, place[0]) * (-6.0 * (k_frame - k_void)))
        )
        value = jnp.where(code == 2.0, value, 0.0)
        if row < 4:
            weighted_first[row] = value
        else:
            weighted_last[row - 4] = value


def grad_kernel(
    rows_total, cols_total, place,
    from_above, first, last, from_below, material, grad_out, message, ext, middle, summed,
):
    rows, height, own = grad_out.shape
    has_above, has_below, _, _ = present(place, rows, own, rows_total, cols_total)
    for r in range(4):
        ext[r] = from_above[r] * has_above
        ext[4 + r] = first[r]
        ext[8 + r] = last[r]
        ext[12 + r] = from_below[r] * has_below
    depth_filter(ext, middle, summed)
    largest = jnp.zeros((height, LANES), f32)
    for r in range(rows):
        grad = filter_lanes(filter_height(summed[r]))[:, :own]
        grad_out[r] = grad
        size = jnp.where(material[r] == 1, jnp.abs(grad), 0.0)
        for block in range(own // LANES):
            largest = jnp.maximum(largest, size[:, block * LANES:(block + 1) * LANES])
    message[...] = jnp.broadcast_to(jnp.max(largest, axis=0, keepdims=True), message.shape)


def lines_kernel(
    solid, newer, older, below_spacing, above_spacing, material,
    below_out, above_out, up_out, low_out, least_out, most_out, upper_out, lower_out, bend_out,
    tallies,
):
    rows, height, own = solid.shape
    base = jnp.zeros((height, LANES), f32)
    count = jnp.zeros((height, LANES), f32)
    for r in range(rows):
        x = solid[r]
        design = material[r] == 1
        gamma = 0.95 + 0.25 * jnp.tanh(gamma_slope * newer[r] * older[r])
        below = x - gamma * below_spacing[r]
        above = x + gamma * above_spacing[r]
        below_out[r] = below
        above_out[r] = above
        up = above - x
        low = x - below
        floor = jnp.maximum(jnp.maximum(0.0, below + 0.1 * low), x - move_limit)
        ceiling = jnp.minimum(jnp.minimum(1.0, above - 0.1 * up), x + move_limit)
        up_out[r] = up
        low_out[r] = low
        least_out[r] = floor - below
        most_out[r] = ceiling - below
        upper_out[r] = jnp.where(design, above_weight * up * up, 0.0)
        lower_out[r] = jnp.where(design, below_weight * low * low, 0.0)
        bend_out[r] = jnp.where(design, up * low / (2.0 * (up + low)), 0.0)
        term = jnp.where(
            design, x - solid_allowance - above_weight * up - below_weight * low, 0.0
        )
        one = jnp.where(design, curve_floor, 0.0)
        for block in range(own // LANES):
            base = base + term[:, block * LANES:(block + 1) * LANES]
            count = count + one[:, block * LANES:(block + 1) * LANES]
    tallies[0] = base
    tallies[1] = count


def reached(rate_above, rate_below, y, up, low, least, most):
    root_above = rate_above + y * above_weight
    root_below = rate_below + y * below_weight
    inv_above, inv_below = lax.rsqrt(root_above), lax.rsqrt(root_below)
    root_above, root_below = root_above * inv_above, root_below * inv_below
    width = up + low
    pull = low * root_below
    trial = width * pull / (up * root_above + pull)
    return trial, jnp.clip(trial, least, most), width, root_above, root_below, inv_above, inv_below


def sums_to_message(slope, curve, message):
    slope = jnp.sum(slope, axis=0, keepdims=True)
    curve = jnp.sum(curve, axis=0, keepdims=True)
    slope = slope + pltpu.roll(slope, LANES // 2, 1)
    curve = curve + pltpu.roll(curve, LANES // 2, 1)
    lane = lane_iota((1, LANES))
    message[...] = jnp.broadcast_to(jnp.where(lane < LANES // 2, slope, curve), message.shape)


def evaluate(y, rate_above, rate_below, up, low, least, most, upper, lower, bend, tallies, message):
    rows, height, own = up.shape
    slope_sum, curve_sum = tallies[0], tallies[1]
    for r in range(rows):
        trial, chosen, width, root_above, root_below, inv_above, inv_below = reached(
            rate_above(r), rate_below(r), y, up[r], low[r], least[r], most[r]
        )
        rest = width - chosen
        slope = (upper[r] * chosen + lower[r] * rest) / (rest * chosen)
        split = above_weight * (inv_above * inv_above) - below_weight * (inv_below * inv_below)
        curve = bend[r] * (root_above * root_below) * (split * split)
        free = (trial > least[r]) & (trial < most[r])
        curve = jnp.where(free, curve, 0.0)
        for block in range(own // LANES):
            slope_sum = slope_sum + slope[:, block * LANES:(block + 1) * LANES]
            curve_sum = curve_sum + curve[:, block * LANES:(block + 1) * LANES]
    sums_to_message(slope_sum, curve_sum, message)


def first_kernel(
    arrived, grad, up, low, least, most, upper, lower, bend, tallies,
    message, rate_above_out, rate_below_out,
):
    scale = jnp.max(jnp.max(arrived[...], axis=0, keepdims=True), axis=1, keepdims=True)
    inverse = 1.0 / (scale + 1e-06)

    def above(r):
        element = grad[r] * inverse
        value = jnp.maximum(1.001 * element, -0.001 * element) + 1e-05
        rate_above_out[r] = value
        return value

    def below(r):
        element = grad[r] * inverse
        value = jnp.maximum(0.001 * element, -1.001 * element) + 1e-05
        rate_below_out[r] = value
        return value

    evaluate(
        jnp.ones((1, 1), f32), above, below, up, low, least, most, upper, lower, bend, tallies, message
    )


def advance(arrived, y):
    total = jnp.sum(arrived[...], axis=0, keepdims=True)
    lane = lane_iota(total.shape)
    slope = jnp.sum(jnp.where(lane < LANES // 2, total, 0.0), axis=1, keepdims=True)
    curve = jnp.sum(jnp.where(lane < LANES // 2, 0.0, total), axis=1, keepdims=True)
    return jnp.maximum(0.0, y + slope / curve)


def step_kernel(
    arrived, y_ref, rate_above, rate_below, up, low, least, most, upper, lower, bend, tallies,
    message, y_out,
):
    y = advance(arrived, y_ref[0:1, 0:1])
    y_out[...] = jnp.broadcast_to(y, y_out.shape)
    evaluate(
        y, lambda r: rate_above[r], lambda r: rate_below[r],
        up, low, least, most, upper, lower, bend, tallies, message,
    )


def last_kernel(
    arrived, y_ref, rate_above, rate_below, up, low, least, most, below, solid, material, out
):
    y = advance(arrived, y_ref[0:1, 0:1])
    for r in range(out.shape[0]):
        chosen = reached(rate_above[r], rate_below[r], y, up[r], low[r], least[r], most[r])[1]
        out[r] = jnp.where(material[r] == 1, below[r] + chosen, solid[r])


def with_place(kernel, rows_total, cols_total):
    def body(place_ref, *refs):
        kernel(rows_total, cols_total, (place_ref[0], place_ref[1]), *refs)

    return body


def placed_call(kernel, place, outs, args, scratch, totals):
    vmem = pl.BlockSpec(memory_space=pltpu.VMEM)
    return pl.pallas_call(
        with_place(kernel, *totals),
        out_shape=[jax.ShapeDtypeStruct(shape, f32) for shape in outs],
        in_specs=[pl.BlockSpec(memory_space=pltpu.SMEM)] + [vmem] * len(args),
        out_specs=[vmem] * len(outs),
        scratch_shapes=[pltpu.VMEM(shape, f32) for shape in scratch],
        compiler_params=pltpu.CompilerParams(vmem_limit_bytes=40 * 1024 * 1024),
    )(place, *args)


def launch_messages(density, material, source, prior, temp):
    rows, height, own = density.shape
    end = own // LANES - 1
    block, message = (rows, height, LANES), (8, height, own)
    first = pl.BlockSpec(block, lambda i: (0, 0, 0))
    last = pl.BlockSpec(block, lambda i: (0, 0, end))

    def layers(count, index):
        return pl.BlockSpec((count, height, own), lambda i: (index, 0, 0))

    strips = (density, material, source, prior, temp)
    layered = (prior, source, temp)

    def same(shape):
        return [jax.ShapeDtypeStruct(shape, f32)] * 2, [pl.BlockSpec(shape, lambda i: (0, 0, 0))] * 2

    shapes, specs = same(block)
    to_sides = pl.pallas_call(
        launch_kernel, grid=(1,), out_shape=shapes, out_specs=specs,
        in_specs=[first] * 5 + [last] * 5,
    )(*strips, *strips)
    shapes, specs = same(message)
    to_depths = pl.pallas_call(
        rows_kernel, grid=(1,), out_shape=shapes, out_specs=specs,
        in_specs=[layers(4, 0)] * 2 + [layers(1, 0)]
        + [layers(4, rows // 4 - 1)] * 2 + [layers(1, rows - 1)],
    )(*layered, *layered)
    return (*to_sides, *to_depths)


def on_device(
    solid_occupancy,
    newer_occupancy_shift,
    older_occupancy_shift,
    below_limit_spacing,
    above_limit_spacing,
    thermal_state,
    loss_state_derivative,
    prior_dual_state,
    cell_material,
):
    rows, height, own = solid_occupancy.shape
    deep, long = lax.axis_size("thick"), lax.axis_size("facade")
    totals = (rows * deep, own * long)
    place = jnp.stack(
        [lax.axis_index("thick") * rows, lax.axis_index("facade") * own]
    ).astype(jnp.int32)
    width = own + LANES
    whole = (rows, height, own)

    def turn(axis, size, step):
        pairs = [(i, (i + step) % size) for i in range(size)]
        return lambda value: lax.ppermute(value, axis, pairs)

    to_right, to_left = turn("facade", long, 1), turn("facade", long, -1)
    to_deeper, to_nearer = turn("thick", deep, 1), turn("thick", deep, -1)

    first_strips, last_strips, rows_up, rows_down = launch_messages(
        solid_occupancy, cell_material, loss_state_derivative, prior_dual_state, thermal_state
    )
    right, left = to_left(first_strips), to_right(last_strips)

    def side_by_side(strips, start):
        return jnp.concatenate([strips[start + r] for r in range(4)], axis=1)[None]

    def density_message(start):
        return jnp.concatenate(
            [
                solid_occupancy[start:start + 4],
                side_by_side(left, start), side_by_side(right, start),
            ]
        )

    from_above, from_below = to_deeper(rows_up), to_nearer(rows_down)
    density_above = to_deeper(density_message(rows - 4))
    density_below = to_nearer(density_message(0))

    (below, above, up, low, least, most, upper, lower, bend, tallies) = call(
        lines_kernel,
        [whole] * 9 + [(2, height, LANES)],
        (
            solid_occupancy, newer_occupancy_shift, older_occupancy_shift,
            below_limit_spacing, above_limit_spacing, cell_material,
        ),
    )

    four = (4, height, width)
    rho, cond_first, cond_last = placed_call(
        rho_kernel, place,
        [(rows, height, width), four, four],
        (
            solid_occupancy, cell_material, density_above, density_below, left, right,
        ),
        [(BOTH_SIDES, height, width), (BOTH_SIDES - 4, height, width), (rows, height, width)],
        totals,
    )
    cond_above, cond_below = to_deeper(cond_last), to_nearer(cond_first)
    tall, own_wide, inner = (
        (BOTH_SIDES, height, width), (rows, height, width), (len(INNER), height, width),
    )
    prepared = call(
        prepare_kernel,
        [tall, tall, (rows + 2, height, width)] + [own_wide] * 9 + [inner] * 4,
        (
            cond_first, cond_last, prior_dual_state, loss_state_derivative, thermal_state,
            from_above, from_below, density_above, density_below, left, right,
        ),
    )
    dual_state, weighted_first, weighted_last = placed_call(
        sweep_kernel, place,
        [whole, four, four],
        (
            cond_above, cond_first, cond_last, cond_below, rho, cell_material, *prepared,
            left, right, tallies,
        ),
        [tall] * 8 + [(2, height, width)] * 2,
        totals,
    )
    weighted_above, weighted_below = to_deeper(weighted_last), to_nearer(weighted_first)
    count = deep * long
    note = (count, LANES)
    grad, message = placed_call(
        grad_kernel, place,
        [whole, note],
        (weighted_above, weighted_first, weighted_last, weighted_below, cell_material),
        [tall, (BOTH_SIDES - 4, height, width), (rows, height, width)],
        totals,
    )

    def everyone(rows_out):
        return lax.all_to_all(rows_out, AXES, 0, 0, tiled=True)

    fixed = (up, low, least, most, upper, lower, bend, tallies)
    message, rate_above, rate_below = call(
        first_kernel, [note, whole, whole], (everyone(message), grad) + fixed
    )
    y = jnp.ones((8, LANES), f32)
    for _ in range(NEWTON - 1):
        message, y = call(
            step_kernel, [note, (8, LANES)],
            (everyone(message), y, rate_above, rate_below) + fixed,
        )
    (density_new,) = call(
        last_kernel, [whole],
        (
            everyone(message), y, rate_above, rate_below, up, low, least, most, below,
            solid_occupancy, cell_material,
        ),
    )
    return (density_new, below, above, dual_state)


def solution(mesh):
    spec = P("thick", None, "facade")
    return jax.shard_map(
        on_device,
        mesh=mesh,
        in_specs=(spec,) * 9,
        out_specs=(spec,) * 4,
        check_vma=False,
    )
```
